32 devices in a mesh: mid: 4 (over y, x), off: 8 (over z, core).
Axes of the slice: x: 2, y: 2, z: 4, core: 2. Of those that a mesh axis runs over, the one named last changes fastest.
Arguments:
- bins_data: bfloat16 [16, 32, 2, 2048], P('off', None, None, 'mid'), may hold values from -6 to 6
- operators: bfloat16 [16, 16, 128, 128], P('off'), may hold values from -0.5 to 0.5
- targets: int32 [16, 16], P('off'), may hold values from 0 to 255
- counts: int32 [16], P('off'), may hold values from 1 to 16, 128 in all
- layer_index: int32 [2, 8, 16], P(None, None, 'mid'), may hold values from 0 to 15
- slowness: float32 [2, 16], replicated, may hold values from 0.8 to 1.25
Outputs:
- wavefield: float32 [32, 256, 2, 2048], P('off', None, None, 'mid')
The draws below stay inside these ranges and needn't reach their ends.
Inputs may be any that keep to these rules, and one draw needn't show every extreme that they name: Slots at positions counts[b] and beyond of bin b's list are unused; some bin has all 16 slots live.
All inputs are finite; a program needn't handle non-finite values. No bound on the sum of `counts` on one device may be relied on, other than what follows from the above.
Results may differ from the reference program's by a relative error of at most 0.0003.
Values may be sent and summed in bfloat16 or wider, within the bound.
No kernel may reach another device: no remote copies, remote signals or barrier semaphores. Data moves between devices by JAX's collectives and lax.ppermute only.
A program may use at most 192 MiB of HBM per device.

```python
import math
import jax
import jax.numpy as jnp
import numpy as np
from jax import lax

NB = 16
NH = 256
NM = 2048
BLK = 128
ENT = 16
LAYERS = 16
OFFBLK = 32
STEPS = 2
NF = 32


def plant(entries, key, low, top_value):
    extent = entries.shape
    spot = [jax.random.randint(jax.random.fold_in(key, axis), (), 0, extent[axis]) for axis in range(len(extent))]
    entries = entries.at[tuple(spot)].set(low)
    longest = extent.index(max(extent))
    spot[longest] = (spot[longest] + 1) % extent[longest]
    return entries.at[tuple(spot)].set(top_value)


def levels(rng, extent, pieces, least, high):
    factor_of, own = 1.0, jax.random.fold_in(rng, 6)
    for dim, blocks in pieces:
        draws = jnp.exp(jax.random.uniform(jax.random.fold_in(own, dim), (blocks,), jnp.float32, least / len(pieces), high / len(pieces)))
        factor_of = factor_of * jnp.repeat(draws, extent[dim] // blocks).reshape([-1 if axis == dim else 1 for axis in range(len(extent))])
    return factor_of


def split_up(count, total, most, skew):
    portions = [(1 << 20) // math.isqrt(standing ** skew) + 1 for standing in range(2, count + 1)]
    rest, holding = total - most - (count - 1), [1] * (count - 1)
    while rest > 0:
        free = [i for i in range(count - 1) if holding[i] < most]
        whole, left = sum([portions[i] for i in free]), rest
        for i in free:
            more = min(most - holding[i], max(1, left * portions[i] // whole), rest)
            holding[i] = holding[i] + more
            rest = rest - more
    return np.array([most] + holding)


def ragged_sizes(key, count, total, reach, lean):
    if count == 2:
        one = jax.random.randint(key, (), max(1, total - reach), min(reach, total - 1) + 1)
        return jnp.stack([one, total - one])
    tallies = jnp.asarray(split_up(count, total, reach, lean), jnp.int32)
    pairs = (count - 1) // 2
    donor, sink = tallies[1:1 + 2 * pairs:2], tallies[2:2 + 2 * pairs:2]
    slack = jnp.minimum(donor - 1, reach - sink)
    passed = jax.random.randint(jax.random.fold_in(key, 1), (pairs,), 0, 1 << 20) % (slack + 1)
    tallies = tallies.at[1:1 + 2 * pairs:2].set(donor - passed).at[2:2 + 2 * pairs:2].set(sink + passed)
    return tallies[jax.random.permutation(jax.random.fold_in(key, 2), count)]


def gaussian(own_key, dims, spread, limit, shards=(), kind=jnp.bfloat16):
    array = jax.random.normal(own_key, dims, jnp.float32) * spread
    if len(shards) > 0:
        array = levels(own_key, dims, shards, -0.22, 0.18) * array
    return jnp.clip(array, min=-limit, max=limit).astype(kind)


def setup_inputs(seed: int = 0) -> dict:
    key_of = jax.random.split(jax.random.key(seed), 7)
    return {
        "bins_data": gaussian(key_of[0], (NB, NF, 2, NM), 1.0, 6.0, ((0, 8), (3, 4))),
        "operators": gaussian(key_of[1], (NB, ENT, BLK, BLK), BLK ** -0.5, 0.5, ((0, 8),)),
        "targets": plant(jax.random.randint(key_of[2], (NB, ENT), 0, NH), jax.random.fold_in(key_of[2], 1), 0, NH - 1).astype(jnp.int32),
        "counts": ragged_sizes(key_of[3], NB, NB * ENT // 2, ENT, 2).astype(jnp.int32),
        "layer_index": plant(jax.random.randint(key_of[4], (STEPS, NH // OFFBLK, NM // BLK), 0, LAYERS), jax.random.fold_in(key_of[4], 1), 0, LAYERS - 1).astype(jnp.int32),
        "slowness": jnp.clip(jax.random.uniform(key_of[5], (STEPS, LAYERS), jnp.float32, 0.8, 1.25), 0.8, 1.25),
    }


dz_cells = 2.0
damping = 0.1

def signed_wave(index, length):
    signed = (index + length // 2) % length - length // 2
    return signed.astype(jnp.float32) * (2.0 * math.pi / length)

def root_pair(level):
    magnitude = jnp.sqrt(level * level + damping * damping)
    larger = jnp.sqrt(0.5 * (magnitude + jnp.abs(level)))
    smaller = damping / (2.0 * larger)
    return (jnp.where(level >= 0, larger, smaller), jnp.where(level >= 0, smaller, larger))

def propagator(omega_sq, mid_wave, offset_wave):
    source = 0.5 * (mid_wave - offset_wave)
    receiver = 0.5 * (mid_wave + offset_wave)
    real_s, imag_s = root_pair(omega_sq - source * source)
    real_r, imag_r = root_pair(omega_sq - receiver * receiver)
    decay = jnp.exp(-dz_cells * (imag_s + imag_r))
    turn = dz_cells * (real_s + real_r)
    return (decay * jnp.cos(turn), decay * jnp.sin(turn))

def apply_block(source, weight_block):
    return jnp.dot(source.reshape(-1, weight_block.shape[0]), weight_block, preferred_element_type=jnp.float32).reshape(source.shape)

def reference(bins_data, operators, targets, counts, layer_index, slowness):
    start_field = jnp.zeros((NF, NH, 2, NM), jnp.float32)

    def add_slot(slot_at, current):
        bin_at = slot_at // ENT
        entry_at = slot_at % ENT
        added = apply_block(bins_data[bin_at], operators[bin_at, entry_at])
        live = (entry_at < counts[bin_at]).astype(jnp.float32)
        return current.at[:, targets[bin_at, entry_at]].add(live * added)
    moved = lax.fori_loop(0, NB * ENT, add_slot, start_field)
    field = moved[:, :, 0] + 1j * moved[:, :, 1]
    omega_values = math.pi * (0.1 + 0.8 * (jnp.arange(NF).astype(jnp.float32) + 0.5) / NF)
    offset_wave = signed_wave(jnp.arange(NH), NH)
    mid_wave = signed_wave(jnp.arange(NM), NM)
    phase_real, phase_imag = propagator((omega_values * omega_values)[:, None, None], mid_wave[None, None, :], offset_wave[None, :, None])
    phase = phase_real + 1j * phase_imag
    for depth_step in range(STEPS):
        spectrum = jnp.fft.fft2(field, axes=(1, 2))
        field = jnp.fft.ifft2(spectrum * phase, axes=(1, 2))
        block_slow = slowness[depth_step][layer_index[depth_step]]
        cell_slow = jnp.repeat(jnp.repeat(block_slow, NH // layer_index.shape[1], 0), BLK, 1)
        turn = 2.0 * dz_cells * omega_values[:, None, None] * (cell_slow - 1.0)[None]
        field = field * (jnp.cos(turn) + 1j * jnp.sin(turn))
    return jnp.stack([jnp.real(field), jnp.imag(field)], 2).astype(jnp.float32)
```

```python
import functools
import math

import jax
import jax.numpy as jnp
import numpy as np
from jax import lax
from jax.experimental import pallas as pl
from jax.experimental.pallas import tpu as pltpu
from jax.sharding import PartitionSpec as P

NH = 256
BLK = 128

dz_cells = 2.0
damping = 0.1

HALF = NH // 2
STEP_LOG = 64.0
TOP = 32767.0
GROUP = 8
VMEM = 56 * 1024 * 1024


def signed_wave(index, length):
    signed = (index + length // 2) % length - length // 2
    return signed.astype(jnp.float32) * (2.0 * math.pi / length)


def root_pair(level):
    magnitude = jnp.sqrt(level * level + damping * damping)
    larger = jnp.sqrt(0.5 * (magnitude + jnp.abs(level)))
    smaller = damping / (2.0 * larger)
    return (jnp.where(level >= 0, larger, smaller), jnp.where(level >= 0, smaller, larger))


def propagator(omega_sq, mid_wave, offset_wave):
    source = 0.5 * (mid_wave - offset_wave)
    receiver = 0.5 * (mid_wave + offset_wave)
    real_s, imag_s = root_pair(omega_sq - source * source)
    real_r, imag_r = root_pair(omega_sq - receiver * receiver)
    decay = jnp.exp(-dz_cells * (imag_s + imag_r))
    turn = dz_cells * (real_s + real_r)
    return (decay * jnp.cos(turn), decay * jnp.sin(turn))


def halves_np(table):
    high = table.astype(np.float32).astype(jnp.bfloat16)
    low = (table - high.astype(np.float64)).astype(np.float32).astype(jnp.bfloat16)
    return high, low


def block_tables():
    index = np.arange(BLK)
    angles = 2.0 * np.pi * (np.outer(index, index) % BLK) / BLK
    cos, sin = np.cos(angles), np.sin(angles)
    upper = np.block([[cos, sin], [-sin, cos]])
    lower = np.block([[cos, -sin], [sin, cos]])
    tables = []
    for axis, pair in ((1, (upper, lower)), (0, (lower, upper))):
        for table in pair:
            high, low = halves_np(table)
            tables.append(np.concatenate([high, high, low], axis=axis))
    return tables


def twiddle_tables(outer):
    ka, b = np.arange(outer)[:, None], np.arange(BLK)[None, :]
    angles = 2.0 * np.pi * ka * b / (outer * BLK)
    middle = np.stack([np.cos(angles), np.sin(angles)]).astype(np.float32)
    rows = 2.0 * np.pi * np.arange(HALF) / NH
    offset = np.stack([np.cos(rows), np.sin(rows)]).astype(np.float32)
    return middle, np.broadcast_to(offset[:, :, None], (2, HALF, BLK)).copy()


def halves(value):
    high = value.astype(jnp.bfloat16)
    return high, (value - high.astype(jnp.float32)).astype(jnp.bfloat16)


def dot(left, right):
    return jnp.dot(left, right, preferred_element_type=jnp.float32)


def left_product(table, value):
    high, low = halves(value)
    return dot(table, jnp.concatenate([high, low, high], axis=0))


def right_product(value, table):
    high, low = halves(value)
    return dot(jnp.concatenate([high, low, high], axis=1), table)


def cmul(real_a, imag_a, real_b, imag_b):
    return real_a * real_b - imag_a * imag_b, real_a * imag_b + imag_a * real_b


def small_transform(values, sign):
    count = len(values)
    if count == 1:
        return values
    even = small_transform(values[0::2], sign)
    odd = small_transform(values[1::2], sign)
    first, second = [], []
    for k in range(count // 2):
        er, ei = even[k]
        xr, xi = odd[k]
        if k == 0:
            tr, ti = xr, xi
        elif 4 * k == count:
            tr, ti = (-xi, xr) if sign > 0 else (xi, -xr)
        else:
            c, s = math.cos(2 * math.pi * k / count), sign * math.sin(2 * math.pi * k / count)
            if 8 * k == count:
                tr, ti = ((xr - xi) * c, (xr + xi) * c) if sign > 0 else ((xr + xi) * c, (xi - xr) * c)
            elif 8 * k == 3 * count:
                tr, ti = ((xr + xi) * c, (xi - xr) * c) if sign > 0 else ((xr - xi) * c, (xr + xi) * c)
            else:
                tr, ti = xr * c - xi * s, xr * s + xi * c
        first.append((er + tr, ei + ti))
        second.append((er - tr, ei - ti))
    return first + second


def scale_code(biggest):
    return (jnp.floor(jnp.log(jnp.maximum(biggest, 1e-30)) * STEP_LOG) + 1.0).astype(jnp.int32)


def scale_of(code):
    return jnp.exp(code.astype(jnp.float32) * (1.0 / STEP_LOG)) * (1.0 / TOP)


def inverse_scale_of(code):
    return jnp.exp(code.astype(jnp.float32) * (-1.0 / STEP_LOG)) * TOP


def coded(value, inverse):
    return jnp.floor(value * inverse + 0.5).astype(jnp.int32)


def packed(high, low):
    return (high << 16) | (low & 0xFFFF)


def unpacked(word):
    return (word >> 16).astype(jnp.float32), ((word << 16) >> 16).astype(jnp.float32)


def contribution_kernel(slot_ref, bin_ref, data_ref, weight_ref, out_ref, held):
    freqs, groups = out_ref.shape[:2]
    outer = out_ref.shape[2] - 1

    @pl.loop(0, groups)
    def _(group):
        for at in range(GROUP):
            slot = slot_ref[group * GROUP + at]
            source = bin_ref[group * GROUP + at]
            held[pl.ds(at, data_ref.shape[1], GROUP), :] = dot(data_ref[source], weight_ref[slot])
        for f in range(freqs):
            base = f * 2 * outer * GROUP
            biggest = jnp.abs(held[pl.ds(base, GROUP), :])
            for at in range(1, 2 * outer):
                biggest = jnp.maximum(biggest, jnp.abs(held[pl.ds(base + at * GROUP, GROUP), :]))
            code = scale_code(biggest)
            inverse = inverse_scale_of(code)
            for a in range(outer):
                real = held[pl.ds(base + a * GROUP, GROUP), :]
                imag = held[pl.ds(base + (outer + a) * GROUP, GROUP), :]
                out_ref[f, group, a] = packed(coded(real, inverse), coded(imag, inverse))
            out_ref[f, group, outer] = code


def column_of(plane, a):
    lanes = pl.ds(pl.multiple_of(a * BLK, BLK), BLK)
    return jnp.concatenate(
        [
            jnp.concatenate([plane[p, 0, :, lanes], plane[p, 1, :, lanes]], axis=0)
            for p in range(2)
        ],
        axis=1,
    )


def store_column(plane, a, value):
    lanes = pl.ds(pl.multiple_of(a * BLK, BLK), BLK)
    for p in range(2):
        for c in range(2):
            plane[p, c, :, lanes] = value[c * HALF : (c + 1) * HALF, p * BLK : (p + 1) * BLK]


def offset_forward(low_half, high_half, upper, turn):
    first = [low_half[c] + high_half[c] for c in range(2)]
    second = cmul(low_half[0] - high_half[0], low_half[1] - high_half[1], turn[0], -turn[1])
    value = jnp.concatenate(
        [jnp.concatenate(first, axis=0), jnp.concatenate(second, axis=0)], axis=1
    )
    return left_product(upper[...], value)


def offset_inverse(value, lower, turn):
    value = left_product(lower[...], value)
    first = value[:HALF, :BLK], value[HALF:, :BLK]
    second = cmul(value[:HALF, BLK:], value[HALF:, BLK:], turn[0], turn[1])
    return (
        [first[c] + second[c] for c in range(2)],
        [first[c] - second[c] for c in range(2)],
    )


def layer_turn(halves_in, layer_ref, step, a):
    blocks = layer_ref.shape[2]
    tall = NH // blocks
    results = []
    for p in range(2):
        parts = [[], []]
        for at in range(HALF // tall):
            block = p * (HALF // tall) + at
            cos, sin = layer_ref[0, step, block, a], layer_ref[1, step, block, a]
            rows = slice(at * tall, (at + 1) * tall)
            real, imag = cmul(halves_in[p][0][rows], halves_in[p][1][rows], cos, sin)
            parts[0].append(real)
            parts[1].append(imag)
        results.append([jnp.concatenate(part, axis=0) for part in parts])
    return results


def midpoint_pass(plane, out, phase_refs, forward, inverse, middle_ref, rows):
    outer = middle_ref.shape[1]
    per_half = HALF // rows

    @pl.loop(0, 2 * per_half, unroll=2)
    def _(at):
        p = at // per_half
        here = pl.ds(pl.multiple_of((at % per_half) * rows, rows), rows)
        there = pl.ds(pl.multiple_of(at * rows, rows), rows)
        lanes = [slice(a * BLK, (a + 1) * BLK) for a in range(outer)]
        values = [(plane[p, 0, here, lane], plane[p, 1, here, lane]) for lane in lanes]
        values = small_transform(values, -1)
        turned = []
        for a in range(outer):
            real, imag = cmul(*values[a], middle_ref[0, a : a + 1], -middle_ref[1, a : a + 1])
            turned.append(jnp.concatenate([real, imag], axis=1))
        value = right_product(jnp.concatenate(turned, axis=0), forward[...])
        turned = []
        for a in range(outer):
            part = value[a * rows : (a + 1) * rows]
            real, imag = cmul(
                part[:, :BLK], part[:, BLK:], phase_refs[0][there, lanes[a]], phase_refs[1][there, lanes[a]]
            )
            turned.append(jnp.concatenate([real, imag], axis=1))
        value = right_product(jnp.concatenate(turned, axis=0), inverse[...])
        values = []
        for a in range(outer):
            part = value[a * rows : (a + 1) * rows]
            values.append(
                cmul(part[:, :BLK], part[:, BLK:], middle_ref[0, a : a + 1], middle_ref[1, a : a + 1])
            )
        values = small_transform(values, 1)
        for a in range(outer):
            out[p, 0, here, lanes[a]] = values[a][0]
            out[p, 1, here, lanes[a]] = values[a][1]


def march_kernel(
    layer_ref, code_ref, pick_ref, phase_real, phase_imag, rows_forward, rows_inverse, lanes_forward,
    lanes_inverse, middle_ref, offset_ref, out_ref, plane, other, scales, coded_rows,
):
    sources, groups = code_ref.shape[:2]
    outer = middle_ref.shape[1]
    steps = layer_ref.shape[1]
    slots = sources * groups * GROUP
    turn = offset_ref[0], offset_ref[1]

    scales[...] = scale_of(code_ref[:, :, outer].reshape(slots, BLK))

    @pl.loop(0, outer, unroll=2)
    def _(a):
        real, imag = unpacked(code_ref[:, :, a].reshape(slots, BLK))
        scale = scales[...]
        value = jnp.concatenate([real * scale, imag * scale], axis=1)
        moved = dot(pick_ref[...], jnp.concatenate(halves(value), axis=0))
        low_half = [moved[:HALF, :BLK], moved[:HALF, BLK:]]
        high_half = [moved[HALF:, :BLK], moved[HALF:, BLK:]]
        store_column(plane, a, offset_forward(low_half, high_half, rows_forward, turn))

    for step in range(steps):
        midpoint_pass(
            plane, other, (phase_real, phase_imag), lanes_forward, lanes_inverse, middle_ref, 16
        )
        if step < steps - 1:

            @pl.loop(0, outer, unroll=2)
            def _(a):
                parts = offset_inverse(column_of(other, a), rows_inverse, turn)
                parts = layer_turn(parts, layer_ref, step, a)
                store_column(plane, a, offset_forward(parts[0], parts[1], rows_forward, turn))

    dests = out_ref.shape[0]
    here = outer // dests

    @pl.loop(0, dests)
    def _(dest):
        for at in range(here):
            a = dest * here + at
            parts = offset_inverse(column_of(other, a), rows_inverse, turn)
            parts = layer_turn(parts, layer_ref, steps - 1, a)
            for c in range(2):
                both = jnp.maximum(jnp.abs(parts[0][c]), jnp.abs(parts[1][c]))
                code = scale_code(jnp.max(both, axis=0, keepdims=True))
                inverse = inverse_scale_of(code)
                words = packed(coded(parts[0][c], inverse), coded(parts[1][c], inverse))
                row = at * 2 + c
                coded_rows[pl.ds(row, HALF, 2 * here), :] = words
                coded_rows[pl.ds(HALF * 2 * here + row, 1), :] = code
        out_ref[dest] = coded_rows[...]


def result_kernel(code_ref, out_ref):
    per = code_ref.shape[1] - 1
    scale = scale_of(code_ref[0, per])
    first, second = unpacked(code_ref[0, :per])
    out_ref[0, :per] = first * scale[None]
    out_ref[0, per:] = second * scale[None]


def slot_lists(counts_all, targets_all, bins_local, fl, per_device, room):
    offs = counts_all.shape[0] // bins_local
    entries = targets_all.shape[1]
    counts_in = counts_all.reshape(offs, bins_local)
    live = jnp.sum(counts_in, axis=1)
    quarter = jnp.arange(fl, dtype=jnp.int32)
    held = (live[None, :] - quarter[:, None] + fl - 1) // fl
    upto = jnp.sum(
        jnp.where(jnp.arange(offs)[None, :] <= jnp.arange(offs)[:, None], held[:, None, :], 0), axis=2
    )
    at = jnp.arange(room, dtype=jnp.int32)
    past = (at[None, :, None] >= upto[:, None, :]).astype(jnp.int32)
    off_at = jnp.sum(past, axis=2)
    valid = off_at < offs
    off_at = jnp.minimum(off_at, offs - 1)
    start = jnp.sum(past * held[:, None, :], axis=2)
    nth = jnp.clip(at[None, :] - start, 0, per_device - 1)
    entry = nth * fl + quarter[:, None]
    bin_at = off_at * bins_local
    mine = off_at[:, :, None] == jnp.arange(offs)[None, None, :]
    for b in range(bins_local - 1):
        size = jnp.sum(jnp.where(mine, counts_in[None, None, :, b], 0), axis=2)
        over = (bin_at == off_at * bins_local + b) & (entry >= size)
        bin_at = bin_at + over
        entry = entry - jnp.where(over, size, 0)
    flat = bin_at * entries + entry
    total = targets_all.size
    picks = flat[:, :, None] == jnp.arange(total)[None, None, :]
    target = jnp.sum(jnp.where(picks, targets_all.reshape(1, 1, total), 0), axis=2)
    target = jnp.where(valid, target, -1)
    return off_at * per_device + nth, bin_at, target


def take_kernel(place_ref, source_ref, out_ref):
    out_ref[...] = source_ref[...]


def local(bins_data, operators, targets, counts, layer_index, slowness):
    off_count = lax.axis_size("off")
    mid_count = lax.axis_size("mid")
    bins_local, freq_total, _, mid_local = bins_data.shape
    entries = operators.shape[1]
    bins_total = bins_local * off_count
    fl = freq_total // off_count
    total_mid = mid_local * mid_count
    outer = total_mid // BLK
    mid_at, off_at = lax.axis_index("mid"), lax.axis_index("off")
    assert mid_count % fl == 0 and (bins_local * entries) % fl == 0
    mine = mid_at % fl
    rounds = mid_count // fl
    groups = (
        None if rounds == 1 else [list(range(g * fl, (g + 1) * fl)) for g in range(rounds)]
    )

    per_device = bins_local * entries // fl
    local_slot = jnp.arange(per_device, dtype=jnp.int32) * fl + mine
    place = local_slot
    for b in range(bins_local - 1):
        size = counts[b]
        first = b * entries
        place = jnp.where(place - first >= size, jnp.where(place >= first, place + entries - size, place), place)
    place = jnp.clip(place, 0, bins_local * entries - 1)
    own = pl.pallas_call(
        take_kernel,
        grid_spec=pltpu.PrefetchScalarGridSpec(
            num_scalar_prefetch=1,
            grid=(per_device,),
            in_specs=[pl.BlockSpec((1, BLK, BLK), lambda n, place: (place[n], 0, 0))],
            out_specs=pl.BlockSpec((1, BLK, BLK), lambda n, place: (n, 0, 0)),
        ),
        out_shape=jax.ShapeDtypeStruct((per_device, BLK, BLK), jnp.bfloat16),
        name="take_own",
    )(place, operators.reshape(bins_local * entries, BLK, BLK))
    weights = lax.all_gather(own, "off", axis=0, tiled=True)

    pairs = fl * 2

    def extra(whole_numbers, copies):
        flat = whole_numbers.astype(jnp.bfloat16).reshape(1, 1, 1, -1)
        flat = jnp.pad(flat, ((0, 0), (0, 0), (0, pairs - 1), (0, mid_local - flat.shape[3])))
        return jnp.broadcast_to(flat, (1, copies, pairs, mid_local))

    lists = jnp.concatenate([counts[:, None], targets], axis=1)
    data = bins_data.reshape(bins_local, off_count, pairs, mid_local)
    data = jnp.concatenate([data, extra(lists, off_count)], axis=0)
    data = lax.all_to_all(data, "off", split_axis=1, concat_axis=0, tiled=True)
    data = data.reshape(off_count, bins_local + 1, pairs, mid_local)
    lists = data[:, bins_local, 0, : lists.size].astype(jnp.int32).reshape(bins_total, 1 + entries)
    data = data[:, :bins_local].reshape(bins_total, pairs, mid_local)
    data = jnp.concatenate([data, extra(layer_index, 1)[0]], axis=0)
    data = lax.all_gather(data, "mid", axis=0)
    layers = data[:, bins_total, 0, : layer_index.size].astype(jnp.int32)
    layers = layers.reshape(mid_count, *layer_index.shape).transpose(1, 2, 0, 3)
    layers = layers.reshape(*layer_index.shape[:2], outer)
    data = data[:, :bins_total].reshape(mid_count, bins_total, pairs, mid_local // BLK, BLK)
    data = data.transpose(1, 2, 0, 3, 4).reshape(bins_total, pairs * outer, BLK)

    live_total = bins_total * entries // 2
    room = -(-(live_total + (fl - 1) * off_count) // fl)
    room = min(-(-room // GROUP) * GROUP, per_device * off_count)
    slots, bins, goal = slot_lists(lists[:, 0], lists[:, 1:], bins_local, fl, per_device, room)
    pick = (
        jnp.tile(goal.reshape(1, fl * room), (1, 2))
        == lax.broadcasted_iota(jnp.int32, (NH, 2 * fl * room), 0)
    ).astype(jnp.bfloat16)

    own_slots = lax.dynamic_index_in_dim(slots, mine, 0, False)
    own_bins = lax.dynamic_index_in_dim(bins, mine, 0, False)
    list_groups = room // GROUP
    smem = pl.BlockSpec(memory_space=pltpu.SMEM)
    vmem = pl.BlockSpec(memory_space=pltpu.VMEM)
    terms = pl.pallas_call(
        contribution_kernel,
        in_specs=[smem, smem, vmem, vmem],
        out_specs=vmem,
        out_shape=jax.ShapeDtypeStruct((fl, list_groups, outer + 1, GROUP, BLK), jnp.int32),
        scratch_shapes=[pltpu.VMEM((fl * 2 * outer * GROUP, BLK), jnp.float32)],
        compiler_params=pltpu.CompilerParams(vmem_limit_bytes=VMEM),
        name="contributions",
    )(own_slots, own_bins, data, weights)
    terms, freq_at = lax.optimization_barrier((terms, off_at * fl + mine))
    omega = math.pi * (0.1 + 0.8 * (freq_at.astype(jnp.float32) + 0.5) / freq_total)
    row = lax.broadcasted_iota(jnp.int32, (NH, total_mid), 0)
    lane = lax.broadcasted_iota(jnp.int32, (NH, total_mid), 1)
    offset_wave = signed_wave(2 * (row % HALF) + row // HALF, NH)
    mid_wave = signed_wave(lane // BLK + outer * (lane % BLK), total_mid)
    phase_real, phase_imag = propagator(omega * omega, mid_wave, offset_wave)
    phase_real, phase_imag = (x * (1.0 / (NH * total_mid)) for x in (phase_real, phase_imag))

    layer_total = slowness.shape[1]
    chosen = layers[..., None] == jnp.arange(layer_total)
    slow = jnp.sum(jnp.where(chosen, slowness[:, None, None, :], 0.0), axis=-1)
    turn = 2.0 * dz_cells * omega * (slow - 1.0)
    layer_turns = jnp.stack([jnp.cos(turn), jnp.sin(turn)])

    terms = lax.all_to_all(
        terms, "mid", split_axis=0, concat_axis=0, axis_index_groups=groups, tiled=True
    )

    middle, offset_turn = twiddle_tables(outer)
    here = mid_local // BLK
    rows_out = (HALF + 1) * 2 * here
    sent = pl.pallas_call(
        march_kernel,
        in_specs=[smem] + [vmem] * 10,
        out_specs=vmem,
        out_shape=jax.ShapeDtypeStruct((mid_count, rows_out, BLK), jnp.int32),
        scratch_shapes=[
            pltpu.VMEM((2, 2, HALF, total_mid), jnp.float32),
            pltpu.VMEM((2, 2, HALF, total_mid), jnp.float32),
            pltpu.VMEM((fl * room, BLK), jnp.float32),
            pltpu.VMEM((rows_out, BLK), jnp.int32),
        ],
        compiler_params=pltpu.CompilerParams(vmem_limit_bytes=VMEM),
        name="march",
    )(
        layer_turns, terms, pick, phase_real, phase_imag, *[jnp.asarray(t) for t in block_tables()],
        jnp.asarray(middle), jnp.asarray(offset_turn),
    )
    if rounds > 1:
        sent = lax.dynamic_slice_in_dim(sent, (mid_at // fl) * fl, fl, 0)
    got = lax.all_to_all(
        sent, "mid", split_axis=0, concat_axis=0, axis_index_groups=groups, tiled=True
    )
    got = got.reshape(fl, HALF + 1, 2 * here, BLK)
    field = pl.pallas_call(
        result_kernel,
        grid=(fl,),
        in_specs=[pl.BlockSpec((1, HALF + 1, 2 * here, BLK), lambda f: (f, 0, 0, 0))],
        out_specs=pl.BlockSpec((1, NH, 2 * here, BLK), lambda f: (f, 0, 0, 0)),
        out_shape=jax.ShapeDtypeStruct((fl, NH, 2 * here, BLK), jnp.float32),
        name="result",
    )(got)
    field = field.reshape(fl, NH, here, 2, BLK).transpose(0, 1, 3, 2, 4)
    return field.reshape(fl, NH, 2, mid_local)


def solution(mesh):
    in_specs = (
        P("off", None, None, "mid"),
        P("off", None, None, None),
        P("off", None),
        P("off"),
        P(None, None, "mid"),
        P(),
    )
    out_specs = P("off", None, None, "mid")
    return jax.shard_map(local, mesh=mesh, in_specs=in_specs, out_specs=out_specs, check_vma=False)
```

```python
import functools
import math

import jax
import jax.numpy as jnp
import numpy as np
from jax import lax
from jax.experimental import pallas as pl
from jax.experimental.pallas import tpu as pltpu
from jax.sharding import PartitionSpec as P

NH = 256
BLK = 128

dz_cells = 2.0
damping = 0.1

HALF = NH // 2
STEP_LOG = 64.0
TOP = 32767.0
GROUP = 8
VMEM = 56 * 1024 * 1024


def signed_wave(index, length):
    signed = (index + length // 2) % length - length // 2
    return signed.astype(jnp.float32) * (2.0 * math.pi / length)


def root_pair(level):
    magnitude = jnp.sqrt(level * level + damping * damping)
    larger = jnp.sqrt(0.5 * (magnitude + jnp.abs(level)))
    smaller = damping / (2.0 * larger)
    return (jnp.where(level >= 0, larger, smaller), jnp.where(level >= 0, smaller, larger))


def propagator(omega_sq, mid_wave, offset_wave):
    source = 0.5 * (mid_wave - offset_wave)
    receiver = 0.5 * (mid_wave + offset_wave)
    real_s, imag_s = root_pair(omega_sq - source * source)
    real_r, imag_r = root_pair(omega_sq - receiver * receiver)
    decay = jnp.exp(-dz_cells * (imag_s + imag_r))
    turn = dz_cells * (real_s + real_r)
    return (decay * jnp.cos(turn), decay * jnp.sin(turn))


def halves_np(table):
    high = table.astype(np.float32).astype(jnp.bfloat16)
    low = (table - high.astype(np.float64)).astype(np.float32).astype(jnp.bfloat16)
    return high, low


def block_tables():
    index = np.arange(BLK)
    angles = 2.0 * np.pi * (np.outer(index, index) % BLK) / BLK
    cos, sin = np.cos(angles), np.sin(angles)
    upper = np.block([[cos, sin], [-sin, cos]])
    lower = np.block([[cos, -sin], [sin, cos]])
    tables = []
    for axis, pair in ((1, (upper, lower)), (0, (lower, upper))):
        for table in pair:
            high, low = halves_np(table)
            tables.append(np.concatenate([high, high, low], axis=axis))
    return tables


def twiddle_tables(outer):
    ka, b = np.arange(outer)[:, None], np.arange(BLK)[None, :]
    angles = 2.0 * np.pi * ka * b / (outer * BLK)
    middle = np.stack([np.cos(angles), np.sin(angles)]).astype(np.float32)
    rows = 2.0 * np.pi * np.arange(HALF) / NH
    offset = np.stack([np.cos(rows), np.sin(rows)]).astype(np.float32)
    return middle, np.broadcast_to(offset[:, :, None], (2, HALF, BLK)).copy()


def halves(value):
    high = value.astype(jnp.bfloat16)
    return high, (value - high.astype(jnp.float32)).astype(jnp.bfloat16)


def dot(left, right):
    return jnp.dot(left, right, preferred_element_type=jnp.float32)


def left_product(table, value):
    high, low = halves(value)
    return dot(table, jnp.concatenate([high, low, high], axis=0))


def right_product(value, table):
    high, low = halves(value)
    return dot(jnp.concatenate([high, low, high], axis=1), table)


def cmul(real_a, imag_a, real_b, imag_b):
    return real_a * real_b - imag_a * imag_b, real_a * imag_b + imag_a * real_b


def small_transform(values, sign):
    count = len(values)
    if count == 1:
        return values
    even = small_transform(values[0::2], sign)
    odd = small_transform(values[1::2], sign)
    first, second = [], []
    for k in range(count // 2):
        er, ei = even[k]
        xr, xi = odd[k]
        if k == 0:
            tr, ti = xr, xi
        elif 4 * k == count:
            tr, ti = (-xi, xr) if sign > 0 else (xi, -xr)
        else:
            c, s = math.cos(2 * math.pi * k / count), sign * math.sin(2 * math.pi * k / count)
            if 8 * k == count:
                tr, ti = ((xr - xi) * c, (xr + xi) * c) if sign > 0 else ((xr + xi) * c, (xi - xr) * c)
            elif 8 * k == 3 * count:
                tr, ti = ((xr + xi) * c, (xi - xr) * c) if sign > 0 else ((xr - xi) * c, (xr + xi) * c)
            else:
                tr, ti = xr * c - xi * s, xr * s + xi * c
        first.append((er + tr, ei + ti))
        second.append((er - tr, ei - ti))
    return first + second


def scale_code(biggest):
    return (jnp.floor(jnp.log(jnp.maximum(biggest, 1e-30)) * STEP_LOG) + 1.0).astype(jnp.int32)


def scale_of(code):
    return jnp.exp(code.astype(jnp.float32) * (1.0 / STEP_LOG)) * (1.0 / TOP)


def inverse_scale_of(code):
    return jnp.exp(code.astype(jnp.float32) * (-1.0 / STEP_LOG)) * TOP


def coded(value, inverse):
    return jnp.floor(value * inverse + 0.5).astype(jnp.int32)


def packed(high, low):
    return (high << 16) | (low & 0xFFFF)


def unpacked(word):
    return (word >> 16).astype(jnp.float32), ((word << 16) >> 16).astype(jnp.float32)


def contribution_kernel(
    slot_ref, bin_ref, data_ref, near_ref, far_ref, out_ref, held, weight_ref, near_sem, far_sem
):
    count = near_ref.shape[0]
    near = pltpu.make_async_copy(near_ref, weight_ref.at[pl.ds(0, count)], near_sem)
    far = pltpu.make_async_copy(far_ref, weight_ref.at[pl.ds(count, count)], far_sem)
    near.start()
    far.start()
    near.wait()
    far.wait()
    freqs, groups = out_ref.shape[:2]
    outer = out_ref.shape[2] - 1

    @pl.loop(0, groups)
    def _(group):
        for at in range(GROUP):
            slot = slot_ref[group * GROUP + at]
            source = bin_ref[group * GROUP + at]
            held[pl.ds(at, data_ref.shape[1], GROUP), :] = dot(data_ref[source], weight_ref[slot])
        for f in range(freqs):
            base = f * 2 * outer * GROUP
            biggest = jnp.abs(held[pl.ds(base, GROUP), :])
            for at in range(1, 2 * outer):
                biggest = jnp.maximum(biggest, jnp.abs(held[pl.ds(base + at * GROUP, GROUP), :]))
            code = scale_code(biggest)
            inverse = inverse_scale_of(code)
            for a in range(outer):
                real = held[pl.ds(base + a * GROUP, GROUP), :]
                imag = held[pl.ds(base + (outer + a) * GROUP, GROUP), :]
                out_ref[f, group, a] = packed(coded(real, inverse), coded(imag, inverse))
            out_ref[f, group, outer] = code


def column_of(plane, a):
    lanes = pl.ds(pl.multiple_of(a * BLK, BLK), BLK)
    return jnp.concatenate(
        [
            jnp.concatenate([plane[p, 0, :, lanes], plane[p, 1, :, lanes]], axis=0)
            for p in range(2)
        ],
        axis=1,
    )


def store_column(plane, a, value):
    lanes = pl.ds(pl.multiple_of(a * BLK, BLK), BLK)
    for p in range(2):
        for c in range(2):
            plane[p, c, :, lanes] = value[c * HALF : (c + 1) * HALF, p * BLK : (p + 1) * BLK]


def offset_forward(low_half, high_half, upper, turn):
    first = [low_half[c] + high_half[c] for c in range(2)]
    second = cmul(low_half[0] - high_half[0], low_half[1] - high_half[1], turn[0], -turn[1])
    value = jnp.concatenate(
        [jnp.concatenate(first, axis=0), jnp.concatenate(second, axis=0)], axis=1
    )
    return left_product(upper[...], value)


def offset_inverse(value, lower, turn):
    value = left_product(lower[...], value)
    first = value[:HALF, :BLK], value[HALF:, :BLK]
    second = cmul(value[:HALF, BLK:], value[HALF:, BLK:], turn[0], turn[1])
    return (
        [first[c] + second[c] for c in range(2)],
        [first[c] - second[c] for c in range(2)],
    )


def layer_turn(halves_in, layer_ref, step, a):
    blocks = layer_ref.shape[2]
    tall = NH // blocks
    results = []
    for p in range(2):
        parts = [[], []]
        for at in range(HALF // tall):
            block = p * (HALF // tall) + at
            cos, sin = layer_ref[0, step, block, a], layer_ref[1, step, block, a]
            rows = slice(at * tall, (at + 1) * tall)
            real, imag = cmul(halves_in[p][0][rows], halves_in[p][1][rows], cos, sin)
            parts[0].append(real)
            parts[1].append(imag)
        results.append([jnp.concatenate(part, axis=0) for part in parts])
    return results


def midpoint_pass(plane, out, phase_refs, forward, inverse, middle_ref, rows):
    outer = middle_ref.shape[1]
    per_half = HALF // rows

    @pl.loop(0, 2 * per_half, unroll=2)
    def _(at):
        p = at // per_half
        here = pl.ds(pl.multiple_of((at % per_half) * rows, rows), rows)
        there = pl.ds(pl.multiple_of(at * rows, rows), rows)
        lanes = [slice(a * BLK, (a + 1) * BLK) for a in range(outer)]
        values = [(plane[p, 0, here, lane], plane[p, 1, here, lane]) for lane in lanes]
        values = small_transform(values, -1)
        turned = []
        for a in range(outer):
            real, imag = cmul(*values[a], middle_ref[0, a : a + 1], -middle_ref[1, a : a + 1])
            turned.append(jnp.concatenate([real, imag], axis=1))
        value = right_product(jnp.concatenate(turned, axis=0), forward[...])
        turned = []
        for a in range(outer):
            part = value[a * rows : (a + 1) * rows]
            real, imag = cmul(
                part[:, :BLK], part[:, BLK:], phase_refs[0][there, lanes[a]], phase_refs[1][there, lanes[a]]
            )
            turned.append(jnp.concatenate([real, imag], axis=1))
        value = right_product(jnp.concatenate(turned, axis=0), inverse[...])
        values = []
        for a in range(outer):
            part = value[a * rows : (a + 1) * rows]
            values.append(
                cmul(part[:, :BLK], part[:, BLK:], middle_ref[0, a : a + 1], middle_ref[1, a : a + 1])
            )
        values = small_transform(values, 1)
        for a in range(outer):
            out[p, 0, here, lanes[a]] = values[a][0]
            out[p, 1, here, lanes[a]] = values[a][1]


def march_kernel(
    layer_ref, code_ref, pick_ref, phase_real, phase_imag, rows_forward, rows_inverse, lanes_forward,
    lanes_inverse, middle_ref, offset_ref, other, plane, scales,
):
    sources, groups = code_ref.shape[:2]
    outer = middle_ref.shape[1]
    steps = layer_ref.shape[1]
    slots = sources * groups * GROUP
    turn = offset_ref[0], offset_ref[1]

    scales[...] = scale_of(code_ref[:, :, outer].reshape(slots, BLK))

    @pl.loop(0, outer, unroll=2)
    def _(a):
        real, imag = unpacked(code_ref[:, :, a].reshape(slots, BLK))
        scale = scales[...]
        value = jnp.concatenate([real * scale, imag * scale], axis=1)
        moved = dot(pick_ref[...], jnp.concatenate(halves(value), axis=0))
        low_half = [moved[:HALF, :BLK], moved[:HALF, BLK:]]
        high_half = [moved[HALF:, :BLK], moved[HALF:, BLK:]]
        store_column(plane, a, offset_forward(low_half, high_half, rows_forward, turn))

    for step in range(steps):
        midpoint_pass(
            plane, other, (phase_real, phase_imag), lanes_forward, lanes_inverse, middle_ref, 32
        )
        if step < steps - 1:

            @pl.loop(0, outer, unroll=2)
            def _(a):
                parts = offset_inverse(column_of(other, a), rows_inverse, turn)
                parts = layer_turn(parts, layer_ref, step, a)
                store_column(plane, a, offset_forward(parts[0], parts[1], rows_forward, turn))


def finish_kernel(dest_ref, layer_ref, plane_ref, rows_inverse, offset_ref, out_ref):
    here = plane_ref.shape[3] // BLK
    turn = offset_ref[0], offset_ref[1]
    for at in range(here):
        parts = offset_inverse(column_of(plane_ref, at), rows_inverse, turn)
        parts = layer_turn(parts, layer_ref, layer_ref.shape[1] - 1, dest_ref[0] * here + at)
        for c in range(2):
            both = jnp.maximum(jnp.abs(parts[0][c]), jnp.abs(parts[1][c]))
            code = scale_code(jnp.max(both, axis=0, keepdims=True))
            inverse = inverse_scale_of(code)
            words = packed(coded(parts[0][c], inverse), coded(parts[1][c], inverse))
            row = at * 2 + c
            out_ref[pl.ds(row, HALF, 2 * here), :] = words
            out_ref[pl.ds(HALF * 2 * here + row, 1), :] = code


def result_kernel(freq_ref, code_ref, *rest):
    out_ref = rest[-1]
    tall = out_ref.shape[2]
    per = code_ref.shape[0] // tall - 1
    scale = scale_of(code_ref[per * tall :])
    first, second = unpacked(code_ref[: per * tall].reshape(per, tall, BLK))
    out_ref[0, :per] = first * scale[None]
    out_ref[0, per:] = second * scale[None]


def take_kernel(mine_ref, counts_ref, source_ref, out_ref, sems):
    taken, entries = out_ref.shape[0], source_ref.shape[1]
    bins_here, stride = source_ref.shape[0], source_ref.shape[0] * entries // taken
    copies = []
    for n in range(taken):
        entry, bin_at = n * stride + mine_ref[0], 0
        for b in range(bins_here - 1):
            over = (bin_at == b) & (entry >= counts_ref[b])
            entry = jnp.where(over, entry - counts_ref[b], entry)
            bin_at = jnp.where(over, b + 1, bin_at)
        entry = jnp.minimum(entry, entries - 1)
        copies.append(
            pltpu.make_async_copy(source_ref.at[bin_at, entry], out_ref.at[n], sems.at[n])
        )
        copies[-1].start()
    for copy in copies:
        copy.wait()


def slot_lists(counts_all, targets_all, bins_local, fl, per_device, room):
    offs = counts_all.shape[0] // bins_local
    entries = targets_all.shape[1]
    counts_in = counts_all.reshape(offs, bins_local)
    live = jnp.sum(counts_in, axis=1)
    quarter = jnp.arange(fl, dtype=jnp.int32)
    held = (live[None, :] - quarter[:, None] + fl - 1) // fl
    upto = jnp.sum(
        jnp.where(jnp.arange(offs)[None, :] <= jnp.arange(offs)[:, None], held[:, None, :], 0), axis=2
    )
    at = jnp.arange(room, dtype=jnp.int32)
    past = (at[None, :, None] >= upto[:, None, :]).astype(jnp.int32)
    off_at = jnp.sum(past, axis=2)
    valid = off_at < offs
    off_at = jnp.minimum(off_at, offs - 1)
    start = jnp.sum(past * held[:, None, :], axis=2)
    nth = jnp.clip(at[None, :] - start, 0, per_device - 1)
    entry = nth * fl + quarter[:, None]
    bin_at = off_at * bins_local
    mine = off_at[:, :, None] == jnp.arange(offs)[None, None, :]
    for b in range(bins_local - 1):
        size = jnp.sum(jnp.where(mine, counts_in[None, None, :, b], 0), axis=2)
        over = (bin_at == off_at * bins_local + b) & (entry >= size)
        bin_at = bin_at + over
        entry = entry - jnp.where(over, size, 0)
    flat = bin_at * entries + entry
    total = targets_all.size
    picks = flat[:, :, None] == jnp.arange(total)[None, None, :]
    target = jnp.sum(jnp.where(picks, targets_all.reshape(1, 1, total), 0), axis=2)
    target = jnp.where(valid, target, -1)
    return off_at, nth, bin_at, target


def local(bins_data, operators, targets, counts, layer_index, slowness):
    off_count = lax.axis_size("off")
    mid_count = lax.axis_size("mid")
    bins_local, freq_total, _, mid_local = bins_data.shape
    entries = operators.shape[1]
    bins_total = bins_local * off_count
    fl = freq_total // off_count
    total_mid = mid_local * mid_count
    outer = total_mid // BLK
    mid_at, off_at = lax.axis_index("mid"), lax.axis_index("off")
    assert mid_count % fl == 0 and (bins_local * entries) % fl == 0
    mine = mid_at % fl
    rounds = mid_count // fl
    groups = (
        None if rounds == 1 else [list(range(g * fl, (g + 1) * fl)) for g in range(rounds)]
    )

    per_device = bins_local * entries // fl
    smem = pl.BlockSpec(memory_space=pltpu.SMEM)
    vmem = pl.BlockSpec(memory_space=pltpu.VMEM)
    hbm = pl.BlockSpec(memory_space=pl.ANY)
    own = pl.pallas_call(
        take_kernel,
        in_specs=[smem, smem, hbm],
        out_specs=hbm,
        out_shape=jax.ShapeDtypeStruct((per_device, BLK, BLK), jnp.bfloat16),
        scratch_shapes=[pltpu.SemaphoreType.DMA((per_device,))],
        name="take_own",
    )(mine.reshape(1), counts, operators)
    cores = 2 if off_count % 2 == 0 else 1
    lines = [list(range(c, off_count, cores)) for c in range(cores)]
    near = lax.all_gather(own, "off", axis=0, tiled=True, axis_index_groups=lines)
    far = near if cores == 1 else lax.ppermute(near, "off", [(i, i ^ 1) for i in range(off_count)])

    pairs = fl * 2

    def extra(whole_numbers, copies):
        flat = whole_numbers.astype(jnp.bfloat16).reshape(1, 1, 1, -1)
        flat = jnp.pad(flat, ((0, 0), (0, 0), (0, pairs - 1), (0, mid_local - flat.shape[3])))
        return jnp.broadcast_to(flat, (1, copies, pairs, mid_local))

    lists = jnp.concatenate([counts[:, None], targets], axis=1)
    data = bins_data.reshape(bins_local, off_count, pairs, mid_local)
    data = jnp.concatenate([data, extra(lists, off_count)], axis=0)
    data = lax.all_to_all(data, "off", split_axis=1, concat_axis=0, tiled=True)
    data = data.reshape(off_count, bins_local + 1, pairs, mid_local)
    lists = data[:, bins_local, 0, : lists.size].astype(jnp.int32).reshape(bins_total, 1 + entries)
    data = data[:, :bins_local].reshape(bins_total, pairs, mid_local)
    data = jnp.concatenate([data, extra(layer_index, 1)[0]], axis=0)
    data = lax.all_gather(data, "mid", axis=0)
    layers = data[:, bins_total, 0, : layer_index.size].astype(jnp.int32)
    layers = layers.reshape(mid_count, *layer_index.shape).transpose(1, 2, 0, 3)
    layers = layers.reshape(*layer_index.shape[:2], outer)
    data = data[:, :bins_total].reshape(mid_count, bins_total, pairs, mid_local // BLK, BLK)
    data = data.transpose(1, 2, 0, 3, 4).reshape(bins_total, pairs * outer, BLK)

    live_total = bins_total * entries // 2
    room = -(-(live_total + (fl - 1) * off_count) // fl)
    room = min(-(-room // GROUP) * GROUP, per_device * off_count)
    offs, nth, bins, goal = slot_lists(lists[:, 0], lists[:, 1:], bins_local, fl, per_device, room)
    side = (offs % cores != off_at % cores).astype(jnp.int32) * (off_count // cores)
    slots = (side + offs // cores) * per_device + nth
    pick = (
        jnp.tile(goal.reshape(1, fl * room), (1, 2))
        == lax.broadcasted_iota(jnp.int32, (NH, 2 * fl * room), 0)
    ).astype(jnp.bfloat16)

    own_slots = lax.dynamic_index_in_dim(slots, mine, 0, False)
    own_bins = lax.dynamic_index_in_dim(bins, mine, 0, False)
    list_groups = room // GROUP
    terms = pl.pallas_call(
        contribution_kernel,
        in_specs=[smem, smem, vmem, hbm, hbm],
        out_specs=vmem,
        out_shape=jax.ShapeDtypeStruct((fl, list_groups, outer + 1, GROUP, BLK), jnp.int32),
        scratch_shapes=[
            pltpu.VMEM((fl * 2 * outer * GROUP, BLK), jnp.float32),
            pltpu.VMEM((2 * near.shape[0], BLK, BLK), jnp.bfloat16),
            pltpu.SemaphoreType.DMA,
            pltpu.SemaphoreType.DMA,
        ],
        compiler_params=pltpu.CompilerParams(vmem_limit_bytes=VMEM),
        name="contributions",
    )(own_slots, own_bins, data, near, far)
    terms, freq_at = lax.optimization_barrier((terms, off_at * fl + mine))
    omega = math.pi * (0.1 + 0.8 * (freq_at.astype(jnp.float32) + 0.5) / freq_total)
    row = lax.broadcasted_iota(jnp.int32, (NH, total_mid), 0)
    lane = lax.broadcasted_iota(jnp.int32, (NH, total_mid), 1)
    offset_wave = signed_wave(2 * (row % HALF) + row // HALF, NH)
    mid_wave = signed_wave(lane // BLK + outer * (lane % BLK), total_mid)
    phase_real, phase_imag = propagator(omega * omega, mid_wave, offset_wave)
    phase_real, phase_imag = (x * (1.0 / (NH * total_mid)) for x in (phase_real, phase_imag))

    layer_total = slowness.shape[1]
    chosen = layers[..., None] == jnp.arange(layer_total)
    slow = jnp.sum(jnp.where(chosen, slowness[:, None, None, :], 0.0), axis=-1)
    turn = 2.0 * dz_cells * omega * (slow - 1.0)
    layer_turns = jnp.stack([jnp.cos(turn), jnp.sin(turn)])

    terms = lax.all_to_all(
        terms, "mid", split_axis=0, concat_axis=0, axis_index_groups=groups, tiled=True
    )

    middle, offset_turn = twiddle_tables(outer)
    here = mid_local // BLK
    rows_out = (HALF + 1) * 2 * here
    tables = [jnp.asarray(t) for t in block_tables()]
    middle, offset_turn = jnp.asarray(middle), jnp.asarray(offset_turn)
    plane = pl.pallas_call(
        march_kernel,
        in_specs=[smem] + [vmem] * 10,
        out_specs=vmem,
        out_shape=jax.ShapeDtypeStruct((2, 2, HALF, total_mid), jnp.float32),
        scratch_shapes=[
            pltpu.VMEM((2, 2, HALF, total_mid), jnp.float32),
            pltpu.VMEM((fl * room, BLK), jnp.float32),
        ],
        compiler_params=pltpu.CompilerParams(vmem_limit_bytes=VMEM),
        name="march",
    )(layer_turns, terms, pick, phase_real, phase_imag, *tables, middle, offset_turn)

    finish = pl.pallas_call(
        finish_kernel,
        grid_spec=pltpu.PrefetchScalarGridSpec(
            num_scalar_prefetch=1,
            grid=(1,),
            in_specs=[
                smem,
                pl.BlockSpec((2, 2, HALF, mid_local), lambda i, dest: (0, 0, 0, dest[0])),
                vmem,
                vmem,
            ],
            out_specs=pl.BlockSpec((rows_out, BLK), lambda i, dest: (0, 0)),
        ),
        out_shape=jax.ShapeDtypeStruct((rows_out, BLK), jnp.int32),
        name="finish",
    )
    got = {}
    for ahead in [*range(fl - 1, 0, -1), 0]:
        dest = (mid_at // fl) * fl + (mine + ahead) % fl
        block = finish(dest.reshape(1), layer_turns, plane, tables[1], offset_turn)
        plane, block = lax.optimization_barrier((plane, block))
        if ahead:
            pairs_of = [(s, s // fl * fl + (s % fl + ahead) % fl) for s in range(mid_count)]
            block = lax.ppermute(block, "mid", pairs_of)
        got[ahead] = block

    field = None
    for ahead in [0, *range(fl - 1, 0, -1)]:
        freq = (mine - ahead) % fl
        first = field is None
        field = pl.pallas_call(
            result_kernel,
            grid_spec=pltpu.PrefetchScalarGridSpec(
                num_scalar_prefetch=1,
                grid=(1,),
                in_specs=[pl.BlockSpec((rows_out, BLK), lambda i, f: (0, 0))] + ([] if first else [hbm]),
                out_specs=pl.BlockSpec((1, NH, 2 * here, BLK), lambda i, f: (f[0], 0, 0, 0)),
            ),
            out_shape=jax.ShapeDtypeStruct((fl, NH, 2 * here, BLK), jnp.float32),
            input_output_aliases={} if first else {2: 0},
            name="result",
        )(freq.reshape(1), got[ahead], *([] if first else [field]))
    field = field.reshape(fl, NH, here, 2, BLK).transpose(0, 1, 3, 2, 4)
    return field.reshape(fl, NH, 2, mid_local)


def solution(mesh):
    in_specs = (
        P("off", None, None, "mid"),
        P("off", None, None, None),
        P("off", None),
        P("off"),
        P(None, None, "mid"),
        P(),
    )
    out_specs = P("off", None, None, "mid")
    return jax.shard_map(local, mesh=mesh, in_specs=in_specs, out_specs=out_specs, check_vma=False)
```

```python
import functools
import math

import jax
import jax.numpy as jnp
import numpy as np
from jax import lax
from jax.experimental import pallas as pl
from jax.experimental.pallas import tpu as pltpu
from jax.sharding import PartitionSpec as P

NH = 256
BLK = 128

dz_cells = 2.0
damping = 0.1

HALF = NH // 2
STEP_LOG = 64.0
TOP = 32767.0
GROUP = 8
VMEM = 56 * 1024 * 1024


def signed_wave(index, length):
    signed = (index + length // 2) % length - length // 2
    return signed.astype(jnp.float32) * (2.0 * math.pi / length)


def root_pair(level):
    magnitude = jnp.sqrt(level * level + damping * damping)
    larger = jnp.sqrt(0.5 * (magnitude + jnp.abs(level)))
    smaller = damping / (2.0 * larger)
    return (jnp.where(level >= 0, larger, smaller), jnp.where(level >= 0, smaller, larger))


def propagator(omega_sq, mid_wave, offset_wave):
    source = 0.5 * (mid_wave - offset_wave)
    receiver = 0.5 * (mid_wave + offset_wave)
    real_s, imag_s = root_pair(omega_sq - source * source)
    real_r, imag_r = root_pair(omega_sq - receiver * receiver)
    decay = jnp.exp(-dz_cells * (imag_s + imag_r))
    turn = dz_cells * (real_s + real_r)
    return (decay * jnp.cos(turn), decay * jnp.sin(turn))


def halves_np(table):
    high = table.astype(np.float32).astype(jnp.bfloat16)
    low = (table - high.astype(np.float64)).astype(np.float32).astype(jnp.bfloat16)
    return high, low


def block_tables():
    index = np.arange(BLK)
    angles = 2.0 * np.pi * (np.outer(index, index) % BLK) / BLK
    cos, sin = np.cos(angles), np.sin(angles)
    upper = np.block([[cos, sin], [-sin, cos]])
    lower = np.block([[cos, -sin], [sin, cos]])
    tables = []
    for axis, pair in ((1, (upper, lower)), (0, (lower, upper))):
        for table in pair:
            high, low = halves_np(table)
            tables.append(np.concatenate([high, high, low], axis=axis))
    return tables


def twiddle_tables(outer):
    ka, b = np.arange(outer)[:, None], np.arange(BLK)[None, :]
    angles = 2.0 * np.pi * ka * b / (outer * BLK)
    middle = np.stack([np.cos(angles), np.sin(angles)]).astype(np.float32)
    rows = 2.0 * np.pi * np.arange(HALF) / NH
    offset = np.stack([np.cos(rows), np.sin(rows)]).astype(np.float32)
    return middle, np.broadcast_to(offset[:, :, None], (2, HALF, BLK)).copy()


def halves(value):
    high = value.astype(jnp.bfloat16)
    return high, (value - high.astype(jnp.float32)).astype(jnp.bfloat16)


def dot(left, right):
    return jnp.dot(left, right, preferred_element_type=jnp.float32)


def left_product(table, value):
    high, low = halves(value)
    return dot(table, jnp.concatenate([high, low, high], axis=0))


def right_product(value, table):
    high, low = halves(value)
    return dot(jnp.concatenate([high, low, high], axis=1), table)


def cmul(real_a, imag_a, real_b, imag_b):
    return real_a * real_b - imag_a * imag_b, real_a * imag_b + imag_a * real_b


def small_transform(values, sign):
    count = len(values)
    if count == 1:
        return values
    even = small_transform(values[0::2], sign)
    odd = small_transform(values[1::2], sign)
    first, second = [], []
    for k in range(count // 2):
        er, ei = even[k]
        xr, xi = odd[k]
        if k == 0:
            tr, ti = xr, xi
        elif 4 * k == count:
            tr, ti = (-xi, xr) if sign > 0 else (xi, -xr)
        else:
            c, s = math.cos(2 * math.pi * k / count), sign * math.sin(2 * math.pi * k / count)
            if 8 * k == count:
                tr, ti = ((xr - xi) * c, (xr + xi) * c) if sign > 0 else ((xr + xi) * c, (xi - xr) * c)
            elif 8 * k == 3 * count:
                tr, ti = ((xr + xi) * c, (xi - xr) * c) if sign > 0 else ((xr - xi) * c, (xr + xi) * c)
            else:
                tr, ti = xr * c - xi * s, xr * s + xi * c
        first.append((er + tr, ei + ti))
        second.append((er - tr, ei - ti))
    return first + second


def scale_code(biggest):
    return (jnp.floor(jnp.log(jnp.maximum(biggest, 1e-30)) * STEP_LOG) + 1.0).astype(jnp.int32)


def scale_of(code):
    return jnp.exp(code.astype(jnp.float32) * (1.0 / STEP_LOG)) * (1.0 / TOP)


def inverse_scale_of(code):
    return jnp.exp(code.astype(jnp.float32) * (-1.0 / STEP_LOG)) * TOP


def coded(value, inverse):
    return jnp.floor(value * inverse + 0.5).astype(jnp.int32)


def packed(high, low):
    return (high << 16) | (low & 0xFFFF)


def unpacked(word):
    return (word >> 16).astype(jnp.float32), ((word << 16) >> 16).astype(jnp.float32)


def contribution_kernel(slot_ref, bin_ref, data_ref, *rest):
    *sources, out_ref, held, weight_ref, sems = rest
    count = sources[0].shape[0]
    copies = [
        pltpu.make_async_copy(ref, weight_ref.at[pl.ds(n * count, count)], sems.at[n])
        for n, ref in enumerate(sources)
    ]
    for copy in copies:
        copy.start()
    for copy in copies:
        copy.wait()
    freqs, groups = out_ref.shape[:2]
    outer = out_ref.shape[2] - 1

    @pl.loop(0, groups)
    def _(group):
        for at in range(GROUP):
            slot = slot_ref[group * GROUP + at]
            source = bin_ref[group * GROUP + at]
            held[pl.ds(at, data_ref.shape[1], GROUP), :] = dot(data_ref[source], weight_ref[slot])
        for f in range(freqs):
            base = f * 2 * outer * GROUP
            biggest = jnp.abs(held[pl.ds(base, GROUP), :])
            for at in range(1, 2 * outer):
                biggest = jnp.maximum(biggest, jnp.abs(held[pl.ds(base + at * GROUP, GROUP), :]))
            code = scale_code(biggest)
            inverse = inverse_scale_of(code)
            for a in range(outer):
                real = held[pl.ds(base + a * GROUP, GROUP), :]
                imag = held[pl.ds(base + (outer + a) * GROUP, GROUP), :]
                out_ref[f, group, a] = packed(coded(real, inverse), coded(imag, inverse))
            out_ref[f, group, outer] = code


def column_of(plane, a):
    lanes = pl.ds(pl.multiple_of(a * BLK, BLK), BLK)
    return jnp.concatenate(
        [
            jnp.concatenate([plane[p, 0, :, lanes], plane[p, 1, :, lanes]], axis=0)
            for p in range(2)
        ],
        axis=1,
    )


def store_column(plane, a, value):
    lanes = pl.ds(pl.multiple_of(a * BLK, BLK), BLK)
    for p in range(2):
        for c in range(2):
            plane[p, c, :, lanes] = value[c * HALF : (c + 1) * HALF, p * BLK : (p + 1) * BLK]


def offset_forward(low_half, high_half, upper, turn):
    first = [low_half[c] + high_half[c] for c in range(2)]
    second = cmul(low_half[0] - high_half[0], low_half[1] - high_half[1], turn[0], -turn[1])
    value = jnp.concatenate(
        [jnp.concatenate(first, axis=0), jnp.concatenate(second, axis=0)], axis=1
    )
    return left_product(upper[...], value)


def offset_inverse(value, lower, turn):
    value = left_product(lower[...], value)
    first = value[:HALF, :BLK], value[HALF:, :BLK]
    second = cmul(value[:HALF, BLK:], value[HALF:, BLK:], turn[0], turn[1])
    return (
        [first[c] + second[c] for c in range(2)],
        [first[c] - second[c] for c in range(2)],
    )


def layer_turn(halves_in, layer_ref, step, a):
    blocks = layer_ref.shape[2]
    tall = NH // blocks
    results = []
    for p in range(2):
        parts = [[], []]
        for at in range(HALF // tall):
            block = p * (HALF // tall) + at
            cos, sin = layer_ref[0, step, block, a], layer_ref[1, step, block, a]
            rows = slice(at * tall, (at + 1) * tall)
            real, imag = cmul(halves_in[p][0][rows], halves_in[p][1][rows], cos, sin)
            parts[0].append(real)
            parts[1].append(imag)
        results.append([jnp.concatenate(part, axis=0) for part in parts])
    return results


def midpoint_pass(plane, out, phase_refs, forward, inverse, middle_ref, rows):
    outer = middle_ref.shape[1]
    per_half = HALF // rows

    @pl.loop(0, 2 * per_half, unroll=4)
    def _(at):
        p = at // per_half
        here = pl.ds(pl.multiple_of((at % per_half) * rows, rows), rows)
        there = pl.ds(pl.multiple_of(at * rows, rows), rows)
        lanes = [slice(a * BLK, (a + 1) * BLK) for a in range(outer)]
        values = [(plane[p, 0, here, lane], plane[p, 1, here, lane]) for lane in lanes]
        values = small_transform(values, -1)
        turned = []
        for a in range(outer):
            real, imag = cmul(*values[a], middle_ref[0, a : a + 1], -middle_ref[1, a : a + 1])
            turned.append(jnp.concatenate([real, imag], axis=1))
        value = right_product(jnp.concatenate(turned, axis=0), forward[...])
        turned = []
        for a in range(outer):
            part = value[a * rows : (a + 1) * rows]
            real, imag = cmul(
                part[:, :BLK], part[:, BLK:], phase_refs[0][there, lanes[a]], phase_refs[1][there, lanes[a]]
            )
            turned.append(jnp.concatenate([real, imag], axis=1))
        value = right_product(jnp.concatenate(turned, axis=0), inverse[...])
        values = []
        for a in range(outer):
            part = value[a * rows : (a + 1) * rows]
            values.append(
                cmul(part[:, :BLK], part[:, BLK:], middle_ref[0, a : a + 1], middle_ref[1, a : a + 1])
            )
        values = small_transform(values, 1)
        for a in range(outer):
            out[p, 0, here, lanes[a]] = values[a][0]
            out[p, 1, here, lanes[a]] = values[a][1]


def march_kernel(
    layer_ref, code_ref, pick_ref, phase_real, phase_imag, rows_forward, rows_inverse, lanes_forward,
    lanes_inverse, middle_ref, offset_ref, other, plane, scales,
):
    sources, groups = code_ref.shape[:2]
    outer = middle_ref.shape[1]
    steps = layer_ref.shape[1]
    slots = sources * groups * GROUP
    turn = offset_ref[0], offset_ref[1]

    scales[...] = scale_of(code_ref[:, :, outer].reshape(slots, BLK))

    @pl.loop(0, outer, unroll=4)
    def _(a):
        real, imag = unpacked(code_ref[:, :, a].reshape(slots, BLK))
        scale = scales[...]
        value = jnp.concatenate([real * scale, imag * scale], axis=1)
        moved = dot(pick_ref[...], jnp.concatenate(halves(value), axis=0))
        low_half = [moved[:HALF, :BLK], moved[:HALF, BLK:]]
        high_half = [moved[HALF:, :BLK], moved[HALF:, BLK:]]
        store_column(plane, a, offset_forward(low_half, high_half, rows_forward, turn))

    for step in range(steps):
        midpoint_pass(
            plane, other, (phase_real, phase_imag), lanes_forward, lanes_inverse, middle_ref, 16
        )
        if step < steps - 1:

            @pl.loop(0, outer, unroll=4)
            def _(a):
                parts = offset_inverse(column_of(other, a), rows_inverse, turn)
                parts = layer_turn(parts, layer_ref, step, a)
                store_column(plane, a, offset_forward(parts[0], parts[1], rows_forward, turn))


def finish_kernel(dest_ref, layer_ref, plane_ref, rows_inverse, offset_ref, out_ref):
    here = plane_ref.shape[3] // BLK
    turn = offset_ref[0], offset_ref[1]
    for at in range(here):
        parts = offset_inverse(column_of(plane_ref, at), rows_inverse, turn)
        parts = layer_turn(parts, layer_ref, layer_ref.shape[1] - 1, dest_ref[0] * here + at)
        for c in range(2):
            both = jnp.maximum(jnp.abs(parts[0][c]), jnp.abs(parts[1][c]))
            code = scale_code(jnp.max(both, axis=0, keepdims=True))
            inverse = inverse_scale_of(code)
            words = packed(coded(parts[0][c], inverse), coded(parts[1][c], inverse))
            row = at * 2 + c
            out_ref[pl.ds(row, HALF, 2 * here), :] = words
            out_ref[pl.ds(HALF * 2 * here + row, 1), :] = code


def result_kernel(freq_ref, code_ref, *rest):
    out_ref = rest[-1]
    tall = out_ref.shape[2]
    per = code_ref.shape[0] // tall - 1
    scale = scale_of(code_ref[per * tall :])
    first, second = unpacked(code_ref[: per * tall].reshape(per, tall, BLK))
    out_ref[0, :per] = first * scale[None]
    out_ref[0, per:] = second * scale[None]


def take_kernel(mine_ref, counts_ref, source_ref, out_ref, sems):
    taken, entries = out_ref.shape[0], source_ref.shape[1]
    bins_here, stride = source_ref.shape[0], source_ref.shape[0] * entries // taken
    copies = []
    for n in range(taken):
        entry, bin_at = n * stride + mine_ref[0], 0
        for b in range(bins_here - 1):
            over = (bin_at == b) & (entry >= counts_ref[b])
            entry = jnp.where(over, entry - counts_ref[b], entry)
            bin_at = jnp.where(over, b + 1, bin_at)
        entry = jnp.minimum(entry, entries - 1)
        copies.append(
            pltpu.make_async_copy(source_ref.at[bin_at, entry], out_ref.at[n], sems.at[n])
        )
        copies[-1].start()
    for copy in copies:
        copy.wait()


def slot_lists(counts_all, targets_all, bins_local, fl, per_device, room):
    offs = counts_all.shape[0] // bins_local
    entries = targets_all.shape[1]
    counts_in = counts_all.reshape(offs, bins_local)
    live = jnp.sum(counts_in, axis=1)
    quarter = jnp.arange(fl, dtype=jnp.int32)
    held = (live[None, :] - quarter[:, None] + fl - 1) // fl
    upto = jnp.sum(
        jnp.where(jnp.arange(offs)[None, :] <= jnp.arange(offs)[:, None], held[:, None, :], 0), axis=2
    )
    at = jnp.arange(room, dtype=jnp.int32)
    past = (at[None, :, None] >= upto[:, None, :]).astype(jnp.int32)
    off_at = jnp.sum(past, axis=2)
    valid = off_at < offs
    off_at = jnp.minimum(off_at, offs - 1)
    start = jnp.sum(past * held[:, None, :], axis=2)
    nth = jnp.clip(at[None, :] - start, 0, per_device - 1)
    entry = nth * fl + quarter[:, None]
    bin_at = off_at * bins_local
    mine = off_at[:, :, None] == jnp.arange(offs)[None, None, :]
    for b in range(bins_local - 1):
        size = jnp.sum(jnp.where(mine, counts_in[None, None, :, b], 0), axis=2)
        over = (bin_at == off_at * bins_local + b) & (entry >= size)
        bin_at = bin_at + over
        entry = entry - jnp.where(over, size, 0)
    flat = bin_at * entries + entry
    total = targets_all.size
    picks = flat[:, :, None] == jnp.arange(total)[None, None, :]
    target = jnp.sum(jnp.where(picks, targets_all.reshape(1, 1, total), 0), axis=2)
    target = jnp.where(valid, target, -1)
    return off_at, nth, bin_at, target


def local(bins_data, operators, targets, counts, layer_index, slowness):
    off_count = lax.axis_size("off")
    mid_count = lax.axis_size("mid")
    bins_local, freq_total, _, mid_local = bins_data.shape
    entries = operators.shape[1]
    bins_total = bins_local * off_count
    fl = freq_total // off_count
    total_mid = mid_local * mid_count
    outer = total_mid // BLK
    mid_at, off_at = lax.axis_index("mid"), lax.axis_index("off")
    assert mid_count % fl == 0 and (bins_local * entries) % fl == 0
    mine = mid_at % fl
    rounds = mid_count // fl
    groups = (
        None if rounds == 1 else [list(range(g * fl, (g + 1) * fl)) for g in range(rounds)]
    )

    per_device = bins_local * entries // fl
    smem = pl.BlockSpec(memory_space=pltpu.SMEM)
    vmem = pl.BlockSpec(memory_space=pltpu.VMEM)
    hbm = pl.BlockSpec(memory_space=pl.ANY)
    own = pl.pallas_call(
        take_kernel,
        in_specs=[smem, smem, hbm],
        out_specs=vmem,
        out_shape=jax.ShapeDtypeStruct((per_device, BLK, BLK), jnp.bfloat16),
        scratch_shapes=[pltpu.SemaphoreType.DMA((per_device,))],
        name="take_own",
    )(mine.reshape(1), counts, operators)
    bins_data, own = lax.optimization_barrier((bins_data, own))
    cores = 2 if off_count % 2 == 0 else 1
    line = off_count // cores
    assert line & (line - 1) == 0 and fl & (fl - 1) == 0
    shares = [own] + [
        lax.ppermute(own, "off", [(i, (i // cores ^ away) * cores + i % cores) for i in range(off_count)])
        for away in range(1, line)
    ]
    if cores > 1:
        shares += [lax.ppermute(x, "off", [(i, i ^ 1) for i in range(off_count)]) for x in shares]

    pairs = fl * 2

    def extra(whole_numbers, copies):
        flat = whole_numbers.astype(jnp.bfloat16).reshape(1, 1, 1, -1)
        flat = jnp.pad(flat, ((0, 0), (0, 0), (0, pairs - 1), (0, mid_local - flat.shape[3])))
        return jnp.broadcast_to(flat, (1, copies, pairs, mid_local))

    lists = jnp.concatenate([counts[:, None], targets], axis=1)
    data = bins_data.reshape(bins_local, off_count, pairs, mid_local)
    data = jnp.concatenate([data, extra(lists, off_count)], axis=0)
    data = lax.all_to_all(data, "off", split_axis=1, concat_axis=0, tiled=True)
    data = data.reshape(off_count, bins_local + 1, pairs, mid_local)
    lists = data[:, bins_local, 0, : lists.size].astype(jnp.int32).reshape(bins_total, 1 + entries)
    data = data[:, :bins_local].reshape(bins_total, pairs, mid_local)
    data = jnp.concatenate([data, extra(layer_index, 1)[0]], axis=0)
    data = lax.all_gather(data, "mid", axis=0)
    layers = data[:, bins_total, 0, : layer_index.size].astype(jnp.int32)
    layers = layers.reshape(mid_count, *layer_index.shape).transpose(1, 2, 0, 3)
    layers = layers.reshape(*layer_index.shape[:2], outer)
    data = data[:, :bins_total].reshape(mid_count, bins_total, pairs, mid_local // BLK, BLK)
    data = data.transpose(1, 2, 0, 3, 4).reshape(bins_total, pairs * outer, BLK)

    live_total = bins_total * entries // 2
    room = -(-(live_total + (fl - 1) * off_count) // fl)
    room = min(-(-room // GROUP) * GROUP, per_device * off_count)
    offs, nth, bins, goal = slot_lists(lists[:, 0], lists[:, 1:], bins_local, fl, per_device, room)
    side = (offs % cores != off_at % cores).astype(jnp.int32) * line
    slots = (side + ((offs // cores) ^ (off_at // cores))) * per_device + nth
    pick = (
        jnp.tile(goal.reshape(1, fl * room), (1, 2))
        == lax.broadcasted_iota(jnp.int32, (NH, 2 * fl * room), 0)
    ).astype(jnp.bfloat16)

    own_slots = lax.dynamic_index_in_dim(slots, mine, 0, False)
    own_bins = lax.dynamic_index_in_dim(bins, mine, 0, False)
    list_groups = room // GROUP
    terms = pl.pallas_call(
        contribution_kernel,
        in_specs=[smem, smem, vmem] + [hbm] * len(shares),
        out_specs=vmem,
        out_shape=jax.ShapeDtypeStruct((fl, list_groups, outer + 1, GROUP, BLK), jnp.int32),
        scratch_shapes=[
            pltpu.VMEM((fl * 2 * outer * GROUP, BLK), jnp.float32),
            pltpu.VMEM((len(shares) * per_device, BLK, BLK), jnp.bfloat16),
            pltpu.SemaphoreType.DMA((len(shares),)),
        ],
        compiler_params=pltpu.CompilerParams(vmem_limit_bytes=VMEM),
        name="contributions",
    )(own_slots, own_bins, data, *shares)
    terms, freq_at = lax.optimization_barrier((terms, off_at * fl + mine))
    omega = math.pi * (0.1 + 0.8 * (freq_at.astype(jnp.float32) + 0.5) / freq_total)
    row = lax.broadcasted_iota(jnp.int32, (NH, total_mid), 0)
    lane = lax.broadcasted_iota(jnp.int32, (NH, total_mid), 1)
    offset_wave = signed_wave(2 * (row % HALF) + row // HALF, NH)
    mid_wave = signed_wave(lane // BLK + outer * (lane % BLK), total_mid)
    phase_real, phase_imag = propagator(omega * omega, mid_wave, offset_wave)
    phase_real, phase_imag = (x * (1.0 / (NH * total_mid)) for x in (phase_real, phase_imag))

    layer_total = slowness.shape[1]
    chosen = layers[..., None] == jnp.arange(layer_total)
    slow = jnp.sum(jnp.where(chosen, slowness[:, None, None, :], 0.0), axis=-1)
    turn = 2.0 * dz_cells * omega * (slow - 1.0)
    layer_turns = jnp.stack([jnp.cos(turn), jnp.sin(turn)])

    terms = lax.all_to_all(
        terms, "mid", split_axis=0, concat_axis=0, axis_index_groups=groups, tiled=True
    )

    middle, offset_turn = twiddle_tables(outer)
    here = mid_local // BLK
    rows_out = (HALF + 1) * 2 * here
    tables = [jnp.asarray(t) for t in block_tables()]
    middle, offset_turn = jnp.asarray(middle), jnp.asarray(offset_turn)
    plane = pl.pallas_call(
        march_kernel,
        in_specs=[smem] + [vmem] * 10,
        out_specs=vmem,
        out_shape=jax.ShapeDtypeStruct((2, 2, HALF, total_mid), jnp.float32),
        scratch_shapes=[
            pltpu.VMEM((2, 2, HALF, total_mid), jnp.float32),
            pltpu.VMEM((fl * room, BLK), jnp.float32),
        ],
        compiler_params=pltpu.CompilerParams(vmem_limit_bytes=VMEM),
        name="march",
    )(layer_turns, terms, pick, phase_real, phase_imag, *tables, middle, offset_turn)

    finish = pl.pallas_call(
        finish_kernel,
        grid_spec=pltpu.PrefetchScalarGridSpec(
            num_scalar_prefetch=1,
            grid=(1,),
            in_specs=[
                smem,
                pl.BlockSpec((2, 2, HALF, mid_local), lambda i, dest: (0, 0, 0, dest[0])),
                vmem,
                vmem,
            ],
            out_specs=pl.BlockSpec((rows_out, BLK), lambda i, dest: (0, 0)),
        ),
        out_shape=jax.ShapeDtypeStruct((rows_out, BLK), jnp.int32),
        cost_estimate=pl.CostEstimate(
            flops=6 * NH * NH * 2 * BLK * here, bytes_accessed=6 * NH * mid_local, transcendentals=0
        ),
        name="finish",
    )
    got = {}
    for ahead in [*range(fl - 1, 0, -1), 0]:
        dest = (mid_at // fl) * fl + (mine ^ ahead)
        block = finish(dest.reshape(1), layer_turns, plane, tables[1], offset_turn)
        plane, block = lax.optimization_barrier((plane, block))
        if ahead:
            block = lax.ppermute(block, "mid", [(s, s ^ ahead) for s in range(mid_count)])
        got[ahead] = block

    field = None
    for ahead in [0, *range(fl - 1, 0, -1)]:
        freq = mine ^ ahead
        first = field is None
        field = pl.pallas_call(
            result_kernel,
            grid_spec=pltpu.PrefetchScalarGridSpec(
                num_scalar_prefetch=1,
                grid=(1,),
                in_specs=[pl.BlockSpec((rows_out, BLK), lambda i, f: (0, 0))] + ([] if first else [hbm]),
                out_specs=pl.BlockSpec((1, NH, 2 * here, BLK), lambda i, f: (f[0], 0, 0, 0)),
            ),
            out_shape=jax.ShapeDtypeStruct((fl, NH, 2 * here, BLK), jnp.float32),
            input_output_aliases={} if first else {2: 0},
            compiler_params=pltpu.CompilerParams(vmem_limit_bytes=VMEM),
            cost_estimate=pl.CostEstimate(
                flops=4 * NH * mid_local, bytes_accessed=12 * NH * mid_local, transcendentals=0
            ),
            name="result",
        )(freq.reshape(1), got[ahead], *([] if first else [field]))
    field = field.reshape(fl, NH, here, 2, BLK).transpose(0, 1, 3, 2, 4)
    return field.reshape(fl, NH, 2, mid_local)


def solution(mesh):
    in_specs = (
        P("off", None, None, "mid"),
        P("off", None, None, None),
        P("off", None),
        P("off"),
        P(None, None, "mid"),
        P(),
    )
    out_specs = P("off", None, None, "mid")
    return jax.shard_map(local, mesh=mesh, in_specs=in_specs, out_specs=out_specs, check_vma=False)
```

```python
import functools
import math

import jax
import jax.numpy as jnp
import numpy as np
from jax import lax
from jax.experimental import pallas as pl
from jax.experimental.pallas import tpu as pltpu
from jax.sharding import PartitionSpec as P

NH = 256
BLK = 128

dz_cells = 2.0
damping = 0.1

HALF = NH // 2
STEP_LOG = 64.0
TOP = 32767.0
GROUP = 8
COLUMNS = 2
VMEM = 56 * 1024 * 1024


def signed_wave(index, length):
    signed = (index + length // 2) % length - length // 2
    return signed.astype(jnp.float32) * (2.0 * math.pi / length)


def root_pair(level):
    magnitude = jnp.sqrt(level * level + damping * damping)
    larger = jnp.sqrt(0.5 * (magnitude + jnp.abs(level)))
    smaller = damping / (2.0 * larger)
    return (jnp.where(level >= 0, larger, smaller), jnp.where(level >= 0, smaller, larger))


def propagator(omega_sq, mid_wave, offset_wave):
    source = 0.5 * (mid_wave - offset_wave)
    receiver = 0.5 * (mid_wave + offset_wave)
    real_s, imag_s = root_pair(omega_sq - source * source)
    real_r, imag_r = root_pair(omega_sq - receiver * receiver)
    decay = jnp.exp(-dz_cells * (imag_s + imag_r))
    turn = dz_cells * (real_s + real_r)
    return (decay * jnp.cos(turn), decay * jnp.sin(turn))


def halves_np(table):
    high = table.astype(np.float32).astype(jnp.bfloat16)
    low = (table - high.astype(np.float64)).astype(np.float32).astype(jnp.bfloat16)
    return high, low


def block_tables():
    index = np.arange(BLK)
    angles = 2.0 * np.pi * (np.outer(index, index) % BLK) / BLK
    cos, sin = np.cos(angles), np.sin(angles)
    upper = np.block([[cos, sin], [-sin, cos]])
    lower = np.block([[cos, -sin], [sin, cos]])
    tables = []
    for axis, pair in ((1, (upper, lower)), (0, (lower, upper))):
        for table in pair:
            high, low = halves_np(table)
            tables.append(np.concatenate([high, high, low], axis=axis))
    return tables


def twiddle_tables(outer):
    ka, b = np.arange(outer)[:, None], np.arange(BLK)[None, :]
    angles = 2.0 * np.pi * ka * b / (outer * BLK)
    middle = np.stack([np.cos(angles), np.sin(angles)]).astype(np.float32)
    rows = 2.0 * np.pi * np.arange(HALF) / NH
    offset = np.stack([np.cos(rows), np.sin(rows)]).astype(np.float32)
    return middle, np.broadcast_to(offset[:, :, None], (2, HALF, BLK)).copy()


def halves(value):
    high = value.astype(jnp.bfloat16)
    return high, (value - high.astype(jnp.float32)).astype(jnp.bfloat16)


def dot(left, right):
    return jnp.dot(left, right, preferred_element_type=jnp.float32)


def left_product(table, value):
    high, low = halves(value)
    return dot(table, jnp.concatenate([high, low, high], axis=0))


def right_product(value, table):
    high, low = halves(value)
    return dot(jnp.concatenate([high, low, high], axis=1), table)


def cmul(real_a, imag_a, real_b, imag_b):
    return real_a * real_b - imag_a * imag_b, real_a * imag_b + imag_a * real_b


def small_transform(values, sign):
    count = len(values)
    if count == 1:
        return values
    even = small_transform(values[0::2], sign)
    odd = small_transform(values[1::2], sign)
    first, second = [], []
    for k in range(count // 2):
        er, ei = even[k]
        xr, xi = odd[k]
        if k == 0:
            tr, ti = xr, xi
        elif 4 * k == count:
            tr, ti = (-xi, xr) if sign > 0 else (xi, -xr)
        else:
            c, s = math.cos(2 * math.pi * k / count), sign * math.sin(2 * math.pi * k / count)
            if 8 * k == count:
                tr, ti = ((xr - xi) * c, (xr + xi) * c) if sign > 0 else ((xr + xi) * c, (xi - xr) * c)
            elif 8 * k == 3 * count:
                tr, ti = ((xr + xi) * c, (xi - xr) * c) if sign > 0 else ((xr - xi) * c, (xr + xi) * c)
            else:
                tr, ti = xr * c - xi * s, xr * s + xi * c
        first.append((er + tr, ei + ti))
        second.append((er - tr, ei - ti))
    return first + second


def scale_code(biggest):
    return (jnp.floor(jnp.log(jnp.maximum(biggest, 1e-30)) * STEP_LOG) + 1.0).astype(jnp.int32)


def scale_of(code):
    return jnp.exp(code.astype(jnp.float32) * (1.0 / STEP_LOG)) * (1.0 / TOP)


def inverse_scale_of(code):
    return jnp.exp(code.astype(jnp.float32) * (-1.0 / STEP_LOG)) * TOP


def coded(value, inverse):
    return jnp.floor(value * inverse + 0.5).astype(jnp.int32)


def packed(high, low):
    return (high << 16) | (low & 0xFFFF)


def unpacked(word):
    return (word >> 16).astype(jnp.float32), ((word << 16) >> 16).astype(jnp.float32)


def contribution_kernel(slot_ref, bin_ref, data_ref, *rest):
    *sources, out_ref, held, weight_ref, sems = rest
    count = sources[0].shape[0]
    copies = [
        pltpu.make_async_copy(ref, weight_ref.at[pl.ds(n * count, count)], sems.at[n])
        for n, ref in enumerate(sources)
    ]
    for copy in copies:
        copy.start()
    for copy in copies:
        copy.wait()
    freqs, groups = out_ref.shape[:2]
    outer = out_ref.shape[2] - 1

    @pl.loop(0, groups)
    def _(group):
        for at in range(GROUP):
            slot = slot_ref[group * GROUP + at]
            source = bin_ref[group * GROUP + at]
            held[pl.ds(at, data_ref.shape[1], GROUP), :] = dot(data_ref[source], weight_ref[slot])
        for f in range(freqs):
            base = f * 2 * outer * GROUP
            biggest = jnp.abs(held[pl.ds(base, GROUP), :])
            for at in range(1, 2 * outer):
                biggest = jnp.maximum(biggest, jnp.abs(held[pl.ds(base + at * GROUP, GROUP), :]))
            code = scale_code(biggest)
            inverse = inverse_scale_of(code)
            for a in range(outer):
                real = held[pl.ds(base + a * GROUP, GROUP), :]
                imag = held[pl.ds(base + (outer + a) * GROUP, GROUP), :]
                out_ref[f, group, a] = packed(coded(real, inverse), coded(imag, inverse))
            out_ref[f, group, outer] = code


def column_of(plane, a):
    lanes = pl.ds(pl.multiple_of(a * BLK, BLK), BLK)
    return jnp.concatenate(
        [
            jnp.concatenate([plane[p, 0, :, lanes], plane[p, 1, :, lanes]], axis=0)
            for p in range(2)
        ],
        axis=1,
    )


def store_column(plane, a, value):
    lanes = pl.ds(pl.multiple_of(a * BLK, BLK), BLK)
    for p in range(2):
        for c in range(2):
            plane[p, c, :, lanes] = value[c * HALF : (c + 1) * HALF, p * BLK : (p + 1) * BLK]


def offset_forward(pairs, upper, turn):
    parts = []
    for low_half, high_half in pairs:
        first = [low_half[c] + high_half[c] for c in range(2)]
        second = cmul(low_half[0] - high_half[0], low_half[1] - high_half[1], turn[0], -turn[1])
        parts += [jnp.concatenate(first, axis=0), jnp.concatenate(second, axis=0)]
    value = left_product(upper[...], jnp.concatenate(parts, axis=1))
    return [value[:, n * 2 * BLK : (n + 1) * 2 * BLK] for n in range(len(pairs))]


def offset_inverse(columns, lower, turn):
    value = left_product(lower[...], jnp.concatenate(columns, axis=1))
    pairs = []
    for n in range(len(columns)):
        part = value[:, n * 2 * BLK : (n + 1) * 2 * BLK]
        first = part[:HALF, :BLK], part[HALF:, :BLK]
        second = cmul(part[:HALF, BLK:], part[HALF:, BLK:], turn[0], turn[1])
        pairs.append(
            (
                [first[c] + second[c] for c in range(2)],
                [first[c] - second[c] for c in range(2)],
            )
        )
    return pairs


def layer_turn(halves_in, layer_ref, step, a):
    blocks = layer_ref.shape[2]
    tall = NH // blocks
    results = []
    for p in range(2):
        parts = [[], []]
        for at in range(HALF // tall):
            block = p * (HALF // tall) + at
            cos, sin = layer_ref[0, step, block, a], layer_ref[1, step, block, a]
            rows = slice(at * tall, (at + 1) * tall)
            real, imag = cmul(halves_in[p][0][rows], halves_in[p][1][rows], cos, sin)
            parts[0].append(real)
            parts[1].append(imag)
        results.append([jnp.concatenate(part, axis=0) for part in parts])
    return results


def midpoint_pass(plane, out, phase_refs, forward, inverse, middle_ref, rows):
    outer = middle_ref.shape[1]
    per_half = HALF // rows

    @pl.loop(0, 2 * per_half, unroll=4)
    def _(at):
        p = at // per_half
        here = pl.ds(pl.multiple_of((at % per_half) * rows, rows), rows)
        there = pl.ds(pl.multiple_of(at * rows, rows), rows)
        lanes = [slice(a * BLK, (a + 1) * BLK) for a in range(outer)]
        values = [(plane[p, 0, here, lane], plane[p, 1, here, lane]) for lane in lanes]
        values = small_transform(values, -1)
        turned = []
        for a in range(outer):
            real, imag = cmul(*values[a], middle_ref[0, a : a + 1], -middle_ref[1, a : a + 1])
            turned.append(jnp.concatenate([real, imag], axis=1))
        value = right_product(jnp.concatenate(turned, axis=0), forward[...])
        turned = []
        for a in range(outer):
            part = value[a * rows : (a + 1) * rows]
            real, imag = cmul(
                part[:, :BLK], part[:, BLK:], phase_refs[0][there, lanes[a]], phase_refs[1][there, lanes[a]]
            )
            turned.append(jnp.concatenate([real, imag], axis=1))
        value = right_product(jnp.concatenate(turned, axis=0), inverse[...])
        values = []
        for a in range(outer):
            part = value[a * rows : (a + 1) * rows]
            values.append(
                cmul(part[:, :BLK], part[:, BLK:], middle_ref[0, a : a + 1], middle_ref[1, a : a + 1])
            )
        values = small_transform(values, 1)
        for a in range(outer):
            out[p, 0, here, lanes[a]] = values[a][0]
            out[p, 1, here, lanes[a]] = values[a][1]


def march_kernel(
    layer_ref, code_ref, pick_ref, phase_real, phase_imag, rows_forward, rows_inverse, lanes_forward,
    lanes_inverse, middle_ref, offset_ref, other, plane, scales,
):
    sources, groups = code_ref.shape[:2]
    outer = middle_ref.shape[1]
    steps = layer_ref.shape[1]
    slots = sources * groups * GROUP
    turn = offset_ref[0], offset_ref[1]

    scales[...] = scale_of(code_ref[:, :, outer].reshape(slots, BLK))

    @pl.loop(0, outer // COLUMNS, unroll=2)
    def _(at):
        pairs = []
        for a in range(COLUMNS):
            real, imag = unpacked(code_ref[:, :, at * COLUMNS + a].reshape(slots, BLK))
            scale = scales[...]
            value = jnp.concatenate([real * scale, imag * scale], axis=1)
            moved = dot(pick_ref[...], jnp.concatenate(halves(value), axis=0))
            pairs.append(
                (
                    [moved[:HALF, :BLK], moved[:HALF, BLK:]],
                    [moved[HALF:, :BLK], moved[HALF:, BLK:]],
                )
            )
        for a, value in enumerate(offset_forward(pairs, rows_forward, turn)):
            store_column(plane, at * COLUMNS + a, value)

    for step in range(steps):
        midpoint_pass(
            plane, other, (phase_real, phase_imag), lanes_forward, lanes_inverse, middle_ref, 16
        )
        if step < steps - 1:

            @pl.loop(0, outer // COLUMNS, unroll=2)
            def _(at):
                places = [at * COLUMNS + a for a in range(COLUMNS)]
                pairs = offset_inverse([column_of(other, a) for a in places], rows_inverse, turn)
                pairs = [layer_turn(p, layer_ref, step, a) for p, a in zip(pairs, places)]
                for a, value in zip(places, offset_forward(pairs, rows_forward, turn)):
                    store_column(plane, a, value)


def finish_kernel(dest_ref, layer_ref, plane_ref, rows_inverse, offset_ref, out_ref):
    here = plane_ref.shape[3] // BLK
    turn = offset_ref[0], offset_ref[1]
    pairs = offset_inverse([column_of(plane_ref, at) for at in range(here)], rows_inverse, turn)
    for at in range(here):
        parts = layer_turn(pairs[at], layer_ref, layer_ref.shape[1] - 1, dest_ref[0] * here + at)
        for c in range(2):
            both = jnp.maximum(jnp.abs(parts[0][c]), jnp.abs(parts[1][c]))
            code = scale_code(jnp.max(both, axis=0, keepdims=True))
            inverse = inverse_scale_of(code)
            words = packed(coded(parts[0][c], inverse), coded(parts[1][c], inverse))
            row = at * 2 + c
            out_ref[pl.ds(row, HALF, 2 * here), :] = words
            out_ref[pl.ds(HALF * 2 * here + row, 1), :] = code


def result_kernel(freq_ref, code_ref, *rest):
    out_ref, words, sem = rest[-3:]
    chunk, tall = out_ref.shape[1:3]
    per = words.shape[0] // tall - 1
    at = pl.program_id(0)
    chunks = per // chunk

    @pl.when(at == 0)
    def _():
        copy = pltpu.make_async_copy(code_ref, words, sem)
        copy.start()
        copy.wait()

    scale = scale_of(words[per * tall :])[None]
    rows = pl.ds(pl.multiple_of((at % chunks) * chunk * tall, chunk * tall), chunk * tall)
    here = words[rows].reshape(chunk, tall, BLK)

    @pl.when(at < chunks)
    def _():
        out_ref[0] = unpacked(here)[0] * scale

    @pl.when(at >= chunks)
    def _():
        out_ref[0] = unpacked(here)[1] * scale


def take_kernel(mine_ref, counts_ref, source_ref, out_ref, sems):
    taken, entries = out_ref.shape[0], source_ref.shape[1]
    bins_here, stride = source_ref.shape[0], source_ref.shape[0] * entries // taken
    copies = []
    for n in range(taken):
        entry, bin_at = n * stride + mine_ref[0], 0
        for b in range(bins_here - 1):
            over = (bin_at == b) & (entry >= counts_ref[b])
            entry = jnp.where(over, entry - counts_ref[b], entry)
            bin_at = jnp.where(over, b + 1, bin_at)
        entry = jnp.minimum(entry, entries - 1)
        copies.append(
            pltpu.make_async_copy(source_ref.at[bin_at, entry], out_ref.at[n], sems.at[n])
        )
        copies[-1].start()
    for copy in copies:
        copy.wait()


def slot_lists(counts_all, targets_all, bins_local, fl, per_device, room):
    offs = counts_all.shape[0] // bins_local
    entries = targets_all.shape[1]
    counts_in = counts_all.reshape(offs, bins_local)
    live = jnp.sum(counts_in, axis=1)
    quarter = jnp.arange(fl, dtype=jnp.int32)
    held = (live[None, :] - quarter[:, None] + fl - 1) // fl
    upto = jnp.sum(
        jnp.where(jnp.arange(offs)[None, :] <= jnp.arange(offs)[:, None], held[:, None, :], 0), axis=2
    )
    at = jnp.arange(room, dtype=jnp.int32)
    past = (at[None, :, None] >= upto[:, None, :]).astype(jnp.int32)
    off_at = jnp.sum(past, axis=2)
    valid = off_at < offs
    off_at = jnp.minimum(off_at, offs - 1)
    start = jnp.sum(past * held[:, None, :], axis=2)
    nth = jnp.clip(at[None, :] - start, 0, per_device - 1)
    entry = nth * fl + quarter[:, None]
    bin_at = off_at * bins_local
    mine = off_at[:, :, None] == jnp.arange(offs)[None, None, :]
    for b in range(bins_local - 1):
        size = jnp.sum(jnp.where(mine, counts_in[None, None, :, b], 0), axis=2)
        over = (bin_at == off_at * bins_local + b) & (entry >= size)
        bin_at = bin_at + over
        entry = entry - jnp.where(over, size, 0)
    flat = bin_at * entries + entry
    total = targets_all.size
    picks = flat[:, :, None] == jnp.arange(total)[None, None, :]
    target = jnp.sum(jnp.where(picks, targets_all.reshape(1, 1, total), 0), axis=2)
    target = jnp.where(valid, target, -1)
    return off_at, nth, bin_at, target


def local(bins_data, operators, targets, counts, layer_index, slowness):
    off_count = lax.axis_size("off")
    mid_count = lax.axis_size("mid")
    bins_local, freq_total, _, mid_local = bins_data.shape
    entries = operators.shape[1]
    bins_total = bins_local * off_count
    fl = freq_total // off_count
    total_mid = mid_local * mid_count
    outer = total_mid // BLK
    mid_at, off_at = lax.axis_index("mid"), lax.axis_index("off")
    assert mid_count % fl == 0 and (bins_local * entries) % fl == 0
    mine = mid_at % fl
    rounds = mid_count // fl
    groups = (
        None if rounds == 1 else [list(range(g * fl, (g + 1) * fl)) for g in range(rounds)]
    )

    per_device = bins_local * entries // fl
    smem = pl.BlockSpec(memory_space=pltpu.SMEM)
    vmem = pl.BlockSpec(memory_space=pltpu.VMEM)
    hbm = pl.BlockSpec(memory_space=pl.ANY)
    pairs = fl * 2

    def extra(whole_numbers, copies):
        flat = whole_numbers.astype(jnp.bfloat16).reshape(1, 1, 1, -1)
        flat = jnp.pad(flat, ((0, 0), (0, 0), (0, pairs - 1), (0, mid_local - flat.shape[3])))
        return jnp.broadcast_to(flat, (1, copies, pairs, mid_local))

    lists = jnp.concatenate([counts[:, None], targets], axis=1)
    data = bins_data.reshape(bins_local, off_count, pairs, mid_local)
    data = jnp.concatenate([data, extra(lists, off_count)], axis=0)
    data = lax.all_to_all(data, "off", split_axis=1, concat_axis=0, tiled=True)

    own = pl.pallas_call(
        take_kernel,
        in_specs=[smem, smem, hbm],
        out_specs=vmem,
        out_shape=jax.ShapeDtypeStruct((per_device, BLK, BLK), jnp.bfloat16),
        scratch_shapes=[pltpu.SemaphoreType.DMA((per_device,))],
        name="take_own",
    )(mine.reshape(1), counts, operators)
    data, own = lax.optimization_barrier((data, own))
    cores = 2 if off_count % 2 == 0 else 1
    line = off_count // cores
    assert line & (line - 1) == 0 and fl & (fl - 1) == 0
    shares = [own] + [
        lax.ppermute(own, "off", [(i, (i // cores ^ away) * cores + i % cores) for i in range(off_count)])
        for away in range(1, line)
    ]
    if cores > 1:
        shares += [lax.ppermute(x, "off", [(i, i ^ 1) for i in range(off_count)]) for x in shares]

    data = data.reshape(off_count, bins_local + 1, pairs, mid_local)
    lists = data[:, bins_local, 0, : lists.size].astype(jnp.int32).reshape(bins_total, 1 + entries)
    data = data[:, :bins_local].reshape(bins_total, pairs, mid_local)
    data = jnp.concatenate([data, extra(layer_index, 1)[0]], axis=0)
    data = lax.all_gather(data, "mid", axis=0)
    layers = data[:, bins_total, 0, : layer_index.size].astype(jnp.int32)
    layers = layers.reshape(mid_count, *layer_index.shape).transpose(1, 2, 0, 3)
    layers = layers.reshape(*layer_index.shape[:2], outer)
    data = data[:, :bins_total].reshape(mid_count, bins_total, pairs, mid_local // BLK, BLK)
    data = data.transpose(1, 2, 0, 3, 4).reshape(bins_total, pairs * outer, BLK)

    live_total = bins_total * entries // 2
    room = -(-(live_total + (fl - 1) * off_count) // fl)
    room = min(-(-room // GROUP) * GROUP, per_device * off_count)
    offs, nth, bins, goal = slot_lists(lists[:, 0], lists[:, 1:], bins_local, fl, per_device, room)
    side = (offs % cores != off_at % cores).astype(jnp.int32) * line
    slots = (side + ((offs // cores) ^ (off_at // cores))) * per_device + nth
    own_slots = lax.dynamic_index_in_dim(slots, mine, 0, False)
    own_bins = lax.dynamic_index_in_dim(bins, mine, 0, False)
    list_groups = room // GROUP
    terms = pl.pallas_call(
        contribution_kernel,
        in_specs=[smem, smem, vmem] + [hbm] * len(shares),
        out_specs=vmem,
        out_shape=jax.ShapeDtypeStruct((fl, list_groups, outer + 1, GROUP, BLK), jnp.int32),
        scratch_shapes=[
            pltpu.VMEM((fl * 2 * outer * GROUP, BLK), jnp.float32),
            pltpu.VMEM((len(shares) * per_device, BLK, BLK), jnp.bfloat16),
            pltpu.SemaphoreType.DMA((len(shares),)),
        ],
        compiler_params=pltpu.CompilerParams(vmem_limit_bytes=VMEM),
        name="contributions",
    )(own_slots, own_bins, data, *shares)
    terms, goal, layers, freq_at = lax.optimization_barrier((terms, goal, layers, off_at * fl + mine))
    pick = (
        jnp.tile(goal.reshape(1, fl * room), (1, 2))
        == lax.broadcasted_iota(jnp.int32, (NH, 2 * fl * room), 0)
    ).astype(jnp.bfloat16)

    omega = math.pi * (0.1 + 0.8 * (freq_at.astype(jnp.float32) + 0.5) / freq_total)
    row = lax.broadcasted_iota(jnp.int32, (NH, total_mid), 0)
    lane = lax.broadcasted_iota(jnp.int32, (NH, total_mid), 1)
    offset_wave = signed_wave(2 * (row % HALF) + row // HALF, NH)
    mid_wave = signed_wave(lane // BLK + outer * (lane % BLK), total_mid)
    phase_real, phase_imag = propagator(omega * omega, mid_wave, offset_wave)
    phase_real, phase_imag = (x * (1.0 / (NH * total_mid)) for x in (phase_real, phase_imag))

    layer_total = slowness.shape[1]
    chosen = layers[..., None] == jnp.arange(layer_total)
    slow = jnp.sum(jnp.where(chosen, slowness[:, None, None, :], 0.0), axis=-1)
    turn = 2.0 * dz_cells * omega * (slow - 1.0)
    layer_turns = jnp.stack([jnp.cos(turn), jnp.sin(turn)])

    terms = lax.all_to_all(
        terms, "mid", split_axis=0, concat_axis=0, axis_index_groups=groups, tiled=True
    )

    middle, offset_turn = twiddle_tables(outer)
    here = mid_local // BLK
    rows_out = (HALF + 1) * 2 * here
    tables = [jnp.asarray(t) for t in block_tables()]
    middle, offset_turn = jnp.asarray(middle), jnp.asarray(offset_turn)
    plane = pl.pallas_call(
        march_kernel,
        in_specs=[smem] + [vmem] * 10,
        out_specs=vmem,
        out_shape=jax.ShapeDtypeStruct((2, 2, HALF, total_mid), jnp.float32),
        scratch_shapes=[
            pltpu.VMEM((2, 2, HALF, total_mid), jnp.float32),
            pltpu.VMEM((fl * room, BLK), jnp.float32),
        ],
        compiler_params=pltpu.CompilerParams(vmem_limit_bytes=VMEM),
        name="march",
    )(layer_turns, terms, pick, phase_real, phase_imag, *tables, middle, offset_turn)

    finish = pl.pallas_call(
        finish_kernel,
        grid_spec=pltpu.PrefetchScalarGridSpec(
            num_scalar_prefetch=1,
            grid=(1,),
            in_specs=[
                smem,
                pl.BlockSpec((2, 2, HALF, mid_local), lambda i, dest: (0, 0, 0, dest[0])),
                vmem,
                vmem,
            ],
            out_specs=pl.BlockSpec((rows_out, BLK), lambda i, dest: (0, 0)),
        ),
        out_shape=jax.ShapeDtypeStruct((rows_out, BLK), jnp.int32),
        cost_estimate=pl.CostEstimate(
            flops=6 * NH * NH * 2 * BLK * here, bytes_accessed=6 * NH * mid_local, transcendentals=0
        ),
        name="finish",
    )
    got = {}
    for ahead in [*range(fl - 1, 0, -1), 0]:
        dest = (mid_at // fl) * fl + (mine ^ ahead)
        block = finish(dest.reshape(1), layer_turns, plane, tables[1], offset_turn)
        if ahead:
            block = lax.ppermute(block, "mid", [(s, s ^ ahead) for s in range(mid_count)])
        got[ahead] = block

    field = None
    for ahead in [0, *range(fl - 1, 0, -1)]:
        freq = mine ^ ahead
        first = field is None
        field = pl.pallas_call(
            result_kernel,
            grid_spec=pltpu.PrefetchScalarGridSpec(
                num_scalar_prefetch=1,
                grid=(NH // (HALF // 2),),
                in_specs=[hbm] if first else [hbm, hbm],
                out_specs=pl.BlockSpec((1, HALF // 2, 2 * here, BLK), lambda i, f: (f[0], i, 0, 0)),
                scratch_shapes=[pltpu.VMEM((rows_out, BLK), jnp.int32), pltpu.SemaphoreType.DMA],
            ),
            out_shape=jax.ShapeDtypeStruct((fl, NH, 2 * here, BLK), jnp.float32),
            input_output_aliases={} if first else {2: 0},
            compiler_params=pltpu.CompilerParams(vmem_limit_bytes=VMEM),
            cost_estimate=pl.CostEstimate(
                flops=4 * NH * mid_local, bytes_accessed=12 * NH * mid_local, transcendentals=0
            ),
            name="result",
        )(freq.reshape(1), got[ahead], *([] if first else [field]))
    field = field.reshape(fl, NH, here, 2, BLK).transpose(0, 1, 3, 2, 4)
    return field.reshape(fl, NH, 2, mid_local)


def solution(mesh):
    in_specs = (
        P("off", None, None, "mid"),
        P("off", None, None, None),
        P("off", None),
        P("off"),
        P(None, None, "mid"),
        P(),
    )
    out_specs = P("off", None, None, "mid")
    return jax.shard_map(local, mesh=mesh, in_specs=in_specs, out_specs=out_specs, check_vma=False)
```

```python
import functools
import math

import jax
import jax.numpy as jnp
import numpy as np
from jax import lax
from jax.experimental import pallas as pl
from jax.experimental.pallas import tpu as pltpu
from jax.sharding import PartitionSpec as P

NH = 256
BLK = 128

dz_cells = 2.0
damping = 0.1

HALF = NH // 2
STEP_LOG = 64.0
TOP = 32767.0
GROUP = 8
COLUMNS = 2
ROWS = 8
CHUNKS = 4
UNROLL = 2
VMEM = 28 * 1024 * 1024
SMALL = 10 * 1024 * 1024


def signed_wave(index, length):
    signed = (index + length // 2) % length - length // 2
    return signed.astype(jnp.float32) * (2.0 * math.pi / length)


def root_pair(level):
    magnitude = jnp.sqrt(level * level + damping * damping)
    larger = jnp.sqrt(0.5 * (magnitude + jnp.abs(level)))
    smaller = damping / (2.0 * larger)
    return (jnp.where(level >= 0, larger, smaller), jnp.where(level >= 0, smaller, larger))


def propagator(omega_sq, mid_wave, offset_wave):
    source = 0.5 * (mid_wave - offset_wave)
    receiver = 0.5 * (mid_wave + offset_wave)
    real_s, imag_s = root_pair(omega_sq - source * source)
    real_r, imag_r = root_pair(omega_sq - receiver * receiver)
    decay = jnp.exp(-dz_cells * (imag_s + imag_r))
    turn = dz_cells * (real_s + real_r)
    return (decay * jnp.cos(turn), decay * jnp.sin(turn))


def halves_np(table):
    high = table.astype(np.float32).astype(jnp.bfloat16)
    low = (table - high.astype(np.float64)).astype(np.float32).astype(jnp.bfloat16)
    return high, low


def block_tables():
    index = np.arange(BLK)
    angles = 2.0 * np.pi * (np.outer(index, index) % BLK) / BLK
    cos, sin = np.cos(angles), np.sin(angles)
    upper = np.block([[cos, sin], [-sin, cos]])
    lower = np.block([[cos, -sin], [sin, cos]])
    tables = []
    for axis, pair in ((1, (upper, lower)), (0, (lower, upper))):
        for table in pair:
            high, low = halves_np(table)
            tables.append(np.concatenate([high, high, low], axis=axis))
    return tables


def twiddle_tables(outer):
    ka, b = np.arange(outer)[:, None], np.arange(BLK)[None, :]
    angles = 2.0 * np.pi * ka * b / (outer * BLK)
    middle = np.stack([np.cos(angles), np.sin(angles)]).astype(np.float32)
    rows = 2.0 * np.pi * np.arange(HALF) / NH
    offset = np.stack([np.cos(rows), np.sin(rows)]).astype(np.float32)
    return middle, np.broadcast_to(offset[:, :, None], (2, HALF, BLK)).copy()


def halves(value):
    high = value.astype(jnp.bfloat16)
    return high, (value - high.astype(jnp.float32)).astype(jnp.bfloat16)


def dot(left, right):
    return jnp.dot(left, right, preferred_element_type=jnp.float32)


def left_product(table, value):
    high, low = halves(value)
    return dot(table, jnp.concatenate([high, low, high], axis=0))


def right_product(value, table):
    high, low = halves(value)
    return dot(jnp.concatenate([high, low, high], axis=1), table)


def cmul(real_a, imag_a, real_b, imag_b):
    return real_a * real_b - imag_a * imag_b, real_a * imag_b + imag_a * real_b


def small_transform(values, sign):
    count = len(values)
    if count == 1:
        return values
    even = small_transform(values[0::2], sign)
    odd = small_transform(values[1::2], sign)
    first, second = [], []
    for k in range(count // 2):
        er, ei = even[k]
        xr, xi = odd[k]
        if k == 0:
            tr, ti = xr, xi
        elif 4 * k == count:
            tr, ti = (-xi, xr) if sign > 0 else (xi, -xr)
        else:
            c, s = math.cos(2 * math.pi * k / count), sign * math.sin(2 * math.pi * k / count)
            if 8 * k == count:
                tr, ti = ((xr - xi) * c, (xr + xi) * c) if sign > 0 else ((xr + xi) * c, (xi - xr) * c)
            elif 8 * k == 3 * count:
                tr, ti = ((xr + xi) * c, (xi - xr) * c) if sign > 0 else ((xr - xi) * c, (xr + xi) * c)
            else:
                tr, ti = xr * c - xi * s, xr * s + xi * c
        first.append((er + tr, ei + ti))
        second.append((er - tr, ei - ti))
    return first + second


def scale_code(biggest):
    return (jnp.floor(jnp.log(jnp.maximum(biggest, 1e-30)) * STEP_LOG) + 1.0).astype(jnp.int32)


def scale_of(code):
    return jnp.exp(code.astype(jnp.float32) * (1.0 / STEP_LOG)) * (1.0 / TOP)


def inverse_scale_of(code):
    return jnp.exp(code.astype(jnp.float32) * (-1.0 / STEP_LOG)) * TOP


def coded(value, inverse):
    return jnp.floor(value * inverse + 0.5).astype(jnp.int32)


def packed(high, low):
    return (high << 16) | (low & 0xFFFF)


def unpacked(word):
    return (word >> 16).astype(jnp.float32), ((word << 16) >> 16).astype(jnp.float32)


def contribution_kernel(slot_ref, bin_ref, data_ref, *rest):
    *sources, out_ref, held, weight_ref, sems = rest
    count = sources[0].shape[0]
    copies = [
        pltpu.make_async_copy(ref, weight_ref.at[pl.ds(n * count, count)], sems.at[n])
        for n, ref in enumerate(sources)
    ]
    for copy in copies:
        copy.start()
    for copy in copies:
        copy.wait()
    freqs, groups = out_ref.shape[:2]
    outer = out_ref.shape[2] - 1

    @pl.loop(0, groups)
    def _(group):
        for at in range(GROUP):
            slot = slot_ref[group * GROUP + at]
            source = bin_ref[group * GROUP + at]
            held[pl.ds(at, data_ref.shape[1], GROUP), :] = dot(data_ref[source], weight_ref[slot])
        for f in range(freqs):
            base = f * 2 * outer * GROUP
            biggest = jnp.abs(held[pl.ds(base, GROUP), :])
            for at in range(1, 2 * outer):
                biggest = jnp.maximum(biggest, jnp.abs(held[pl.ds(base + at * GROUP, GROUP), :]))
            code = scale_code(biggest)
            inverse = inverse_scale_of(code)
            for a in range(outer):
                real = held[pl.ds(base + a * GROUP, GROUP), :]
                imag = held[pl.ds(base + (outer + a) * GROUP, GROUP), :]
                out_ref[f, group, a] = packed(coded(real, inverse), coded(imag, inverse))
            out_ref[f, group, outer] = code


def column_of(plane, a):
    lanes = pl.ds(pl.multiple_of(a * BLK, BLK), BLK)
    return jnp.concatenate(
        [
            jnp.concatenate([plane[p, 0, :, lanes], plane[p, 1, :, lanes]], axis=0)
            for p in range(2)
        ],
        axis=1,
    )


def store_column(plane, a, value):
    lanes = pl.ds(pl.multiple_of(a * BLK, BLK), BLK)
    for p in range(2):
        for c in range(2):
            plane[p, c, :, lanes] = value[c * HALF : (c + 1) * HALF, p * BLK : (p + 1) * BLK]


def row_blocks(tall):
    return [slice(at * tall, (at + 1) * tall) for at in range(HALF // tall)]


def turn_at(offset_ref, rows):
    return offset_ref[0, rows], offset_ref[1, rows]


def forward_rows(low, high, turn):
    first = low[0] + high[0], low[1] + high[1]
    second = cmul(low[0] - high[0], low[1] - high[1], turn[0], -turn[1])
    return (*first, *second)


def inverse_rows(value, rows, turn):
    upper, below = rows, slice(HALF + rows.start, HALF + rows.stop)
    first = value[upper, :BLK], value[below, :BLK]
    second = cmul(value[upper, BLK:], value[below, BLK:], turn[0], turn[1])
    low = first[0] + second[0], first[1] + second[1]
    high = first[0] - second[0], first[1] - second[1]
    return low, high


def assembled(blocks):
    parts = [jnp.concatenate(part, axis=0) for part in zip(*blocks)]
    return jnp.concatenate(
        [jnp.concatenate(parts[:2], axis=0), jnp.concatenate(parts[2:], axis=0)], axis=1
    )


def offset_product(table, columns):
    value = left_product(table[...], jnp.concatenate(columns, axis=1))
    return [value[:, n * 2 * BLK : (n + 1) * 2 * BLK] for n in range(len(columns))]


def layer_turn(pair, layer_ref, step, block, a):
    half = layer_ref.shape[2] // 2
    return [
        cmul(*part, layer_ref[0, step, block + p * half, a], layer_ref[1, step, block + p * half, a])
        for p, part in enumerate(pair)
    ]


def midpoint_pass(plane, out, phase_refs, forward, inverse, middle_ref):
    outer = middle_ref.shape[1]
    lanes = [slice(a * BLK, (a + 1) * BLK) for a in range(outer)]
    tall = ROWS * CHUNKS
    per_half = HALF // tall

    @pl.loop(0, 2 * per_half, unroll=UNROLL)
    def _(at):
        p = at // per_half
        base = pl.multiple_of((at % per_half) * tall, tall)
        phase_base = pl.multiple_of(at * tall, tall)

        def gathered(pieces):
            return jnp.concatenate([jnp.concatenate(pair, axis=1) for pair in pieces], axis=0)

        pieces = []
        for chunk in range(CHUNKS):
            here = pl.ds(base + chunk * ROWS, ROWS)
            values = [(plane[p, 0, here, lane], plane[p, 1, here, lane]) for lane in lanes]
            values = small_transform(values, -1)
            for a in range(outer):
                pieces.append(cmul(*values[a], middle_ref[0, a : a + 1], -middle_ref[1, a : a + 1]))
        value = right_product(gathered(pieces), forward[...])
        pieces = []
        for chunk in range(CHUNKS):
            there = pl.ds(phase_base + chunk * ROWS, ROWS)
            for a in range(outer):
                row = (chunk * outer + a) * ROWS
                part = value[row : row + ROWS]
                pieces.append(
                    cmul(
                        part[:, :BLK], part[:, BLK:],
                        phase_refs[0][there, lanes[a]], phase_refs[1][there, lanes[a]],
                    )
                )
        value = right_product(gathered(pieces), inverse[...])
        for chunk in range(CHUNKS):
            here = pl.ds(base + chunk * ROWS, ROWS)
            values = []
            for a in range(outer):
                row = (chunk * outer + a) * ROWS
                part = value[row : row + ROWS]
                values.append(
                    cmul(part[:, :BLK], part[:, BLK:], middle_ref[0, a : a + 1], middle_ref[1, a : a + 1])
                )
            values = small_transform(values, 1)
            for a in range(outer):
                out[p, 0, here, lanes[a]] = values[a][0]
                out[p, 1, here, lanes[a]] = values[a][1]


def march_kernel(
    layer_ref, code_ref, pick_ref, phase_real, phase_imag, rows_forward, rows_inverse, lanes_forward,
    lanes_inverse, middle_ref, offset_ref, other, plane, scales,
):
    sources, groups = code_ref.shape[:2]
    outer = middle_ref.shape[1]
    steps = layer_ref.shape[1]
    slots = sources * groups * GROUP
    tall = NH // layer_ref.shape[2]

    scales[...] = scale_of(code_ref[:, :, outer].reshape(slots, BLK))

    @pl.loop(0, outer // COLUMNS, unroll=2)
    def _(at):
        columns = []
        for a in range(COLUMNS):
            real, imag = unpacked(code_ref[:, :, at * COLUMNS + a].reshape(slots, BLK))
            scale = scales[...]
            value = jnp.concatenate([real * scale, imag * scale], axis=1)
            moved = dot(pick_ref[...], jnp.concatenate(halves(value), axis=0))
            blocks = []
            for rows in row_blocks(tall):
                low, high = moved[rows], moved[HALF + rows.start : HALF + rows.stop]
                blocks.append(
                    forward_rows(
                        (low[:, :BLK], low[:, BLK:]), (high[:, :BLK], high[:, BLK:]),
                        turn_at(offset_ref, rows),
                    )
                )
            columns.append(assembled(blocks))
        for a, value in enumerate(offset_product(rows_forward, columns)):
            store_column(plane, at * COLUMNS + a, value)

    for step in range(steps):
        midpoint_pass(plane, other, (phase_real, phase_imag), lanes_forward, lanes_inverse, middle_ref)
        if step < steps - 1:

            @pl.loop(0, outer // COLUMNS, unroll=2)
            def _(at):
                places = [at * COLUMNS + a for a in range(COLUMNS)]
                columns = []
                for a, value in zip(
                    places, offset_product(rows_inverse, [column_of(other, a) for a in places])
                ):
                    blocks = []
                    for block, rows in enumerate(row_blocks(tall)):
                        turn = turn_at(offset_ref, rows)
                        pair = inverse_rows(value, rows, turn)
                        blocks.append(forward_rows(*layer_turn(pair, layer_ref, step, block, a), turn))
                    columns.append(assembled(blocks))
                for a, value in zip(places, offset_product(rows_forward, columns)):
                    store_column(plane, a, value)


def finish_kernel(dest_ref, layer_ref, plane_ref, rows_inverse, offset_ref, *rest):
    out_ref = rest[-1]
    here = plane_ref.shape[3] // BLK
    tall = NH // layer_ref.shape[2]
    step = layer_ref.shape[1] - 1
    columns = offset_product(rows_inverse, [column_of(plane_ref, at) for at in range(here)])
    for at in range(here):
        found = []
        for block, rows in enumerate(row_blocks(tall)):
            pair = inverse_rows(columns[at], rows, turn_at(offset_ref, rows))
            found.append(layer_turn(pair, layer_ref, step, block, dest_ref[0] * here + at))
        for c in range(2):
            biggest = functools.reduce(jnp.maximum, [jnp.abs(part[c]) for pair in found for part in pair])
            code = scale_code(jnp.max(biggest, axis=0, keepdims=True))
            inverse = inverse_scale_of(code)
            row = at * 2 + c
            for block, pair in enumerate(found):
                words = packed(coded(pair[0][c], inverse), coded(pair[1][c], inverse))
                out_ref[pl.ds(block * tall * 2 * here + row, tall, 2 * here), :] = words
            out_ref[pl.ds(HALF * 2 * here + row, 1), :] = code


def result_kernel(freq_ref, code_ref, *rest):
    out_ref = rest[-1]
    per, tall = out_ref.shape[1:3]
    scale = scale_of(code_ref[per * tall :])[None]
    for half in range(2):

        @pl.when(pl.program_id(0) == half)
        def _():
            out_ref[0] = unpacked(code_ref[: per * tall].reshape(per, tall, BLK))[half] * scale


def take_kernel(mine_ref, counts_ref, source_ref, out_ref, sems):
    taken, entries = out_ref.shape[0], source_ref.shape[1]
    bins_here, stride = source_ref.shape[0], source_ref.shape[0] * entries // taken
    copies = []
    for n in range(taken):
        entry, bin_at = n * stride + mine_ref[0], 0
        for b in range(bins_here - 1):
            over = (bin_at == b) & (entry >= counts_ref[b])
            entry = jnp.where(over, entry - counts_ref[b], entry)
            bin_at = jnp.where(over, b + 1, bin_at)
        entry = jnp.minimum(entry, entries - 1)
        copies.append(
            pltpu.make_async_copy(source_ref.at[bin_at, entry], out_ref.at[n], sems.at[n])
        )
        copies[-1].start()
    for copy in copies:
        copy.wait()


def slot_lists(counts_all, targets_all, bins_local, fl, per_device, room):
    offs = counts_all.shape[0] // bins_local
    entries = targets_all.shape[1]
    counts_in = counts_all.reshape(offs, bins_local)
    live = jnp.sum(counts_in, axis=1)
    quarter = jnp.arange(fl, dtype=jnp.int32)
    held = (live[None, :] - quarter[:, None] + fl - 1) // fl
    upto = jnp.sum(
        jnp.where(jnp.arange(offs)[None, :] <= jnp.arange(offs)[:, None], held[:, None, :], 0), axis=2
    )
    at = jnp.arange(room, dtype=jnp.int32)
    past = (at[None, :, None] >= upto[:, None, :]).astype(jnp.int32)
    off_at = jnp.sum(past, axis=2)
    valid = off_at < offs
    off_at = jnp.minimum(off_at, offs - 1)
    start = jnp.sum(past * held[:, None, :], axis=2)
    nth = jnp.clip(at[None, :] - start, 0, per_device - 1)
    entry = nth * fl + quarter[:, None]
    bin_at = off_at * bins_local
    mine = off_at[:, :, None] == jnp.arange(offs)[None, None, :]
    for b in range(bins_local - 1):
        size = jnp.sum(jnp.where(mine, counts_in[None, None, :, b], 0), axis=2)
        over = (bin_at == off_at * bins_local + b) & (entry >= size)
        bin_at = bin_at + over
        entry = entry - jnp.where(over, size, 0)
    flat = bin_at * entries + entry
    total = targets_all.size
    picks = flat[:, :, None] == jnp.arange(total)[None, None, :]
    target = jnp.sum(jnp.where(picks, targets_all.reshape(1, 1, total), 0), axis=2)
    target = jnp.where(valid, target, -1)
    return off_at, nth, bin_at, target


def local(bins_data, operators, targets, counts, layer_index, slowness):
    off_count = lax.axis_size("off")
    mid_count = lax.axis_size("mid")
    bins_local, freq_total, _, mid_local = bins_data.shape
    entries = operators.shape[1]
    bins_total = bins_local * off_count
    fl = freq_total // off_count
    total_mid = mid_local * mid_count
    outer = total_mid // BLK
    mid_at, off_at = lax.axis_index("mid"), lax.axis_index("off")
    assert mid_count % fl == 0 and (bins_local * entries) % fl == 0
    mine = mid_at % fl
    rounds = mid_count // fl
    groups = (
        None if rounds == 1 else [list(range(g * fl, (g + 1) * fl)) for g in range(rounds)]
    )

    per_device = bins_local * entries // fl
    smem = pl.BlockSpec(memory_space=pltpu.SMEM)
    vmem = pl.BlockSpec(memory_space=pltpu.VMEM)
    hbm = pl.BlockSpec(memory_space=pl.ANY)
    pairs = fl * 2

    def extra(whole_numbers, copies):
        flat = whole_numbers.astype(jnp.bfloat16).reshape(1, 1, 1, -1)
        flat = jnp.pad(flat, ((0, 0), (0, 0), (0, pairs - 1), (0, mid_local - flat.shape[3])))
        return jnp.broadcast_to(flat, (1, copies, pairs, mid_local))

    lists = jnp.concatenate([counts[:, None], targets], axis=1)
    data = bins_data.reshape(bins_local, off_count, pairs, mid_local)
    data = jnp.concatenate([data, extra(lists, off_count)], axis=0)
    data = lax.all_to_all(data, "off", split_axis=1, concat_axis=0, tiled=True)

    own = pl.pallas_call(
        take_kernel,
        in_specs=[smem, smem, hbm],
        out_specs=vmem,
        out_shape=jax.ShapeDtypeStruct((per_device, BLK, BLK), jnp.bfloat16),
        scratch_shapes=[pltpu.SemaphoreType.DMA((per_device,))],
        compiler_params=pltpu.CompilerParams(vmem_limit_bytes=SMALL),
        name="take_own",
    )(mine.reshape(1), counts, operators)
    data, own = lax.optimization_barrier((data, own))
    cores = 2 if off_count % 2 == 0 else 1
    line = off_count // cores
    assert line & (line - 1) == 0 and fl & (fl - 1) == 0
    shares = [own]
    for away in range(1, line):
        low = away & -away
        shares.append(
            lax.ppermute(
                shares[away ^ low],
                "off",
                [(i, (i // cores ^ low) * cores + i % cores) for i in range(off_count)],
            )
        )
    if cores > 1:
        shares += [lax.ppermute(x, "off", [(i, i ^ 1) for i in range(off_count)]) for x in shares]

    data = data.reshape(off_count, bins_local + 1, pairs, mid_local)
    lists = data[:, bins_local, 0, : lists.size].astype(jnp.int32).reshape(bins_total, 1 + entries)
    data = data[:, :bins_local].reshape(bins_total, pairs, mid_local)
    data = jnp.concatenate([data, extra(layer_index, 1)[0]], axis=0)
    data = lax.all_gather(data, "mid", axis=0)
    layers = data[:, bins_total, 0, : layer_index.size].astype(jnp.int32)
    layers = layers.reshape(mid_count, *layer_index.shape).transpose(1, 2, 0, 3)
    layers = layers.reshape(*layer_index.shape[:2], outer)
    data = data[:, :bins_total].reshape(mid_count, bins_total, pairs, mid_local // BLK, BLK)
    data = data.transpose(1, 2, 0, 3, 4).reshape(bins_total, pairs * outer, BLK)

    live_total = bins_total * entries // 2
    room = -(-(live_total + (fl - 1) * off_count) // fl)
    room = min(-(-room // GROUP) * GROUP, per_device * off_count)
    offs, nth, bins, goal = slot_lists(lists[:, 0], lists[:, 1:], bins_local, fl, per_device, room)
    side = (offs % cores != off_at % cores).astype(jnp.int32) * line
    slots = (side + ((offs // cores) ^ (off_at // cores))) * per_device + nth
    own_slots = lax.dynamic_index_in_dim(slots, mine, 0, False)
    own_bins = lax.dynamic_index_in_dim(bins, mine, 0, False)
    list_groups = room // GROUP
    terms = pl.pallas_call(
        contribution_kernel,
        in_specs=[smem, smem, vmem] + [hbm] * len(shares),
        out_specs=vmem,
        out_shape=jax.ShapeDtypeStruct((fl, list_groups, outer + 1, GROUP, BLK), jnp.int32),
        scratch_shapes=[
            pltpu.VMEM((fl * 2 * outer * GROUP, BLK), jnp.float32),
            pltpu.VMEM((len(shares) * per_device, BLK, BLK), jnp.bfloat16),
            pltpu.SemaphoreType.DMA((len(shares),)),
        ],
        compiler_params=pltpu.CompilerParams(vmem_limit_bytes=SMALL),
        name="contributions",
    )(own_slots, own_bins, data, *shares)
    terms, goal, layers, freq_at = lax.optimization_barrier((terms, goal, layers, off_at * fl + mine))
    pick = (
        jnp.tile(goal.reshape(1, fl * room), (1, 2))
        == lax.broadcasted_iota(jnp.int32, (NH, 2 * fl * room), 0)
    ).astype(jnp.bfloat16)

    omega = math.pi * (0.1 + 0.8 * (freq_at.astype(jnp.float32) + 0.5) / freq_total)
    row = lax.broadcasted_iota(jnp.int32, (NH, total_mid), 0)
    lane = lax.broadcasted_iota(jnp.int32, (NH, total_mid), 1)
    offset_wave = signed_wave(2 * (row % HALF) + row // HALF, NH)
    mid_wave = signed_wave(lane // BLK + outer * (lane % BLK), total_mid)
    phase_real, phase_imag = propagator(omega * omega, mid_wave, offset_wave)
    phase_real, phase_imag = (x * (1.0 / (NH * total_mid)) for x in (phase_real, phase_imag))

    layer_total = slowness.shape[1]
    chosen = layers[..., None] == jnp.arange(layer_total)
    slow = jnp.sum(jnp.where(chosen, slowness[:, None, None, :], 0.0), axis=-1)
    turn = 2.0 * dz_cells * omega * (slow - 1.0)
    layer_turns = jnp.stack([jnp.cos(turn), jnp.sin(turn)])

    terms = lax.all_to_all(
        terms, "mid", split_axis=0, concat_axis=0, axis_index_groups=groups, tiled=True
    )

    middle, offset_turn = twiddle_tables(outer)
    here = mid_local // BLK
    rows_out = (HALF + 1) * 2 * here
    tables = [jnp.asarray(t) for t in block_tables()]
    middle, offset_turn = jnp.asarray(middle), jnp.asarray(offset_turn)
    plane = pl.pallas_call(
        march_kernel,
        in_specs=[smem] + [vmem] * 10,
        out_specs=vmem,
        out_shape=jax.ShapeDtypeStruct((2, 2, HALF, total_mid), jnp.float32),
        scratch_shapes=[
            pltpu.VMEM((2, 2, HALF, total_mid), jnp.float32),
            pltpu.VMEM((fl * room, BLK), jnp.float32),
        ],
        compiler_params=pltpu.CompilerParams(vmem_limit_bytes=VMEM),
        name="march",
    )(layer_turns, terms, pick, phase_real, phase_imag, *tables, middle, offset_turn)

    def finish(dest, *before):
        return pl.pallas_call(
            finish_kernel,
            grid_spec=pltpu.PrefetchScalarGridSpec(
                num_scalar_prefetch=1,
                grid=(1,),
                in_specs=[
                    smem,
                    pl.BlockSpec((2, 2, HALF, mid_local), lambda i, dest: (0, 0, 0, dest[0])),
                    vmem,
                    vmem,
                ]
                + [hbm] * len(before),
                out_specs=pl.BlockSpec((rows_out, BLK), lambda i, dest: (0, 0)),
            ),
            out_shape=jax.ShapeDtypeStruct((rows_out, BLK), jnp.int32),
            cost_estimate=pl.CostEstimate(
                flops=6 * NH * NH * 2 * BLK * here, bytes_accessed=6 * NH * mid_local, transcendentals=0
            ),
            compiler_params=pltpu.CompilerParams(vmem_limit_bytes=SMALL),
            name="finish",
        )(dest.reshape(1), layer_turns, plane, tables[1], offset_turn, *before)

    got, before = {}, []
    for ahead in [*range(fl - 1, 0, -1), 0]:
        dest = (mid_at // fl) * fl + (mine ^ ahead)
        block = finish(dest, *before)
        before = [block]
        if ahead:
            block = lax.ppermute(block, "mid", [(s, s ^ ahead) for s in range(mid_count)])
        got[ahead] = block

    field = None
    for ahead in [0, *range(fl - 1, 0, -1)]:
        freq = mine ^ ahead
        first = field is None
        field = pl.pallas_call(
            result_kernel,
            grid_spec=pltpu.PrefetchScalarGridSpec(
                num_scalar_prefetch=1,
                grid=(2,),
                in_specs=[vmem] if first else [vmem, hbm],
                out_specs=pl.BlockSpec((1, HALF, 2 * here, BLK), lambda i, f: (f[0], i, 0, 0)),
            ),
            out_shape=jax.ShapeDtypeStruct((fl, NH, 2 * here, BLK), jnp.float32),
            input_output_aliases={} if first else {2: 0},
            compiler_params=pltpu.CompilerParams(vmem_limit_bytes=SMALL),
            cost_estimate=pl.CostEstimate(
                flops=4 * NH * mid_local, bytes_accessed=12 * NH * mid_local, transcendentals=0
            ),
            name="result",
        )(freq.reshape(1), got[ahead], *([] if first else [field]))
    field = field.reshape(fl, NH, here, 2, BLK).transpose(0, 1, 3, 2, 4)
    return field.reshape(fl, NH, 2, mid_local)


def solution(mesh):
    in_specs = (
        P("off", None, None, "mid"),
        P("off", None, None, None),
        P("off", None),
        P("off"),
        P(None, None, "mid"),
        P(),
    )
    out_specs = P("off", None, None, "mid")
    return jax.shard_map(local, mesh=mesh, in_specs=in_specs, out_specs=out_specs, check_vma=False)
```

```python
import functools
import math

import jax
import jax.numpy as jnp
import numpy as np
from jax import lax
from jax.experimental import pallas as pl
from jax.experimental.pallas import tpu as pltpu
from jax.sharding import PartitionSpec as P

NH = 256
BLK = 128

dz_cells = 2.0
damping = 0.1

HALF = NH // 2
STEP_LOG = 64.0
TOP = 32767.0
GROUP = 8
COLUMNS = 2
ROWS = 8
CHUNKS = 4
UNROLL = 2
VMEM = 28 * 1024 * 1024
SMALL = 10 * 1024 * 1024


def signed_wave(index, length):
    signed = (index + length // 2) % length - length // 2
    return signed.astype(jnp.float32) * (2.0 * math.pi / length)


def root_pair(level):
    magnitude = jnp.sqrt(level * level + damping * damping)
    larger = jnp.sqrt(0.5 * (magnitude + jnp.abs(level)))
    smaller = damping / (2.0 * larger)
    return (jnp.where(level >= 0, larger, smaller), jnp.where(level >= 0, smaller, larger))


def propagator(omega_sq, mid_wave, offset_wave):
    source = 0.5 * (mid_wave - offset_wave)
    receiver = 0.5 * (mid_wave + offset_wave)
    real_s, imag_s = root_pair(omega_sq - source * source)
    real_r, imag_r = root_pair(omega_sq - receiver * receiver)
    decay = jnp.exp(-dz_cells * (imag_s + imag_r))
    turn = dz_cells * (real_s + real_r)
    return (decay * jnp.cos(turn), decay * jnp.sin(turn))


def halves_np(table):
    high = table.astype(np.float32).astype(jnp.bfloat16)
    low = (table - high.astype(np.float64)).astype(np.float32).astype(jnp.bfloat16)
    return high, low


def block_tables():
    index = np.arange(BLK)
    angles = 2.0 * np.pi * (np.outer(index, index) % BLK) / BLK
    cos, sin = np.cos(angles), np.sin(angles)
    upper = np.block([[cos, sin], [-sin, cos]])
    lower = np.block([[cos, -sin], [sin, cos]])
    tables = []
    for axis, pair in ((1, (upper, lower)), (0, (lower, upper))):
        for table in pair:
            high, low = halves_np(table)
            tables.append(np.concatenate([high, high, low], axis=axis))
    return tables


def twiddle_tables(outer):
    ka, b = np.arange(outer)[:, None], np.arange(BLK)[None, :]
    angles = 2.0 * np.pi * ka * b / (outer * BLK)
    middle = np.stack([np.cos(angles), np.sin(angles)]).astype(np.float32)
    rows = 2.0 * np.pi * np.arange(HALF) / NH
    offset = np.stack([np.cos(rows), np.sin(rows)]).astype(np.float32)
    return middle, np.broadcast_to(offset[:, :, None], (2, HALF, BLK)).copy()


def halves(value):
    high = value.astype(jnp.bfloat16)
    return high, (value - high.astype(jnp.float32)).astype(jnp.bfloat16)


def dot(left, right):
    return jnp.dot(left, right, preferred_element_type=jnp.float32)


def left_product(table, value):
    high, low = halves(value)
    return dot(table, jnp.concatenate([high, low, high], axis=0))


def right_product(value, table):
    high, low = halves(value)
    return dot(jnp.concatenate([high, low, high], axis=1), table)


def cmul(real_a, imag_a, real_b, imag_b):
    return real_a * real_b - imag_a * imag_b, real_a * imag_b + imag_a * real_b


def small_transform(values, sign):
    count = len(values)
    if count == 1:
        return values
    even = small_transform(values[0::2], sign)
    odd = small_transform(values[1::2], sign)
    first, second = [], []
    for k in range(count // 2):
        er, ei = even[k]
        xr, xi = odd[k]
        if k == 0:
            tr, ti = xr, xi
        elif 4 * k == count:
            tr, ti = (-xi, xr) if sign > 0 else (xi, -xr)
        else:
            c, s = math.cos(2 * math.pi * k / count), sign * math.sin(2 * math.pi * k / count)
            if 8 * k == count:
                tr, ti = ((xr - xi) * c, (xr + xi) * c) if sign > 0 else ((xr + xi) * c, (xi - xr) * c)
            elif 8 * k == 3 * count:
                tr, ti = ((xr + xi) * c, (xi - xr) * c) if sign > 0 else ((xr - xi) * c, (xr + xi) * c)
            else:
                tr, ti = xr * c - xi * s, xr * s + xi * c
        first.append((er + tr, ei + ti))
        second.append((er - tr, ei - ti))
    return first + second


def scale_code(biggest):
    return (jnp.floor(jnp.log(jnp.maximum(biggest, 1e-30)) * STEP_LOG) + 1.0).astype(jnp.int32)


def scale_of(code):
    return jnp.exp(code.astype(jnp.float32) * (1.0 / STEP_LOG)) * (1.0 / TOP)


def inverse_scale_of(code):
    return jnp.exp(code.astype(jnp.float32) * (-1.0 / STEP_LOG)) * TOP


def coded(value, inverse):
    return jnp.floor(value * inverse + 0.5).astype(jnp.int32)


def packed(high, low):
    return (high << 16) | (low & 0xFFFF)


def unpacked(word):
    return (word >> 16).astype(jnp.float32), ((word << 16) >> 16).astype(jnp.float32)


def contribution_kernel(place_ref, order_ref, slot_ref, bin_ref, data_ref, *rest, freqs):
    *sources, held, weight_ref, sems = rest
    sources, outs = sources[:-freqs], sources[-freqs:]
    groups, outer = outs[0].shape[0], outs[0].shape[1] - 1
    count = sources[0].shape[0]
    copies = [
        pltpu.make_async_copy(ref, weight_ref.at[pl.ds(n * count, count)], sems.at[n])
        for n, ref in enumerate(sources)
    ]
    for copy in copies:
        copy.start()
    for copy in copies:
        copy.wait()

    @pl.loop(0, groups)
    def _(group):
        for at in range(GROUP):
            slot = slot_ref[group * GROUP + at]
            source = bin_ref[group * GROUP + at]
            held[pl.ds(at, data_ref.shape[1], GROUP), :] = dot(data_ref[source], weight_ref[slot])
        for away, out_ref in enumerate(outs):
            base = (place_ref[0] ^ away) * (2 * outer * GROUP)

            def term(at):
                return held[pl.ds(pl.multiple_of(base + at * GROUP, GROUP), GROUP), :]

            biggest = functools.reduce(jnp.maximum, [jnp.abs(term(at)) for at in range(2 * outer)])
            code = scale_code(biggest)
            inverse = inverse_scale_of(code)
            for a in range(outer):
                words = packed(coded(term(a), inverse), coded(term(outer + a), inverse))
                out_ref[group, order_ref[a]] = words
            out_ref[group, outer] = code


def column_of(plane, a):
    lanes = pl.ds(pl.multiple_of(a * BLK, BLK), BLK)
    return jnp.concatenate(
        [
            jnp.concatenate([plane[p, 0, :, lanes], plane[p, 1, :, lanes]], axis=0)
            for p in range(2)
        ],
        axis=1,
    )


def store_column(plane, a, value):
    lanes = pl.ds(pl.multiple_of(a * BLK, BLK), BLK)
    for p in range(2):
        for c in range(2):
            plane[p, c, :, lanes] = value[c * HALF : (c + 1) * HALF, p * BLK : (p + 1) * BLK]


def row_blocks(tall):
    return [slice(at * tall, (at + 1) * tall) for at in range(HALF // tall)]


def turn_at(offset_ref, rows):
    return offset_ref[0, rows], offset_ref[1, rows]


def forward_rows(low, high, turn):
    first = low[0] + high[0], low[1] + high[1]
    second = cmul(low[0] - high[0], low[1] - high[1], turn[0], -turn[1])
    return (*first, *second)


def inverse_rows(value, rows, turn):
    upper, below = rows, slice(HALF + rows.start, HALF + rows.stop)
    first = value[upper, :BLK], value[below, :BLK]
    second = cmul(value[upper, BLK:], value[below, BLK:], turn[0], turn[1])
    low = first[0] + second[0], first[1] + second[1]
    high = first[0] - second[0], first[1] - second[1]
    return low, high


def assembled(blocks):
    parts = [jnp.concatenate(part, axis=0) for part in zip(*blocks)]
    return jnp.concatenate(
        [jnp.concatenate(parts[:2], axis=0), jnp.concatenate(parts[2:], axis=0)], axis=1
    )


def propagator_kernel(omega_ref, real_ref, imag_ref):
    total = real_ref.shape[1]
    scale = 1.0 / (NH * total)
    omega_sq = omega_ref[0] * omega_ref[0]

    @pl.loop(0, NH // GROUP)
    def _(at):
        start = pl.multiple_of(at * GROUP, GROUP)
        row = lax.broadcasted_iota(jnp.int32, (GROUP, BLK), 0) + at * GROUP
        lane = lax.broadcasted_iota(jnp.int32, (GROUP, BLK), 1)
        offset_wave = signed_wave(2 * (row % HALF) + row // HALF, NH)
        for a in range(total // BLK):
            mid_wave = signed_wave(a + total // BLK * lane, total)
            real, imag = propagator(omega_sq, mid_wave, offset_wave)
            real_ref[pl.ds(start, GROUP), a * BLK : (a + 1) * BLK] = real * scale
            imag_ref[pl.ds(start, GROUP), a * BLK : (a + 1) * BLK] = imag * scale


def offset_product(table, columns):
    value = left_product(table[...], jnp.concatenate(columns, axis=1))
    return [value[:, n * 2 * BLK : (n + 1) * 2 * BLK] for n in range(len(columns))]


def layer_turn(pair, layer_ref, step, block, a):
    half = layer_ref.shape[2] // 2
    return [
        cmul(*part, layer_ref[0, step, block + p * half, a], layer_ref[1, step, block + p * half, a])
        for p, part in enumerate(pair)
    ]


def midpoint_pass(plane, out, phase_refs, forward, inverse, middle_ref):
    outer = middle_ref.shape[1]
    lanes = [slice(a * BLK, (a + 1) * BLK) for a in range(outer)]
    tall = ROWS * CHUNKS
    per_half = HALF // tall

    @pl.loop(0, 2 * per_half, unroll=UNROLL)
    def _(at):
        p = at // per_half
        base = pl.multiple_of((at % per_half) * tall, tall)
        phase_base = pl.multiple_of(at * tall, tall)

        def gathered(pieces):
            return jnp.concatenate([jnp.concatenate(pair, axis=1) for pair in pieces], axis=0)

        pieces = []
        for chunk in range(CHUNKS):
            here = pl.ds(base + chunk * ROWS, ROWS)
            values = [(plane[p, 0, here, lane], plane[p, 1, here, lane]) for lane in lanes]
            values = small_transform(values, -1)
            for a in range(outer):
                pieces.append(cmul(*values[a], middle_ref[0, a : a + 1], -middle_ref[1, a : a + 1]))
        value = right_product(gathered(pieces), forward[...])
        pieces = []
        for chunk in range(CHUNKS):
            there = pl.ds(phase_base + chunk * ROWS, ROWS)
            for a in range(outer):
                row = (chunk * outer + a) * ROWS
                part = value[row : row + ROWS]
                pieces.append(
                    cmul(
                        part[:, :BLK], part[:, BLK:],
                        phase_refs[0][there, lanes[a]], phase_refs[1][there, lanes[a]],
                    )
                )
        value = right_product(gathered(pieces), inverse[...])
        for chunk in range(CHUNKS):
            here = pl.ds(base + chunk * ROWS, ROWS)
            values = []
            for a in range(outer):
                row = (chunk * outer + a) * ROWS
                part = value[row : row + ROWS]
                values.append(
                    cmul(part[:, :BLK], part[:, BLK:], middle_ref[0, a : a + 1], middle_ref[1, a : a + 1])
                )
            values = small_transform(values, 1)
            for a in range(outer):
                out[p, 0, here, lanes[a]] = values[a][0]
                out[p, 1, here, lanes[a]] = values[a][1]


def march_kernel(layer_ref, *rest, sources):
    code_refs, rest = rest[:sources], rest[sources:]
    (
        pick_ref, phase_real, phase_imag, rows_forward, rows_inverse, lanes_forward, lanes_inverse,
        middle_ref, offset_ref, other, plane, scales,
    ) = rest
    groups = code_refs[0].shape[0]
    outer = middle_ref.shape[1]
    steps = layer_ref.shape[1]
    tall = NH // layer_ref.shape[2]

    def words(a):
        return jnp.concatenate([ref[:, a].reshape(groups * GROUP, BLK) for ref in code_refs], axis=0)

    scales[...] = scale_of(words(outer))

    @pl.loop(0, outer // COLUMNS, unroll=2)
    def _(at):
        columns = []
        for a in range(COLUMNS):
            real, imag = unpacked(words(at * COLUMNS + a))
            scale = scales[...]
            value = jnp.concatenate([real * scale, imag * scale], axis=1)
            moved = dot(pick_ref[...], jnp.concatenate(halves(value), axis=0))
            blocks = []
            for rows in row_blocks(tall):
                low, high = moved[rows], moved[HALF + rows.start : HALF + rows.stop]
                blocks.append(
                    forward_rows(
                        (low[:, :BLK], low[:, BLK:]), (high[:, :BLK], high[:, BLK:]),
                        turn_at(offset_ref, rows),
                    )
                )
            columns.append(assembled(blocks))
        for a, value in enumerate(offset_product(rows_forward, columns)):
            store_column(plane, at * COLUMNS + a, value)

    for step in range(steps):
        midpoint_pass(plane, other, (phase_real, phase_imag), lanes_forward, lanes_inverse, middle_ref)
        if step < steps - 1:

            @pl.loop(0, outer // COLUMNS, unroll=2)
            def _(at):
                places = [at * COLUMNS + a for a in range(COLUMNS)]
                columns = []
                for a, value in zip(
                    places, offset_product(rows_inverse, [column_of(other, a) for a in places])
                ):
                    blocks = []
                    for block, rows in enumerate(row_blocks(tall)):
                        turn = turn_at(offset_ref, rows)
                        pair = inverse_rows(value, rows, turn)
                        blocks.append(forward_rows(*layer_turn(pair, layer_ref, step, block, a), turn))
                    columns.append(assembled(blocks))
                for a, value in zip(places, offset_product(rows_forward, columns)):
                    store_column(plane, a, value)


def finish_kernel(dest_ref, layer_ref, plane_ref, rows_inverse, offset_ref, *rest):
    out_ref = rest[-1]
    here = plane_ref.shape[3] // BLK
    tall = NH // layer_ref.shape[2]
    step = layer_ref.shape[1] - 1
    columns = offset_product(rows_inverse, [column_of(plane_ref, at) for at in range(here)])
    for at in range(here):
        found = []
        for block, rows in enumerate(row_blocks(tall)):
            pair = inverse_rows(columns[at], rows, turn_at(offset_ref, rows))
            found.append(layer_turn(pair, layer_ref, step, block, dest_ref[0] * here + at))
        for c in range(2):
            biggest = functools.reduce(jnp.maximum, [jnp.abs(part[c]) for pair in found for part in pair])
            code = scale_code(jnp.max(biggest, axis=0, keepdims=True))
            inverse = inverse_scale_of(code)
            row = at * 2 + c
            for block, pair in enumerate(found):
                words = packed(coded(pair[0][c], inverse), coded(pair[1][c], inverse))
                out_ref[pl.ds(block * tall * 2 * here + row, tall, 2 * here), :] = words
            out_ref[pl.ds(HALF * 2 * here + row, 1), :] = code


def result_kernel(freq_ref, code_ref, *rest):
    out_ref = rest[-1]
    per, tall = out_ref.shape[1:3]
    scale = scale_of(code_ref[per * tall :])[None]
    for half in range(2):

        @pl.when(pl.program_id(0) == half)
        def _():
            out_ref[0] = unpacked(code_ref[: per * tall].reshape(per, tall, BLK))[half] * scale


def take_kernel(mine_ref, counts_ref, source_ref, out_ref, sems):
    taken, entries = out_ref.shape[0], source_ref.shape[1]
    bins_here, stride = source_ref.shape[0], source_ref.shape[0] * entries // taken
    copies = []
    for n in range(taken):
        entry, bin_at = n * stride + mine_ref[0], 0
        for b in range(bins_here - 1):
            over = (bin_at == b) & (entry >= counts_ref[b])
            entry = jnp.where(over, entry - counts_ref[b], entry)
            bin_at = jnp.where(over, b + 1, bin_at)
        entry = jnp.minimum(entry, entries - 1)
        copies.append(
            pltpu.make_async_copy(source_ref.at[bin_at, entry], out_ref.at[n], sems.at[n])
        )
        copies[-1].start()
    for copy in copies:
        copy.wait()


def slot_lists(counts_all, targets_all, bins_local, fl, per_device, room):
    offs = counts_all.shape[0] // bins_local
    entries = targets_all.shape[1]
    counts_in = counts_all.reshape(offs, bins_local)
    live = jnp.sum(counts_in, axis=1)
    quarter = jnp.arange(fl, dtype=jnp.int32)
    held = (live[None, :] - quarter[:, None] + fl - 1) // fl
    upto = jnp.sum(
        jnp.where(jnp.arange(offs)[None, :] <= jnp.arange(offs)[:, None], held[:, None, :], 0), axis=2
    )
    at = jnp.arange(room, dtype=jnp.int32)
    past = (at[None, :, None] >= upto[:, None, :]).astype(jnp.int32)
    off_at = jnp.sum(past, axis=2)
    valid = off_at < offs
    off_at = jnp.minimum(off_at, offs - 1)
    start = jnp.sum(past * held[:, None, :], axis=2)
    nth = jnp.clip(at[None, :] - start, 0, per_device - 1)
    entry = nth * fl + quarter[:, None]
    bin_at = off_at * bins_local
    mine = off_at[:, :, None] == jnp.arange(offs)[None, None, :]
    for b in range(bins_local - 1):
        size = jnp.sum(jnp.where(mine, counts_in[None, None, :, b], 0), axis=2)
        over = (bin_at == off_at * bins_local + b) & (entry >= size)
        bin_at = bin_at + over
        entry = entry - jnp.where(over, size, 0)
    flat = bin_at * entries + entry
    total = targets_all.size
    picks = flat[:, :, None] == jnp.arange(total)[None, None, :]
    target = jnp.sum(jnp.where(picks, targets_all.reshape(1, 1, total), 0), axis=2)
    target = jnp.where(valid, target, -1)
    return off_at, nth, bin_at, target


def local(bins_data, operators, targets, counts, layer_index, slowness):
    off_count = lax.axis_size("off")
    mid_count = lax.axis_size("mid")
    bins_local, freq_total, _, mid_local = bins_data.shape
    entries = operators.shape[1]
    bins_total = bins_local * off_count
    fl = freq_total // off_count
    total_mid = mid_local * mid_count
    outer = total_mid // BLK
    mid_at, off_at = lax.axis_index("mid"), lax.axis_index("off")
    assert mid_count % fl == 0 and (bins_local * entries) % fl == 0
    mine = mid_at % fl
    rounds = mid_count // fl
    groups = (
        None if rounds == 1 else [list(range(g * fl, (g + 1) * fl)) for g in range(rounds)]
    )

    per_device = bins_local * entries // fl
    smem = pl.BlockSpec(memory_space=pltpu.SMEM)
    vmem = pl.BlockSpec(memory_space=pltpu.VMEM)
    hbm = pl.BlockSpec(memory_space=pl.ANY)
    own = pl.pallas_call(
        take_kernel,
        in_specs=[smem, smem, hbm],
        out_specs=vmem,
        out_shape=jax.ShapeDtypeStruct((per_device, BLK, BLK), jnp.bfloat16),
        scratch_shapes=[pltpu.SemaphoreType.DMA((per_device,))],
        compiler_params=pltpu.CompilerParams(vmem_limit_bytes=SMALL),
        name="take_own",
    )(mine.reshape(1), counts, operators)
    bins_data, own = lax.optimization_barrier((bins_data, own))
    cores = 2 if off_count % 2 == 0 else 1
    line = off_count // cores
    assert line & (line - 1) == 0 and fl & (fl - 1) == 0
    shares = [own]
    for away in range(1, line):
        low = away & -away
        shares.append(
            lax.ppermute(
                shares[away ^ low],
                "off",
                [(i, (i // cores ^ low) * cores + i % cores) for i in range(off_count)],
            )
        )
    if cores > 1:
        shares += [lax.ppermute(x, "off", [(i, i ^ 1) for i in range(off_count)]) for x in shares]

    pairs = fl * 2

    def extra(whole_numbers, copies):
        flat = whole_numbers.astype(jnp.bfloat16).reshape(1, 1, 1, -1)
        flat = jnp.pad(flat, ((0, 0), (0, 0), (0, pairs - 1), (0, mid_local - flat.shape[3])))
        return jnp.broadcast_to(flat, (1, copies, pairs, mid_local))

    lists = jnp.concatenate([counts[:, None], targets], axis=1)
    data = bins_data.reshape(bins_local, off_count, pairs, mid_local)
    data = jnp.concatenate([data, extra(lists, off_count)], axis=0)
    data = lax.all_to_all(data, "off", split_axis=1, concat_axis=0, tiled=True)

    data = data.reshape(off_count, bins_local + 1, pairs, mid_local)
    lists = data[:, bins_local, 0, : lists.size].astype(jnp.int32).reshape(bins_total, 1 + entries)
    data = data[:, :bins_local].reshape(bins_total, pairs, mid_local)
    data = jnp.concatenate([data, extra(layer_index, 1)[0]], axis=0)
    assert mid_count & (mid_count - 1) == 0
    parts = [data] + [
        lax.ppermute(data, "mid", [(i, i ^ away) for i in range(mid_count)])
        for away in range(mid_count - 1, 0, -1)
    ]
    data = jnp.stack(parts[:1] + parts[:0:-1])
    partner = jnp.arange(mid_count, dtype=jnp.int32) ^ mid_at
    layers = data[:, bins_total, 0, : layer_index.size].astype(jnp.int32)
    layers = jnp.sum(
        jnp.where((partner[:, None] == jnp.arange(mid_count))[:, :, None], layers[None], 0), axis=1
    )
    layers = layers.reshape(mid_count, *layer_index.shape).transpose(1, 2, 0, 3)
    layers = layers.reshape(*layer_index.shape[:2], outer)
    data = data[:, :bins_total].reshape(mid_count, bins_total, pairs, mid_local // BLK, BLK)
    data = data.transpose(1, 2, 0, 3, 4).reshape(bins_total, pairs * outer, BLK)
    order = (partner[:, None] * (mid_local // BLK) + jnp.arange(mid_local // BLK)).reshape(outer)

    live_total = bins_total * entries // 2
    room = -(-(live_total + (fl - 1) * off_count) // fl)
    room = min(-(-room // GROUP) * GROUP, per_device * off_count)
    offs, nth, bins, goal = slot_lists(lists[:, 0], lists[:, 1:], bins_local, fl, per_device, room)
    side = (offs % cores != off_at % cores).astype(jnp.int32) * line
    slots = (side + ((offs // cores) ^ (off_at // cores))) * per_device + nth
    own_slots = lax.dynamic_index_in_dim(slots, mine, 0, False)
    own_bins = lax.dynamic_index_in_dim(bins, mine, 0, False)
    list_groups = room // GROUP
    shape = jax.ShapeDtypeStruct((list_groups, outer + 1, GROUP, BLK), jnp.int32)
    terms = pl.pallas_call(
        functools.partial(contribution_kernel, freqs=fl),
        in_specs=[smem, smem, smem, smem, vmem] + [hbm] * len(shares),
        out_specs=[vmem] * fl,
        out_shape=[shape] * fl,
        scratch_shapes=[
            pltpu.VMEM((fl * 2 * outer * GROUP, BLK), jnp.float32),
            pltpu.VMEM((len(shares) * per_device, BLK, BLK), jnp.bfloat16),
            pltpu.SemaphoreType.DMA((len(shares),)),
        ],
        compiler_params=pltpu.CompilerParams(vmem_limit_bytes=SMALL),
        name="contributions",
    )(mine.reshape(1), order, own_slots, own_bins, data, *shares)
    terms, goal, layers, freq_at = lax.optimization_barrier(
        (terms, goal, layers, off_at * fl + mine)
    )
    got = {0: terms[0]}
    for away in range(fl - 1, 0, -1):
        got[away] = lax.ppermute(terms[away], "mid", [(i, i ^ away) for i in range(mid_count)])
    terms = [got[away] for away in range(fl)]

    source = jnp.arange(fl, dtype=jnp.int32) ^ mine
    goal = jnp.sum(jnp.where((source[:, None] == jnp.arange(fl))[:, :, None], goal[None], 0), axis=1)
    pick = (
        jnp.tile(goal.reshape(1, fl * room), (1, 2))
        == lax.broadcasted_iota(jnp.int32, (NH, 2 * fl * room), 0)
    ).astype(jnp.bfloat16)
    omega = math.pi * (0.1 + 0.8 * (freq_at.astype(jnp.float32) + 0.5) / freq_total)
    phase_real, phase_imag = pl.pallas_call(
        propagator_kernel,
        in_specs=[smem],
        out_specs=[vmem] * 2,
        out_shape=[jax.ShapeDtypeStruct((NH, total_mid), jnp.float32)] * 2,
        compiler_params=pltpu.CompilerParams(vmem_limit_bytes=SMALL),
        cost_estimate=pl.CostEstimate(
            flops=60 * NH * total_mid, bytes_accessed=8 * NH * total_mid, transcendentals=10 * NH * total_mid
        ),
        name="propagator",
    )(omega.reshape(1))

    layer_total = slowness.shape[1]
    chosen = layers[..., None] == jnp.arange(layer_total)
    slow = jnp.sum(jnp.where(chosen, slowness[:, None, None, :], 0.0), axis=-1)
    turn = 2.0 * dz_cells * omega * (slow - 1.0)
    layer_turns = jnp.stack([jnp.cos(turn), jnp.sin(turn)])

    middle, offset_turn = twiddle_tables(outer)
    here = mid_local // BLK
    rows_out = (HALF + 1) * 2 * here
    tables = [jnp.asarray(t) for t in block_tables()]
    middle, offset_turn = jnp.asarray(middle), jnp.asarray(offset_turn)
    plane = pl.pallas_call(
        functools.partial(march_kernel, sources=fl),
        in_specs=[smem] + [vmem] * (fl + 9),
        out_specs=vmem,
        out_shape=jax.ShapeDtypeStruct((2, 2, HALF, total_mid), jnp.float32),
        scratch_shapes=[
            pltpu.VMEM((2, 2, HALF, total_mid), jnp.float32),
            pltpu.VMEM((fl * room, BLK), jnp.float32),
        ],
        compiler_params=pltpu.CompilerParams(vmem_limit_bytes=VMEM),
        name="march",
    )(layer_turns, *terms, pick, phase_real, phase_imag, *tables, middle, offset_turn)

    def finish(dest, *before):
        return pl.pallas_call(
            finish_kernel,
            grid_spec=pltpu.PrefetchScalarGridSpec(
                num_scalar_prefetch=1,
                grid=(1,),
                in_specs=[
                    smem,
                    pl.BlockSpec((2, 2, HALF, mid_local), lambda i, dest: (0, 0, 0, dest[0])),
                    vmem,
                    vmem,
                ]
                + [hbm] * len(before),
                out_specs=pl.BlockSpec((rows_out, BLK), lambda i, dest: (0, 0)),
            ),
            out_shape=jax.ShapeDtypeStruct((rows_out, BLK), jnp.int32),
            cost_estimate=pl.CostEstimate(
                flops=6 * NH * NH * 2 * BLK * here, bytes_accessed=6 * NH * mid_local, transcendentals=0
            ),
            compiler_params=pltpu.CompilerParams(vmem_limit_bytes=SMALL),
            name="finish",
        )(dest.reshape(1), layer_turns, plane, tables[1], offset_turn, *before)

    got, before = {}, []
    for ahead in [*range(fl - 1, 0, -1), 0]:
        dest = (mid_at // fl) * fl + (mine ^ ahead)
        block = finish(dest, *before)
        before = [block]
        if ahead:
            block = lax.ppermute(block, "mid", [(s, s ^ ahead) for s in range(mid_count)])
        got[ahead] = block

    field = None
    for ahead in [0, *range(fl - 1, 0, -1)]:
        freq = mine ^ ahead
        first = field is None
        field = pl.pallas_call(
            result_kernel,
            grid_spec=pltpu.PrefetchScalarGridSpec(
                num_scalar_prefetch=1,
                grid=(2,),
                in_specs=[vmem] if first else [vmem, hbm],
                out_specs=pl.BlockSpec((1, HALF, 2 * here, BLK), lambda i, f: (f[0], i, 0, 0)),
            ),
            out_shape=jax.ShapeDtypeStruct((fl, NH, 2 * here, BLK), jnp.float32),
            input_output_aliases={} if first else {2: 0},
            compiler_params=pltpu.CompilerParams(vmem_limit_bytes=SMALL),
            cost_estimate=pl.CostEstimate(
                flops=4 * NH * mid_local, bytes_accessed=12 * NH * mid_local, transcendentals=0
            ),
            name="result",
        )(freq.reshape(1), got[ahead], *([] if first else [field]))
    field = field.reshape(fl, NH, here, 2, BLK).transpose(0, 1, 3, 2, 4)
    return field.reshape(fl, NH, 2, mid_local)


def solution(mesh):
    in_specs = (
        P("off", None, None, "mid"),
        P("off", None, None, None),
        P("off", None),
        P("off"),
        P(None, None, "mid"),
        P(),
    )
    out_specs = P("off", None, None, "mid")
    return jax.shard_map(local, mesh=mesh, in_specs=in_specs, out_specs=out_specs, check_vma=False)
```

```python
import functools
import math

import jax
import jax.numpy as jnp
import numpy as np
from jax import lax
from jax.experimental import pallas as pl
from jax.experimental.pallas import tpu as pltpu
from jax.sharding import PartitionSpec as P

NH = 256
BLK = 128

dz_cells = 2.0
damping = 0.1

HALF = NH // 2
STEP_LOG = 64.0
TOP = 32767.0
GROUP = 8
ROWS = 8
CHUNKS = 2
VMEM = 28 * 1024 * 1024
SMALL = 10 * 1024 * 1024


def signed_wave(index, length):
    signed = (index + length // 2) % length - length // 2
    return signed.astype(jnp.float32) * (2.0 * math.pi / length)


def root_pair(level):
    magnitude = jnp.sqrt(level * level + damping * damping)
    larger = jnp.sqrt(0.5 * (magnitude + jnp.abs(level)))
    smaller = damping / (2.0 * larger)
    return (jnp.where(level >= 0, larger, smaller), jnp.where(level >= 0, smaller, larger))


def propagator(omega_sq, mid_wave, offset_wave):
    source = 0.5 * (mid_wave - offset_wave)
    receiver = 0.5 * (mid_wave + offset_wave)
    real_s, imag_s = root_pair(omega_sq - source * source)
    real_r, imag_r = root_pair(omega_sq - receiver * receiver)
    decay = jnp.exp(-dz_cells * (imag_s + imag_r))
    turn = dz_cells * (real_s + real_r)
    return (decay * jnp.cos(turn), decay * jnp.sin(turn))


def halves_np(table):
    high = table.astype(np.float32).astype(jnp.bfloat16)
    low = (table - high.astype(np.float64)).astype(np.float32).astype(jnp.bfloat16)
    return high, low


def block_tables():
    index = np.arange(BLK)
    angles = 2.0 * np.pi * (np.outer(index, index) % BLK) / BLK
    cos, sin = np.cos(angles), np.sin(angles)
    upper = np.block([[cos, sin], [-sin, cos]])
    lower = np.block([[cos, -sin], [sin, cos]])
    tables = []
    for axis, pair in ((1, (upper, lower)), (0, (lower, upper))):
        for table in pair:
            high, low = halves_np(table)
            tables.append(np.concatenate([high, high, low], axis=axis))
    return tables


def twiddle_tables(outer):
    ka, b = np.arange(outer)[:, None], np.arange(BLK)[None, :]
    angles = 2.0 * np.pi * ka * b / (outer * BLK)
    middle = np.stack([np.cos(angles), np.sin(angles)]).astype(np.float32)
    rows = 2.0 * np.pi * np.arange(HALF) / NH
    offset = np.stack([np.cos(rows), np.sin(rows)]).astype(np.float32)
    return middle, np.broadcast_to(offset[:, :, None], (2, HALF, BLK)).copy()


def halves(value):
    high = value.astype(jnp.bfloat16)
    return high, (value - high.astype(jnp.float32)).astype(jnp.bfloat16)


def dot(left, right):
    return jnp.dot(left, right, preferred_element_type=jnp.float32)


def aligned(start, size):
    return start if isinstance(start, int) else pl.multiple_of(start, size)


def pipelined(count, *stages):
    first, second, third = stages
    first(0, 0)
    second(0, 0)
    first(1, 1)

    @pl.loop(1, count // 2)
    def _(pair):
        tile = 2 * pair
        third(tile - 2, 0)
        second(tile - 1, 1)
        first(tile, 0)
        third(tile - 1, 1)
        second(tile, 0)
        first(tile + 1, 1)

    third(count - 2, 0)
    second(count - 1, 1)
    third(count - 1, 1)


def keep_rows(ref, value):
    size = value.shape[0]
    ref[:size], ref[size:] = halves(value)


def keep_lanes(ref, value):
    size = value.shape[1]
    ref[:, :size], ref[:, size:] = halves(value)


def left_product(table, ref):
    size = ref.shape[0] // 2
    return dot(table, jnp.concatenate([ref[...], ref[:size]], axis=0))


def right_product(ref, table):
    size = ref.shape[1] // 2
    return dot(jnp.concatenate([ref[...], ref[:, :size]], axis=1), table)


def cmul(real_a, imag_a, real_b, imag_b):
    return real_a * real_b - imag_a * imag_b, real_a * imag_b + imag_a * real_b


def small_transform(values, sign):
    count = len(values)
    if count == 1:
        return values
    even = small_transform(values[0::2], sign)
    odd = small_transform(values[1::2], sign)
    first, second = [], []
    for k in range(count // 2):
        er, ei = even[k]
        xr, xi = odd[k]
        if k == 0:
            tr, ti = xr, xi
        elif 4 * k == count:
            tr, ti = (-xi, xr) if sign > 0 else (xi, -xr)
        else:
            c, s = math.cos(2 * math.pi * k / count), sign * math.sin(2 * math.pi * k / count)
            if 8 * k == count:
                tr, ti = ((xr - xi) * c, (xr + xi) * c) if sign > 0 else ((xr + xi) * c, (xi - xr) * c)
            elif 8 * k == 3 * count:
                tr, ti = ((xr + xi) * c, (xi - xr) * c) if sign > 0 else ((xr - xi) * c, (xr + xi) * c)
            else:
                tr, ti = xr * c - xi * s, xr * s + xi * c
        first.append((er + tr, ei + ti))
        second.append((er - tr, ei - ti))
    return first + second


def scale_code(biggest):
    return (jnp.floor(jnp.log(jnp.maximum(biggest, 1e-30)) * STEP_LOG) + 1.0).astype(jnp.int32)


def scale_of(code):
    return jnp.exp(code.astype(jnp.float32) * (1.0 / STEP_LOG)) * (1.0 / TOP)


def inverse_scale_of(code):
    return jnp.exp(code.astype(jnp.float32) * (-1.0 / STEP_LOG)) * TOP


def coded(value, inverse):
    return jnp.floor(value * inverse + 0.5).astype(jnp.int32)


def packed(high, low):
    return (high << 16) | (low & 0xFFFF)


def unpacked(word):
    return (word >> 16).astype(jnp.float32), ((word << 16) >> 16).astype(jnp.float32)


def contribution_kernel(place_ref, order_ref, slot_ref, bin_ref, data_ref, *rest, freqs):
    *sources, held, weight_ref, sems = rest
    sources, outs = sources[:-freqs], sources[-freqs:]
    groups, outer = outs[0].shape[0], outs[0].shape[1] - 1
    count = sources[0].shape[0]
    copies = [
        pltpu.make_async_copy(ref, weight_ref.at[pl.ds(n * count, count)], sems.at[n])
        for n, ref in enumerate(sources)
    ]
    for copy in copies:
        copy.start()
    for copy in copies:
        copy.wait()

    @pl.loop(0, groups)
    def _(group):
        for at in range(GROUP):
            slot = slot_ref[group * GROUP + at]
            source = bin_ref[group * GROUP + at]
            held[pl.ds(at, data_ref.shape[1], GROUP), :] = dot(data_ref[source], weight_ref[slot])
        for away, out_ref in enumerate(outs):
            base = (place_ref[0] ^ away) * (2 * outer * GROUP)

            def term(at):
                return held[pl.ds(pl.multiple_of(base + at * GROUP, GROUP), GROUP), :]

            biggest = functools.reduce(jnp.maximum, [jnp.abs(term(at)) for at in range(2 * outer)])
            code = scale_code(biggest)
            inverse = inverse_scale_of(code)
            for a in range(outer):
                words = packed(coded(term(a), inverse), coded(term(outer + a), inverse))
                out_ref[group, order_ref[a]] = words
            out_ref[group, outer] = code


def column_of(plane, a):
    lanes = pl.ds(aligned(a * BLK, BLK), BLK)
    return jnp.concatenate(
        [
            jnp.concatenate([plane[p, 0, :, lanes], plane[p, 1, :, lanes]], axis=0)
            for p in range(2)
        ],
        axis=1,
    )


def store_column(plane, a, value):
    lanes = pl.ds(aligned(a * BLK, BLK), BLK)
    for p in range(2):
        for c in range(2):
            plane[p, c, :, lanes] = value[c * HALF : (c + 1) * HALF, p * BLK : (p + 1) * BLK]


def row_blocks(tall):
    return [slice(at * tall, (at + 1) * tall) for at in range(HALF // tall)]


def turn_at(offset_ref, rows):
    return offset_ref[0, rows], offset_ref[1, rows]


def forward_rows(low, high, turn):
    first = low[0] + high[0], low[1] + high[1]
    second = cmul(low[0] - high[0], low[1] - high[1], turn[0], -turn[1])
    return (*first, *second)


def inverse_rows(value, rows, turn):
    upper, below = rows, slice(HALF + rows.start, HALF + rows.stop)
    first = value[upper, :BLK], value[below, :BLK]
    second = cmul(value[upper, BLK:], value[below, BLK:], turn[0], turn[1])
    low = first[0] + second[0], first[1] + second[1]
    high = first[0] - second[0], first[1] - second[1]
    return low, high


def assembled(blocks):
    parts = [jnp.concatenate(part, axis=0) for part in zip(*blocks)]
    return jnp.concatenate(
        [jnp.concatenate(parts[:2], axis=0), jnp.concatenate(parts[2:], axis=0)], axis=1
    )


def propagator_kernel(omega_ref, slow_ref, layers_ref, real_ref, imag_ref, turns_ref):
    steps, layer_total = slow_ref.shape
    for step in range(steps):
        layers = layers_ref[step]
        slow = functools.reduce(
            jnp.add, [jnp.where(layers == n, slow_ref[step, n], 0.0) for n in range(layer_total)]
        )
        turn = 2.0 * dz_cells * omega_ref[0] * (slow - 1.0)
        turns_ref[0, step] = jnp.cos(turn)
        turns_ref[1, step] = jnp.sin(turn)

    total = real_ref.shape[1]
    scale = 1.0 / (NH * total)
    omega_sq = omega_ref[0] * omega_ref[0]

    @pl.loop(0, NH // GROUP)
    def _(at):
        start = pl.multiple_of(at * GROUP, GROUP)
        row = lax.broadcasted_iota(jnp.int32, (GROUP, BLK), 0) + at * GROUP
        lane = lax.broadcasted_iota(jnp.int32, (GROUP, BLK), 1)
        offset_wave = signed_wave(2 * (row % HALF) + row // HALF, NH)
        for a in range(total // BLK):
            mid_wave = signed_wave(a + total // BLK * lane, total)
            real, imag = propagator(omega_sq, mid_wave, offset_wave)
            real_ref[pl.ds(start, GROUP), a * BLK : (a + 1) * BLK] = real * scale
            imag_ref[pl.ds(start, GROUP), a * BLK : (a + 1) * BLK] = imag * scale


def layer_turn(pair, layer_ref, step, block, a):
    half = layer_ref.shape[2] // 2
    return [
        cmul(*part, layer_ref[0, step, block + p * half, a], layer_ref[1, step, block + p * half, a])
        for p, part in enumerate(pair)
    ]


def midpoint_pass(plane, out, phase_refs, forward, inverse, middle_ref, first_kept, second_kept):
    outer = middle_ref.shape[1]
    lanes = [slice(a * BLK, (a + 1) * BLK) for a in range(outer)]
    tall = first_kept[0].shape[0] // outer
    per_half = HALF // tall
    chunks = range(0, tall, ROWS)

    def place(at):
        return at // per_half, (at % per_half) * tall

    def gathered(pieces):
        return jnp.concatenate([jnp.concatenate(pair, axis=1) for pair in pieces], axis=0)

    def forward_stage(at, parity):
        p, base = place(at)
        pieces = []
        for chunk in chunks:
            here = pl.ds(aligned(base + chunk, ROWS), ROWS)
            values = [(plane[p, 0, here, lane], plane[p, 1, here, lane]) for lane in lanes]
            values = small_transform(values, -1)
            for a in range(outer):
                pieces.append(cmul(*values[a], middle_ref[0, a : a + 1], -middle_ref[1, a : a + 1]))
        keep_lanes(first_kept[parity], gathered(pieces))

    def phase_stage(at, parity):
        value = right_product(first_kept[parity], forward[...])
        pieces = []
        for chunk in chunks:
            there = pl.ds(aligned(at * tall + chunk, ROWS), ROWS)
            for a in range(outer):
                row = chunk * outer + a * ROWS
                part = value[row : row + ROWS]
                pieces.append(
                    cmul(
                        part[:, :BLK], part[:, BLK:],
                        phase_refs[0][there, lanes[a]], phase_refs[1][there, lanes[a]],
                    )
                )
        keep_lanes(second_kept[parity], gathered(pieces))

    def inverse_stage(at, parity):
        p, base = place(at)
        value = right_product(second_kept[parity], inverse[...])
        for chunk in chunks:
            here = pl.ds(aligned(base + chunk, ROWS), ROWS)
            values = []
            for a in range(outer):
                row = chunk * outer + a * ROWS
                part = value[row : row + ROWS]
                values.append(
                    cmul(part[:, :BLK], part[:, BLK:], middle_ref[0, a : a + 1], middle_ref[1, a : a + 1])
                )
            values = small_transform(values, 1)
            for a in range(outer):
                out[p, 0, here, lanes[a]] = values[a][0]
                out[p, 1, here, lanes[a]] = values[a][1]

    pipelined(2 * per_half, forward_stage, phase_stage, inverse_stage)


def march_kernel(layer_ref, *rest, sources):
    code_refs, rest = rest[:sources], rest[sources:]
    (
        pick_ref, phase_real, phase_imag, rows_forward, rows_inverse, lanes_forward, lanes_inverse,
        middle_ref, offset_ref, other, plane, scales, *kept,
    ) = rest
    column_first, column_second, row_first, row_second, terms = (kept[n : n + 2] for n in range(0, 10, 2))
    groups = code_refs[0].shape[0]
    outer = middle_ref.shape[1]
    steps = layer_ref.shape[1]
    tall = NH // layer_ref.shape[2]

    def words(a):
        return jnp.concatenate([ref[:, a].reshape(groups * GROUP, BLK) for ref in code_refs], axis=0)

    scales[...] = scale_of(words(outer))

    def decode_stage(a, parity):
        real, imag = unpacked(words(a))
        scale = scales[...]
        keep_rows(terms[parity], jnp.concatenate([real * scale, imag * scale], axis=1))

    def place_stage(a, parity):
        moved = dot(pick_ref[...], terms[parity][...])
        blocks = []
        for rows in row_blocks(tall):
            low, high = moved[rows], moved[HALF + rows.start : HALF + rows.stop]
            blocks.append(
                forward_rows(
                    (low[:, :BLK], low[:, BLK:]), (high[:, :BLK], high[:, BLK:]), turn_at(offset_ref, rows)
                )
            )
        keep_rows(column_second[parity], assembled(blocks))

    def store_stage(a, parity):
        store_column(plane, a, left_product(rows_forward[...], column_second[parity]))

    pipelined(outer, decode_stage, place_stage, store_stage)

    for step in range(steps):
        midpoint_pass(
            plane, other, (phase_real, phase_imag), lanes_forward, lanes_inverse, middle_ref, row_first, row_second
        )
        if step < steps - 1:

            def load_stage(a, parity):
                keep_rows(column_first[parity], column_of(other, a))

            def turn_stage(a, parity):
                value = left_product(rows_inverse[...], column_first[parity])
                blocks = []
                for block, rows in enumerate(row_blocks(tall)):
                    turn = turn_at(offset_ref, rows)
                    pair = inverse_rows(value, rows, turn)
                    blocks.append(forward_rows(*layer_turn(pair, layer_ref, step, block, a), turn))
                keep_rows(column_second[parity], assembled(blocks))

            pipelined(outer, load_stage, turn_stage, store_stage)


def finish_kernel(dest_ref, layer_ref, plane_ref, rows_inverse, offset_ref, *rest):
    out_ref, kept = rest[-2:]
    here = plane_ref.shape[3] // BLK
    tall = NH // layer_ref.shape[2]
    step = layer_ref.shape[1] - 1
    keep_rows(kept, jnp.concatenate([column_of(plane_ref, at) for at in range(here)], axis=1))
    value = left_product(rows_inverse[...], kept)
    columns = [value[:, at * 2 * BLK : (at + 1) * 2 * BLK] for at in range(here)]
    for at in range(here):
        found = []
        for block, rows in enumerate(row_blocks(tall)):
            pair = inverse_rows(columns[at], rows, turn_at(offset_ref, rows))
            found.append(layer_turn(pair, layer_ref, step, block, dest_ref[0] * here + at))
        for c in range(2):
            biggest = functools.reduce(jnp.maximum, [jnp.abs(part[c]) for pair in found for part in pair])
            code = scale_code(jnp.max(biggest, axis=0, keepdims=True))
            inverse = inverse_scale_of(code)
            row = at * 2 + c
            for block, pair in enumerate(found):
                words = packed(coded(pair[0][c], inverse), coded(pair[1][c], inverse))
                out_ref[pl.ds(block * tall * 2 * here + row, tall, 2 * here), :] = words
            out_ref[pl.ds(HALF * 2 * here + row, 1), :] = code


def result_kernel(freq_ref, code_ref, *rest):
    out_ref = rest[-1]
    per, tall = out_ref.shape[1:3]
    scale = scale_of(code_ref[per * tall :])[None]
    for half in range(2):

        @pl.when(pl.program_id(0) == half)
        def _():
            out_ref[0] = unpacked(code_ref[: per * tall].reshape(per, tall, BLK))[half] * scale


def take_kernel(mine_ref, counts_ref, source_ref, out_ref, sems):
    taken, entries = out_ref.shape[0], source_ref.shape[1]
    bins_here, stride = source_ref.shape[0], source_ref.shape[0] * entries // taken
    copies = []
    for n in range(taken):
        entry, bin_at = n * stride + mine_ref[0], 0
        for b in range(bins_here - 1):
            over = (bin_at == b) & (entry >= counts_ref[b])
            entry = jnp.where(over, entry - counts_ref[b], entry)
            bin_at = jnp.where(over, b + 1, bin_at)
        entry = jnp.minimum(entry, entries - 1)
        copies.append(
            pltpu.make_async_copy(source_ref.at[bin_at, entry], out_ref.at[n], sems.at[n])
        )
        copies[-1].start()
    for copy in copies:
        copy.wait()


def slot_lists(counts_all, targets_all, bins_local, fl, per_device, room):
    offs = counts_all.shape[0] // bins_local
    entries = targets_all.shape[1]
    counts_in = counts_all.reshape(offs, bins_local)
    live = jnp.sum(counts_in, axis=1)
    quarter = jnp.arange(fl, dtype=jnp.int32)
    held = (live[None, :] - quarter[:, None] + fl - 1) // fl
    upto = jnp.sum(
        jnp.where(jnp.arange(offs)[None, :] <= jnp.arange(offs)[:, None], held[:, None, :], 0), axis=2
    )
    at = jnp.arange(room, dtype=jnp.int32)
    past = (at[None, :, None] >= upto[:, None, :]).astype(jnp.int32)
    off_at = jnp.sum(past, axis=2)
    valid = off_at < offs
    off_at = jnp.minimum(off_at, offs - 1)
    start = jnp.sum(past * held[:, None, :], axis=2)
    nth = jnp.clip(at[None, :] - start, 0, per_device - 1)
    entry = nth * fl + quarter[:, None]
    bin_at = off_at * bins_local
    mine = off_at[:, :, None] == jnp.arange(offs)[None, None, :]
    for b in range(bins_local - 1):
        size = jnp.sum(jnp.where(mine, counts_in[None, None, :, b], 0), axis=2)
        over = (bin_at == off_at * bins_local + b) & (entry >= size)
        bin_at = bin_at + over
        entry = entry - jnp.where(over, size, 0)
    flat = bin_at * entries + entry
    total = targets_all.size
    picks = flat[:, :, None] == jnp.arange(total)[None, None, :]
    target = jnp.sum(jnp.where(picks, targets_all.reshape(1, 1, total), 0), axis=2)
    target = jnp.where(valid, target, -1)
    return off_at, nth, bin_at, target


def local(bins_data, operators, targets, counts, layer_index, slowness):
    off_count = lax.axis_size("off")
    mid_count = lax.axis_size("mid")
    bins_local, freq_total, _, mid_local = bins_data.shape
    entries = operators.shape[1]
    bins_total = bins_local * off_count
    fl = freq_total // off_count
    total_mid = mid_local * mid_count
    outer = total_mid // BLK
    mid_at, off_at = lax.axis_index("mid"), lax.axis_index("off")
    assert mid_count % fl == 0 and (bins_local * entries) % fl == 0
    mine = mid_at % fl
    rounds = mid_count // fl
    groups = (
        None if rounds == 1 else [list(range(g * fl, (g + 1) * fl)) for g in range(rounds)]
    )

    per_device = bins_local * entries // fl
    smem = pl.BlockSpec(memory_space=pltpu.SMEM)
    vmem = pl.BlockSpec(memory_space=pltpu.VMEM)
    hbm = pl.BlockSpec(memory_space=pl.ANY)
    own = pl.pallas_call(
        take_kernel,
        in_specs=[smem, smem, hbm],
        out_specs=vmem,
        out_shape=jax.ShapeDtypeStruct((per_device, BLK, BLK), jnp.bfloat16),
        scratch_shapes=[pltpu.SemaphoreType.DMA((per_device,))],
        compiler_params=pltpu.CompilerParams(vmem_limit_bytes=SMALL),
        name="take_own",
    )(mine.reshape(1), counts, operators)
    bins_data, own = lax.optimization_barrier((bins_data, own))
    cores = 2 if off_count % 2 == 0 else 1
    line = off_count // cores
    assert line & (line - 1) == 0 and fl & (fl - 1) == 0
    shares = [own]
    for away in range(1, line):
        low = away & -away
        shares.append(
            lax.ppermute(
                shares[away ^ low],
                "off",
                [(i, (i // cores ^ low) * cores + i % cores) for i in range(off_count)],
            )
        )
    if cores > 1:
        shares += [lax.ppermute(x, "off", [(i, i ^ 1) for i in range(off_count)]) for x in shares]

    pairs = fl * 2

    def extra(whole_numbers, copies):
        flat = whole_numbers.astype(jnp.bfloat16).reshape(1, 1, 1, -1)
        flat = jnp.pad(flat, ((0, 0), (0, 0), (0, pairs - 1), (0, mid_local - flat.shape[3])))
        return jnp.broadcast_to(flat, (1, copies, pairs, mid_local))

    lists = jnp.concatenate([counts[:, None], targets], axis=1)
    data = bins_data.reshape(bins_local, off_count, pairs, mid_local)
    data = jnp.concatenate([data, extra(lists, off_count)], axis=0)
    data = lax.all_to_all(data, "off", split_axis=1, concat_axis=0, tiled=True)

    data = data.reshape(off_count, bins_local + 1, pairs, mid_local)
    lists = data[:, bins_local, 0, : lists.size].astype(jnp.int32).reshape(bins_total, 1 + entries)
    data = data[:, :bins_local].reshape(bins_total, pairs, mid_local)
    data = jnp.concatenate([data, extra(layer_index, 1)[0]], axis=0)
    assert mid_count & (mid_count - 1) == 0
    parts = [data] + [
        lax.ppermute(data, "mid", [(i, i ^ away) for i in range(mid_count)])
        for away in range(mid_count - 1, 0, -1)
    ]
    data = jnp.stack(parts[:1] + parts[:0:-1])
    partner = jnp.arange(mid_count, dtype=jnp.int32) ^ mid_at
    layers = data[:, bins_total, 0, : layer_index.size].astype(jnp.int32)
    layers = jnp.sum(
        jnp.where((partner[:, None] == jnp.arange(mid_count))[:, :, None], layers[None], 0), axis=1
    )
    layers = layers.reshape(mid_count, *layer_index.shape).transpose(1, 2, 0, 3)
    layers = layers.reshape(*layer_index.shape[:2], outer)
    data = data[:, :bins_total].reshape(mid_count, bins_total, pairs, mid_local // BLK, BLK)
    data = data.transpose(1, 2, 0, 3, 4).reshape(bins_total, pairs * outer, BLK)
    order = (partner[:, None] * (mid_local // BLK) + jnp.arange(mid_local // BLK)).reshape(outer)

    live_total = bins_total * entries // 2
    room = -(-(live_total + (fl - 1) * off_count) // fl)
    room = min(-(-room // GROUP) * GROUP, per_device * off_count)
    offs, nth, bins, goal = slot_lists(lists[:, 0], lists[:, 1:], bins_local, fl, per_device, room)
    side = (offs % cores != off_at % cores).astype(jnp.int32) * line
    slots = (side + ((offs // cores) ^ (off_at // cores))) * per_device + nth
    source = jnp.arange(fl, dtype=jnp.int32) ^ mine
    goal = jnp.sum(jnp.where((source[:, None] == jnp.arange(fl))[:, :, None], goal[None], 0), axis=1)
    pick = (
        jnp.tile(goal.reshape(1, fl * room), (1, 2))
        == lax.broadcasted_iota(jnp.int32, (NH, 2 * fl * room), 0)
    ).astype(jnp.bfloat16)
    own_slots = lax.dynamic_index_in_dim(slots, mine, 0, False)
    own_bins = lax.dynamic_index_in_dim(bins, mine, 0, False)
    list_groups = room // GROUP
    data, order, own_slots, own_bins, layers, pick = lax.optimization_barrier(
        (data, order, own_slots, own_bins, layers, pick)
    )
    shape = jax.ShapeDtypeStruct((list_groups, outer + 1, GROUP, BLK), jnp.int32)
    terms = pl.pallas_call(
        functools.partial(contribution_kernel, freqs=fl),
        in_specs=[smem, smem, smem, smem, vmem] + [hbm] * len(shares),
        out_specs=[vmem] * fl,
        out_shape=[shape] * fl,
        scratch_shapes=[
            pltpu.VMEM((fl * 2 * outer * GROUP, BLK), jnp.float32),
            pltpu.VMEM((len(shares) * per_device, BLK, BLK), jnp.bfloat16),
            pltpu.SemaphoreType.DMA((len(shares),)),
        ],
        compiler_params=pltpu.CompilerParams(vmem_limit_bytes=SMALL),
        name="contributions",
    )(mine.reshape(1), order, own_slots, own_bins, data, *shares)
    terms, freq_at = lax.optimization_barrier((terms, off_at * fl + mine))
    got = {0: terms[0]}
    for away in range(fl - 1, 0, -1):
        got[away] = lax.ppermute(terms[away], "mid", [(i, i ^ away) for i in range(mid_count)])
    terms = [got[away] for away in range(fl)]

    omega = math.pi * (0.1 + 0.8 * (freq_at.astype(jnp.float32) + 0.5) / freq_total)
    phase_real, phase_imag, layer_turns = pl.pallas_call(
        propagator_kernel,
        in_specs=[smem, smem, vmem],
        out_specs=[vmem] * 3,
        out_shape=[jax.ShapeDtypeStruct((NH, total_mid), jnp.float32)] * 2
        + [jax.ShapeDtypeStruct((2, *layers.shape), jnp.float32)],
        compiler_params=pltpu.CompilerParams(vmem_limit_bytes=SMALL),
        cost_estimate=pl.CostEstimate(
            flops=60 * NH * total_mid, bytes_accessed=8 * NH * total_mid, transcendentals=10 * NH * total_mid
        ),
        name="propagator",
    )(omega.reshape(1), slowness, layers)

    middle, offset_turn = twiddle_tables(outer)
    here = mid_local // BLK
    rows_out = (HALF + 1) * 2 * here
    tables = [jnp.asarray(t) for t in block_tables()]
    middle, offset_turn = jnp.asarray(middle), jnp.asarray(offset_turn)
    plane = pl.pallas_call(
        functools.partial(march_kernel, sources=fl),
        in_specs=[smem] + [vmem] * (fl + 9),
        out_specs=vmem,
        out_shape=jax.ShapeDtypeStruct((2, 2, HALF, total_mid), jnp.float32),
        scratch_shapes=[
            pltpu.VMEM((2, 2, HALF, total_mid), jnp.float32),
            pltpu.VMEM((fl * room, BLK), jnp.float32),
            *[pltpu.VMEM((2 * NH, 2 * BLK), jnp.bfloat16)] * 4,
            *[pltpu.VMEM((ROWS * CHUNKS * outer, 4 * BLK), jnp.bfloat16)] * 4,
            *[pltpu.VMEM((2 * fl * room, 2 * BLK), jnp.bfloat16)] * 2,
        ],
        compiler_params=pltpu.CompilerParams(vmem_limit_bytes=VMEM),
        name="march",
    )(layer_turns, *terms, pick, phase_real, phase_imag, *tables, middle, offset_turn)

    def finish(dest, *before):
        return pl.pallas_call(
            finish_kernel,
            grid_spec=pltpu.PrefetchScalarGridSpec(
                num_scalar_prefetch=1,
                grid=(1,),
                in_specs=[
                    smem,
                    pl.BlockSpec((2, 2, HALF, mid_local), lambda i, dest: (0, 0, 0, dest[0])),
                    vmem,
                    vmem,
                ]
                + [hbm] * len(before),
                out_specs=pl.BlockSpec((rows_out, BLK), lambda i, dest: (0, 0)),
                scratch_shapes=[pltpu.VMEM((2 * NH, 2 * mid_local), jnp.bfloat16)],
            ),
            out_shape=jax.ShapeDtypeStruct((rows_out, BLK), jnp.int32),
            cost_estimate=pl.CostEstimate(
                flops=6 * NH * NH * 2 * BLK * here, bytes_accessed=6 * NH * mid_local, transcendentals=0
            ),
            compiler_params=pltpu.CompilerParams(vmem_limit_bytes=SMALL),
            name="finish",
        )(dest.reshape(1), layer_turns, plane, tables[1], offset_turn, *before)

    got, before = {}, []
    for ahead in [*range(fl - 1, 0, -1), 0]:
        dest = (mid_at // fl) * fl + (mine ^ ahead)
        block = finish(dest, *before)
        before = [block]
        if ahead:
            block = lax.ppermute(block, "mid", [(s, s ^ ahead) for s in range(mid_count)])
        got[ahead] = block

    field = None
    for ahead in [0, *range(fl - 1, 0, -1)]:
        freq = mine ^ ahead
        first = field is None
        field = pl.pallas_call(
            result_kernel,
            grid_spec=pltpu.PrefetchScalarGridSpec(
                num_scalar_prefetch=1,
                grid=(2,),
                in_specs=[vmem] if first else [vmem, hbm],
                out_specs=pl.BlockSpec((1, HALF, 2 * here, BLK), lambda i, f: (f[0], i, 0, 0)),
            ),
            out_shape=jax.ShapeDtypeStruct((fl, NH, 2 * here, BLK), jnp.float32),
            input_output_aliases={} if first else {2: 0},
            compiler_params=pltpu.CompilerParams(vmem_limit_bytes=SMALL),
            cost_estimate=pl.CostEstimate(
                flops=4 * NH * mid_local, bytes_accessed=12 * NH * mid_local, transcendentals=0
            ),
            name="result",
        )(freq.reshape(1), got[ahead], *([] if first else [field]))
    field = field.reshape(fl, NH, here, 2, BLK).transpose(0, 1, 3, 2, 4)
    return field.reshape(fl, NH, 2, mid_local)


def solution(mesh):
    in_specs = (
        P("off", None, None, "mid"),
        P("off", None, None, None),
        P("off", None),
        P("off"),
        P(None, None, "mid"),
        P(),
    )
    out_specs = P("off", None, None, "mid")
    return jax.shard_map(local, mesh=mesh, in_specs=in_specs, out_specs=out_specs, check_vma=False)
```

```python
import functools
import math

import jax
import jax.numpy as jnp
import numpy as np
from jax import lax
from jax.experimental import pallas as pl
from jax.experimental.pallas import tpu as pltpu
from jax.sharding import PartitionSpec as P

NH = 256
BLK = 128

dz_cells = 2.0
damping = 0.1

HALF = NH // 2
STEP_LOG = 64.0
TOP = 32767.0
GROUP = 8
ROWS = 8
CHUNKS = 2
VMEM = 28 * 1024 * 1024
SMALL = 10 * 1024 * 1024


def signed_wave(index, length):
    signed = (index + length // 2) % length - length // 2
    return signed.astype(jnp.float32) * (2.0 * math.pi / length)


def root_pair(level):
    magnitude = jnp.sqrt(level * level + damping * damping)
    larger = jnp.sqrt(0.5 * (magnitude + jnp.abs(level)))
    smaller = damping / (2.0 * larger)
    return (jnp.where(level >= 0, larger, smaller), jnp.where(level >= 0, smaller, larger))


def propagator(omega_sq, mid_wave, offset_wave):
    source = 0.5 * (mid_wave - offset_wave)
    receiver = 0.5 * (mid_wave + offset_wave)
    real_s, imag_s = root_pair(omega_sq - source * source)
    real_r, imag_r = root_pair(omega_sq - receiver * receiver)
    decay = jnp.exp(-dz_cells * (imag_s + imag_r))
    turn = dz_cells * (real_s + real_r)
    return (decay * jnp.cos(turn), decay * jnp.sin(turn))


def halves_np(table):
    high = table.astype(np.float32).astype(jnp.bfloat16)
    low = (table - high.astype(np.float64)).astype(np.float32).astype(jnp.bfloat16)
    return high, low


def block_tables():
    index = np.arange(BLK)
    angles = 2.0 * np.pi * (np.outer(index, index) % BLK) / BLK
    cos, sin = np.cos(angles), np.sin(angles)
    upper = np.block([[cos, sin], [-sin, cos]])
    lower = np.block([[cos, -sin], [sin, cos]])
    tables = []
    for axis, pair in ((1, (upper, lower)), (0, (lower, upper))):
        for table in pair:
            high, low = halves_np(table)
            tables.append(np.concatenate([high, high, low], axis=axis))
    return tables


def twiddle_tables(outer):
    ka, b = np.arange(outer)[:, None], np.arange(BLK)[None, :]
    angles = 2.0 * np.pi * ka * b / (outer * BLK)
    middle = np.stack([np.cos(angles), np.sin(angles)]).astype(np.float32)
    rows = 2.0 * np.pi * np.arange(HALF) / NH
    offset = np.stack([np.cos(rows), np.sin(rows)]).astype(np.float32)
    middle = np.broadcast_to(middle[:, :, None], (2, outer, ROWS, BLK)).copy()
    return middle, np.broadcast_to(offset[:, :, None], (2, HALF, BLK)).copy()


def halves(value):
    high = value.astype(jnp.bfloat16)
    return high, (value - high.astype(jnp.float32)).astype(jnp.bfloat16)


def dot(left, right):
    return jnp.dot(left, right, preferred_element_type=jnp.float32)


def aligned(start, size):
    return start if isinstance(start, int) else pl.multiple_of(start, size)


def pipelined(count, *stages):
    first, second, third = stages
    first(0, 0)
    second(0, 0)
    first(1, 1)

    @pl.loop(1, count // 2)
    def _(pair):
        tile = 2 * pair
        third(tile - 2, 0)
        second(tile - 1, 1)
        first(tile, 0)
        third(tile - 1, 1)
        second(tile, 0)
        first(tile + 1, 1)

    third(count - 2, 0)
    second(count - 1, 1)
    third(count - 1, 1)


def keep_rows(ref, value):
    size = value.shape[0]
    ref[:size], ref[size:] = halves(value)


def keep_lanes(ref, value):
    size = value.shape[1]
    ref[:, :size], ref[:, size:] = halves(value)


def left_product(table, ref):
    size = ref.shape[0] // 2
    return dot(table, jnp.concatenate([ref[...], ref[:size]], axis=0))


def right_product(ref, table):
    size = ref.shape[1] // 2
    return dot(jnp.concatenate([ref[...], ref[:, :size]], axis=1), table)


def cmul(real_a, imag_a, real_b, imag_b):
    return real_a * real_b - imag_a * imag_b, real_a * imag_b + imag_a * real_b


def cmul_conj(real_a, imag_a, real_b, imag_b):
    return real_a * real_b + imag_a * imag_b, imag_a * real_b - real_a * imag_b


def small_transform(values, sign):
    count = len(values)
    if count == 1:
        return values
    even = small_transform(values[0::2], sign)
    odd = small_transform(values[1::2], sign)
    first, second = [], []
    for k in range(count // 2):
        er, ei = even[k]
        xr, xi = odd[k]
        if k == 0:
            tr, ti = xr, xi
        elif 4 * k == count:
            tr, ti = (-xi, xr) if sign > 0 else (xi, -xr)
        else:
            c, s = math.cos(2 * math.pi * k / count), sign * math.sin(2 * math.pi * k / count)
            if 8 * k == count:
                tr, ti = ((xr - xi) * c, (xr + xi) * c) if sign > 0 else ((xr + xi) * c, (xi - xr) * c)
            elif 8 * k == 3 * count:
                tr, ti = ((xr + xi) * c, (xi - xr) * c) if sign > 0 else ((xr - xi) * c, (xr + xi) * c)
            else:
                tr, ti = xr * c - xi * s, xr * s + xi * c
        first.append((er + tr, ei + ti))
        second.append((er - tr, ei - ti))
    return first + second


def scale_code(biggest):
    return (jnp.floor(jnp.log(jnp.maximum(biggest, 1e-30)) * STEP_LOG) + 1.0).astype(jnp.int32)


def scale_of(code):
    return jnp.exp(code.astype(jnp.float32) * (1.0 / STEP_LOG)) * (1.0 / TOP)


def inverse_scale_of(code):
    return jnp.exp(code.astype(jnp.float32) * (-1.0 / STEP_LOG)) * TOP


def coded(value, inverse):
    return jnp.floor(value * inverse + 0.5).astype(jnp.int32)


def packed(high, low):
    return (high << 16) | (low & 0xFFFF)


def unpacked(word):
    return (word >> 16).astype(jnp.float32), ((word << 16) >> 16).astype(jnp.float32)


def contribution_kernel(place_ref, order_ref, slot_ref, bin_ref, data_ref, *rest, freqs):
    *sources, held, weight_ref, sems = rest
    sources, outs = sources[:-freqs], sources[-freqs:]
    groups, outer = outs[0].shape[0], outs[0].shape[1] - 1
    count = sources[0].shape[0]
    copies = [
        pltpu.make_async_copy(ref, weight_ref.at[pl.ds(n * count, count)], sems.at[n])
        for n, ref in enumerate(sources)
    ]
    for copy in copies:
        copy.start()
    for copy in copies:
        copy.wait()

    @pl.loop(0, groups)
    def _(group):
        for at in range(GROUP):
            slot = slot_ref[group * GROUP + at]
            source = bin_ref[group * GROUP + at]
            held[pl.ds(at, data_ref.shape[1], GROUP), :] = dot(data_ref[source], weight_ref[slot])
        for away, out_ref in enumerate(outs):
            base = (place_ref[0] ^ away) * (2 * outer * GROUP)

            def term(at):
                return held[pl.ds(pl.multiple_of(base + at * GROUP, GROUP), GROUP), :]

            biggest = functools.reduce(jnp.maximum, [jnp.abs(term(at)) for at in range(2 * outer)])
            code = scale_code(biggest)
            inverse = inverse_scale_of(code)
            for a in range(outer):
                words = packed(coded(term(a), inverse), coded(term(outer + a), inverse))
                out_ref[group, order_ref[a]] = words
            out_ref[group, outer] = code


def column_of(plane, a):
    lanes = pl.ds(aligned(a * BLK, BLK), BLK)
    return jnp.concatenate(
        [
            jnp.concatenate([plane[p, 0, :, lanes], plane[p, 1, :, lanes]], axis=0)
            for p in range(2)
        ],
        axis=1,
    )


def store_column(plane, a, value):
    lanes = pl.ds(aligned(a * BLK, BLK), BLK)
    for p in range(2):
        for c in range(2):
            plane[p, c, :, lanes] = value[c * HALF : (c + 1) * HALF, p * BLK : (p + 1) * BLK]


def row_blocks(tall):
    return [slice(at * tall, (at + 1) * tall) for at in range(HALF // tall)]


def turn_at(offset_ref, rows):
    return offset_ref[0, rows], offset_ref[1, rows]


def forward_rows(low, high, turn):
    first = low[0] + high[0], low[1] + high[1]
    second = cmul_conj(low[0] - high[0], low[1] - high[1], *turn)
    return (*first, *second)


def inverse_rows(value, rows, turn):
    upper, below = rows, slice(HALF + rows.start, HALF + rows.stop)
    first = value[upper, :BLK], value[below, :BLK]
    second = cmul(value[upper, BLK:], value[below, BLK:], turn[0], turn[1])
    low = first[0] + second[0], first[1] + second[1]
    high = first[0] - second[0], first[1] - second[1]
    return low, high


def assembled(blocks):
    parts = [jnp.concatenate(part, axis=0) for part in zip(*blocks)]
    return jnp.concatenate(
        [jnp.concatenate(parts[:2], axis=0), jnp.concatenate(parts[2:], axis=0)], axis=1
    )


def propagator_kernel(omega_ref, slow_ref, layers_ref, real_ref, imag_ref, turns_ref):
    steps, layer_total = slow_ref.shape
    for step in range(steps):
        layers = layers_ref[step]
        slow = functools.reduce(
            jnp.add, [jnp.where(layers == n, slow_ref[step, n], 0.0) for n in range(layer_total)]
        )
        turn = 2.0 * dz_cells * omega_ref[0] * (slow - 1.0)
        turns_ref[0, step] = jnp.cos(turn)
        turns_ref[1, step] = jnp.sin(turn)

    total = real_ref.shape[1]
    scale = 1.0 / (NH * total)
    omega_sq = omega_ref[0] * omega_ref[0]

    @pl.loop(0, NH // GROUP)
    def _(at):
        start = pl.multiple_of(at * GROUP, GROUP)
        row = lax.broadcasted_iota(jnp.int32, (GROUP, BLK), 0) + at * GROUP
        lane = lax.broadcasted_iota(jnp.int32, (GROUP, BLK), 1)
        offset_wave = signed_wave(2 * (row % HALF) + row // HALF, NH)
        for a in range(total // BLK):
            mid_wave = signed_wave(a + total // BLK * lane, total)
            real, imag = propagator(omega_sq, mid_wave, offset_wave)
            real_ref[pl.ds(start, GROUP), a * BLK : (a + 1) * BLK] = real * scale
            imag_ref[pl.ds(start, GROUP), a * BLK : (a + 1) * BLK] = imag * scale


def layer_turn(pair, layer_ref, step, block, a):
    half = layer_ref.shape[2] // 2
    return [
        cmul(*part, layer_ref[0, step, block + p * half, a], layer_ref[1, step, block + p * half, a])
        for p, part in enumerate(pair)
    ]


def midpoint_pass(plane, out, phase_refs, forward, inverse, middle_ref, first_kept, second_kept):
    outer = middle_ref.shape[1]
    lanes = [slice(a * BLK, (a + 1) * BLK) for a in range(outer)]
    tall = first_kept[0].shape[0] // outer
    per_half = HALF // tall
    chunks = range(0, tall, ROWS)

    def place(at):
        return at // per_half, (at % per_half) * tall

    def gathered(pieces):
        return jnp.concatenate([jnp.concatenate(pair, axis=1) for pair in pieces], axis=0)

    def forward_stage(at, parity):
        p, base = place(at)
        pieces = []
        for chunk in chunks:
            here = pl.ds(aligned(base + chunk, ROWS), ROWS)
            values = [(plane[p, 0, here, lane], plane[p, 1, here, lane]) for lane in lanes]
            values = small_transform(values, -1)
            for a in range(outer):
                pieces.append(cmul_conj(*values[a], middle_ref[0, a], middle_ref[1, a]))
        keep_lanes(first_kept[parity], gathered(pieces))

    def phase_stage(at, parity):
        value = right_product(first_kept[parity], forward[...])
        pieces = []
        for chunk in chunks:
            there = pl.ds(aligned(at * tall + chunk, ROWS), ROWS)
            for a in range(outer):
                row = chunk * outer + a * ROWS
                part = value[row : row + ROWS]
                pieces.append(
                    cmul(
                        part[:, :BLK], part[:, BLK:],
                        phase_refs[0][there, lanes[a]], phase_refs[1][there, lanes[a]],
                    )
                )
        keep_lanes(second_kept[parity], gathered(pieces))

    def inverse_stage(at, parity):
        p, base = place(at)
        value = right_product(second_kept[parity], inverse[...])
        for chunk in chunks:
            here = pl.ds(aligned(base + chunk, ROWS), ROWS)
            values = []
            for a in range(outer):
                row = chunk * outer + a * ROWS
                part = value[row : row + ROWS]
                values.append(
                    cmul(part[:, :BLK], part[:, BLK:], middle_ref[0, a], middle_ref[1, a])
                )
            values = small_transform(values, 1)
            for a in range(outer):
                out[p, 0, here, lanes[a]] = values[a][0]
                out[p, 1, here, lanes[a]] = values[a][1]

    pipelined(2 * per_half, forward_stage, phase_stage, inverse_stage)


def march_kernel(layer_ref, *rest, sources):
    code_refs, rest = rest[:sources], rest[sources:]
    (
        pick_ref, phase_real, phase_imag, rows_forward, rows_inverse, lanes_forward, lanes_inverse,
        middle_ref, offset_ref, other, plane, scales, *kept,
    ) = rest
    column_first, column_second, row_first, row_second, terms = (kept[n : n + 2] for n in range(0, 10, 2))
    groups = code_refs[0].shape[0]
    outer = middle_ref.shape[1]
    steps = layer_ref.shape[1]
    tall = NH // layer_ref.shape[2]

    def words(a):
        return jnp.concatenate([ref[:, a].reshape(groups * GROUP, BLK) for ref in code_refs], axis=0)

    scales[...] = scale_of(words(outer))

    def decode_stage(a, parity):
        real, imag = unpacked(words(a))
        scale = scales[...]
        keep_rows(terms[parity], jnp.concatenate([real * scale, imag * scale], axis=1))

    def place_stage(a, parity):
        moved = dot(pick_ref[...], terms[parity][...])
        blocks = []
        for rows in row_blocks(tall):
            low, high = moved[rows], moved[HALF + rows.start : HALF + rows.stop]
            blocks.append(
                forward_rows(
                    (low[:, :BLK], low[:, BLK:]), (high[:, :BLK], high[:, BLK:]), turn_at(offset_ref, rows)
                )
            )
        keep_rows(column_second[parity], assembled(blocks))

    def store_stage(a, parity):
        store_column(plane, a, left_product(rows_forward[...], column_second[parity]))

    pipelined(outer, decode_stage, place_stage, store_stage)

    for step in range(steps):
        midpoint_pass(
            plane, other, (phase_real, phase_imag), lanes_forward, lanes_inverse, middle_ref, row_first, row_second
        )
        if step < steps - 1:

            def load_stage(a, parity):
                keep_rows(column_first[parity], column_of(other, a))

            def turn_stage(a, parity):
                value = left_product(rows_inverse[...], column_first[parity])
                blocks = []
                for block, rows in enumerate(row_blocks(tall)):
                    turn = turn_at(offset_ref, rows)
                    pair = inverse_rows(value, rows, turn)
                    blocks.append(forward_rows(*layer_turn(pair, layer_ref, step, block, a), turn))
                keep_rows(column_second[parity], assembled(blocks))

            pipelined(outer, load_stage, turn_stage, store_stage)


def finish_kernel(dest_ref, layer_ref, plane_ref, rows_inverse, offset_ref, *rest):
    out_ref, kept = rest[-2:]
    here = plane_ref.shape[3] // BLK
    tall = NH // layer_ref.shape[2]
    step = layer_ref.shape[1] - 1
    keep_rows(kept, jnp.concatenate([column_of(plane_ref, at) for at in range(here)], axis=1))
    value = left_product(rows_inverse[...], kept)
    columns = [value[:, at * 2 * BLK : (at + 1) * 2 * BLK] for at in range(here)]
    for at in range(here):
        found = []
        for block, rows in enumerate(row_blocks(tall)):
            pair = inverse_rows(columns[at], rows, turn_at(offset_ref, rows))
            found.append(layer_turn(pair, layer_ref, step, block, dest_ref[0] * here + at))
        for c in range(2):
            biggest = functools.reduce(jnp.maximum, [jnp.abs(part[c]) for pair in found for part in pair])
            code = scale_code(jnp.max(biggest, axis=0, keepdims=True))
            inverse = inverse_scale_of(code)
            row = at * 2 + c
            for block, pair in enumerate(found):
                words = packed(coded(pair[0][c], inverse), coded(pair[1][c], inverse))
                out_ref[pl.ds(block * tall * 2 * here + row, tall, 2 * here), :] = words
            out_ref[pl.ds(HALF * 2 * here + row, 1), :] = code


def result_kernel(freq_ref, code_ref, *rest):
    out_ref = rest[-1]
    per, tall = out_ref.shape[1:3]
    scale = scale_of(code_ref[per * tall :])[None]
    for half in range(2):

        @pl.when(pl.program_id(0) == half)
        def _():
            out_ref[0] = unpacked(code_ref[: per * tall].reshape(per, tall, BLK))[half] * scale


def take_kernel(mine_ref, counts_ref, source_ref, out_ref, sems):
    taken, entries = out_ref.shape[0], source_ref.shape[1]
    bins_here, stride = source_ref.shape[0], source_ref.shape[0] * entries // taken
    copies = []
    for n in range(taken):
        entry, bin_at = n * stride + mine_ref[0], 0
        for b in range(bins_here - 1):
            over = (bin_at == b) & (entry >= counts_ref[b])
            entry = jnp.where(over, entry - counts_ref[b], entry)
            bin_at = jnp.where(over, b + 1, bin_at)
        entry = jnp.minimum(entry, entries - 1)
        copies.append(
            pltpu.make_async_copy(source_ref.at[bin_at, entry], out_ref.at[n], sems.at[n])
        )
        copies[-1].start()
    for copy in copies:
        copy.wait()


def slot_lists(counts_all, targets_all, bins_local, fl, per_device, room):
    offs = counts_all.shape[0] // bins_local
    entries = targets_all.shape[1]
    counts_in = counts_all.reshape(offs, bins_local)
    live = jnp.sum(counts_in, axis=1)
    quarter = jnp.arange(fl, dtype=jnp.int32)
    held = (live[None, :] - quarter[:, None] + fl - 1) // fl
    upto = jnp.sum(
        jnp.where(jnp.arange(offs)[None, :] <= jnp.arange(offs)[:, None], held[:, None, :], 0), axis=2
    )
    at = jnp.arange(room, dtype=jnp.int32)
    past = (at[None, :, None] >= upto[:, None, :]).astype(jnp.int32)
    off_at = jnp.sum(past, axis=2)
    valid = off_at < offs
    off_at = jnp.minimum(off_at, offs - 1)
    start = jnp.sum(past * held[:, None, :], axis=2)
    nth = jnp.clip(at[None, :] - start, 0, per_device - 1)
    entry = nth * fl + quarter[:, None]
    bin_at = off_at * bins_local
    mine = off_at[:, :, None] == jnp.arange(offs)[None, None, :]
    for b in range(bins_local - 1):
        size = jnp.sum(jnp.where(mine, counts_in[None, None, :, b], 0), axis=2)
        over = (bin_at == off_at * bins_local + b) & (entry >= size)
        bin_at = bin_at + over
        entry = entry - jnp.where(over, size, 0)
    flat = bin_at * entries + entry
    total = targets_all.size
    picks = flat[:, :, None] == jnp.arange(total)[None, None, :]
    target = jnp.sum(jnp.where(picks, targets_all.reshape(1, 1, total), 0), axis=2)
    target = jnp.where(valid, target, -1)
    return off_at, nth, bin_at, target


def local(bins_data, operators, targets, counts, layer_index, slowness):
    off_count = lax.axis_size("off")
    mid_count = lax.axis_size("mid")
    bins_local, freq_total, _, mid_local = bins_data.shape
    entries = operators.shape[1]
    bins_total = bins_local * off_count
    fl = freq_total // off_count
    total_mid = mid_local * mid_count
    outer = total_mid // BLK
    mid_at, off_at = lax.axis_index("mid"), lax.axis_index("off")
    assert mid_count % fl == 0 and (bins_local * entries) % fl == 0
    mine = mid_at % fl
    rounds = mid_count // fl
    groups = (
        None if rounds == 1 else [list(range(g * fl, (g + 1) * fl)) for g in range(rounds)]
    )

    per_device = bins_local * entries // fl
    smem = pl.BlockSpec(memory_space=pltpu.SMEM)
    vmem = pl.BlockSpec(memory_space=pltpu.VMEM)
    hbm = pl.BlockSpec(memory_space=pl.ANY)
    pairs = fl * 2

    def extra(whole_numbers, copies):
        flat = whole_numbers.astype(jnp.bfloat16).reshape(1, 1, 1, -1)
        flat = jnp.pad(flat, ((0, 0), (0, 0), (0, pairs - 1), (0, mid_local - flat.shape[3])))
        return jnp.broadcast_to(flat, (1, copies, pairs, mid_local))

    lists = lax.optimization_barrier(jnp.concatenate([counts[:, None], targets], axis=1))
    data = bins_data.reshape(bins_local, off_count, pairs, mid_local)
    data = jnp.concatenate([data, extra(lists, off_count)], axis=0)
    data, operators = lax.optimization_barrier((data, operators))
    data = lax.all_to_all(data, "off", split_axis=1, concat_axis=0, tiled=True)

    own = pl.pallas_call(
        take_kernel,
        in_specs=[smem, smem, hbm],
        out_specs=vmem,
        out_shape=jax.ShapeDtypeStruct((per_device, BLK, BLK), jnp.bfloat16),
        scratch_shapes=[pltpu.SemaphoreType.DMA((per_device,))],
        compiler_params=pltpu.CompilerParams(vmem_limit_bytes=SMALL),
        name="take_own",
    )(mine.reshape(1), counts, operators)
    cores = 2 if off_count % 2 == 0 else 1
    line = off_count // cores
    assert line & (line - 1) == 0 and fl & (fl - 1) == 0
    shares = [own]
    for away in range(1, line):
        low = away & -away
        shares.append(
            lax.ppermute(
                shares[away ^ low],
                "off",
                [(i, (i // cores ^ low) * cores + i % cores) for i in range(off_count)],
            )
        )
    if cores > 1:
        shares += [lax.ppermute(x, "off", [(i, i ^ 1) for i in range(off_count)]) for x in shares]


    data = data.reshape(off_count, bins_local + 1, pairs, mid_local)
    lists = data[:, bins_local, 0, : lists.size].astype(jnp.int32).reshape(bins_total, 1 + entries)
    data = data[:, :bins_local].reshape(bins_total, pairs, mid_local)
    data = jnp.concatenate([data, extra(layer_index, 1)[0]], axis=0)
    assert mid_count & (mid_count - 1) == 0
    parts = [data] + [
        lax.ppermute(data, "mid", [(i, i ^ away) for i in range(mid_count)])
        for away in range(mid_count - 1, 0, -1)
    ]
    data = jnp.stack(parts[:1] + parts[:0:-1])
    partner = jnp.arange(mid_count, dtype=jnp.int32) ^ mid_at
    layers = data[:, bins_total, 0, : layer_index.size].astype(jnp.int32)
    layers = jnp.sum(
        jnp.where((partner[:, None] == jnp.arange(mid_count))[:, :, None], layers[None], 0), axis=1
    )
    layers = layers.reshape(mid_count, *layer_index.shape).transpose(1, 2, 0, 3)
    layers = layers.reshape(*layer_index.shape[:2], outer)
    data = data[:, :bins_total].reshape(mid_count, bins_total, pairs, mid_local // BLK, BLK)
    data = data.transpose(1, 2, 0, 3, 4).reshape(bins_total, pairs * outer, BLK)
    order = (partner[:, None] * (mid_local // BLK) + jnp.arange(mid_local // BLK)).reshape(outer)

    live_total = bins_total * entries // 2
    room = -(-(live_total + (fl - 1) * off_count) // fl)
    room = min(-(-room // GROUP) * GROUP, per_device * off_count)
    offs, nth, bins, goal = slot_lists(lists[:, 0], lists[:, 1:], bins_local, fl, per_device, room)
    side = (offs % cores != off_at % cores).astype(jnp.int32) * line
    slots = (side + ((offs // cores) ^ (off_at // cores))) * per_device + nth
    source = jnp.arange(fl, dtype=jnp.int32) ^ mine
    goal = jnp.sum(jnp.where((source[:, None] == jnp.arange(fl))[:, :, None], goal[None], 0), axis=1)
    pick = (
        jnp.tile(goal.reshape(1, fl * room), (1, 2))
        == lax.broadcasted_iota(jnp.int32, (NH, 2 * fl * room), 0)
    ).astype(jnp.bfloat16)
    own_slots = lax.dynamic_index_in_dim(slots, mine, 0, False)
    own_bins = lax.dynamic_index_in_dim(bins, mine, 0, False)
    list_groups = room // GROUP
    data, order, own_slots, own_bins, layers, pick = lax.optimization_barrier(
        (data, order, own_slots, own_bins, layers, pick)
    )
    shape = jax.ShapeDtypeStruct((list_groups, outer + 1, GROUP, BLK), jnp.int32)
    terms = pl.pallas_call(
        functools.partial(contribution_kernel, freqs=fl),
        in_specs=[smem, smem, smem, smem, vmem] + [hbm] * len(shares),
        out_specs=[vmem] * fl,
        out_shape=[shape] * fl,
        scratch_shapes=[
            pltpu.VMEM((fl * 2 * outer * GROUP, BLK), jnp.float32),
            pltpu.VMEM((len(shares) * per_device, BLK, BLK), jnp.bfloat16),
            pltpu.SemaphoreType.DMA((len(shares),)),
        ],
        compiler_params=pltpu.CompilerParams(vmem_limit_bytes=SMALL),
        name="contributions",
    )(mine.reshape(1), order, own_slots, own_bins, data, *shares)
    terms, freq_at = lax.optimization_barrier((terms, off_at * fl + mine))
    got = {0: terms[0]}
    for away in range(fl - 1, 0, -1):
        got[away] = lax.ppermute(terms[away], "mid", [(i, i ^ away) for i in range(mid_count)])
    terms = [got[away] for away in range(fl)]

    omega = math.pi * (0.1 + 0.8 * (freq_at.astype(jnp.float32) + 0.5) / freq_total)
    phase_real, phase_imag, layer_turns = pl.pallas_call(
        propagator_kernel,
        in_specs=[smem, smem, vmem],
        out_specs=[vmem] * 3,
        out_shape=[jax.ShapeDtypeStruct((NH, total_mid), jnp.float32)] * 2
        + [jax.ShapeDtypeStruct((2, *layers.shape), jnp.float32)],
        compiler_params=pltpu.CompilerParams(vmem_limit_bytes=SMALL),
        cost_estimate=pl.CostEstimate(
            flops=60 * NH * total_mid, bytes_accessed=8 * NH * total_mid, transcendentals=10 * NH * total_mid
        ),
        name="propagator",
    )(omega.reshape(1), slowness, layers)

    middle, offset_turn = twiddle_tables(outer)
    here = mid_local // BLK
    rows_out = (HALF + 1) * 2 * here
    tables = [jnp.asarray(t) for t in block_tables()]
    middle, offset_turn = jnp.asarray(middle), jnp.asarray(offset_turn)
    plane = pl.pallas_call(
        functools.partial(march_kernel, sources=fl),
        in_specs=[smem] + [vmem] * (fl + 9),
        out_specs=vmem,
        out_shape=jax.ShapeDtypeStruct((2, 2, HALF, total_mid), jnp.float32),
        scratch_shapes=[
            pltpu.VMEM((2, 2, HALF, total_mid), jnp.float32),
            pltpu.VMEM((fl * room, BLK), jnp.float32),
            *[pltpu.VMEM((2 * NH, 2 * BLK), jnp.bfloat16)] * 4,
            *[pltpu.VMEM((ROWS * CHUNKS * outer, 4 * BLK), jnp.bfloat16)] * 4,
            *[pltpu.VMEM((2 * fl * room, 2 * BLK), jnp.bfloat16)] * 2,
        ],
        compiler_params=pltpu.CompilerParams(vmem_limit_bytes=VMEM),
        name="march",
    )(layer_turns, *terms, pick, phase_real, phase_imag, *tables, middle, offset_turn)

    def finish(dest, *before):
        return pl.pallas_call(
            finish_kernel,
            grid_spec=pltpu.PrefetchScalarGridSpec(
                num_scalar_prefetch=1,
                grid=(1,),
                in_specs=[
                    smem,
                    pl.BlockSpec((2, 2, HALF, mid_local), lambda i, dest: (0, 0, 0, dest[0])),
                    vmem,
                    vmem,
                ]
                + [hbm] * len(before),
                out_specs=pl.BlockSpec((rows_out, BLK), lambda i, dest: (0, 0)),
                scratch_shapes=[pltpu.VMEM((2 * NH, 2 * mid_local), jnp.bfloat16)],
            ),
            out_shape=jax.ShapeDtypeStruct((rows_out, BLK), jnp.int32),
            cost_estimate=pl.CostEstimate(
                flops=6 * NH * NH * 2 * BLK * here, bytes_accessed=6 * NH * mid_local, transcendentals=0
            ),
            compiler_params=pltpu.CompilerParams(vmem_limit_bytes=SMALL),
            name="finish",
        )(dest.reshape(1), layer_turns, plane, tables[1], offset_turn, *before)

    got, before = {}, []
    for ahead in [*range(fl - 1, 0, -1), 0]:
        dest = (mid_at // fl) * fl + (mine ^ ahead)
        block = finish(dest, *before)
        before = [block]
        if ahead:
            block = lax.ppermute(block, "mid", [(s, s ^ ahead) for s in range(mid_count)])
        got[ahead] = block

    field = None
    for ahead in [0, *range(fl - 1, 0, -1)]:
        freq = mine ^ ahead
        first = field is None
        field = pl.pallas_call(
            result_kernel,
            grid_spec=pltpu.PrefetchScalarGridSpec(
                num_scalar_prefetch=1,
                grid=(2,),
                in_specs=[vmem] if first else [vmem, hbm],
                out_specs=pl.BlockSpec((1, HALF, 2 * here, BLK), lambda i, f: (f[0], i, 0, 0)),
            ),
            out_shape=jax.ShapeDtypeStruct((fl, NH, 2 * here, BLK), jnp.float32),
            input_output_aliases={} if first else {2: 0},
            compiler_params=pltpu.CompilerParams(vmem_limit_bytes=SMALL),
            cost_estimate=pl.CostEstimate(
                flops=4 * NH * mid_local, bytes_accessed=12 * NH * mid_local, transcendentals=0
            ),
            name="result",
        )(freq.reshape(1), got[ahead], *([] if first else [field]))
    field = field.reshape(fl, NH, here, 2, BLK).transpose(0, 1, 3, 2, 4)
    return field.reshape(fl, NH, 2, mid_local)


def solution(mesh):
    in_specs = (
        P("off", None, None, "mid"),
        P("off", None, None, None),
        P("off", None),
        P("off"),
        P(None, None, "mid"),
        P(),
    )
    out_specs = P("off", None, None, "mid")
    return jax.shard_map(local, mesh=mesh, in_specs=in_specs, out_specs=out_specs, check_vma=False)
```

```python
import functools
import math

import jax
import jax.numpy as jnp
import numpy as np
from jax import lax
from jax.experimental import pallas as pl
from jax.experimental.pallas import tpu as pltpu
from jax.sharding import PartitionSpec as P

NH = 256
BLK = 128

dz_cells = 2.0
damping = 0.1

HALF = NH // 2
RADIX = 8
TALL = NH // RADIX
STEP_LOG = 64.0
TOP = 32767.0
GROUP = 8
ROWS = 8
CHUNKS = 2
VMEM = 28 * 1024 * 1024
SMALL = 10 * 1024 * 1024


def signed_wave(index, length):
    signed = (index + length // 2) % length - length // 2
    return signed.astype(jnp.float32) * (2.0 * math.pi / length)


def root_pair(level):
    magnitude = jnp.sqrt(level * level + damping * damping)
    larger = jnp.sqrt(0.5 * (magnitude + jnp.abs(level)))
    smaller = damping / (2.0 * larger)
    return (jnp.where(level >= 0, larger, smaller), jnp.where(level >= 0, smaller, larger))


def propagator(omega_sq, mid_wave, offset_wave):
    source = 0.5 * (mid_wave - offset_wave)
    receiver = 0.5 * (mid_wave + offset_wave)
    real_s, imag_s = root_pair(omega_sq - source * source)
    real_r, imag_r = root_pair(omega_sq - receiver * receiver)
    decay = jnp.exp(-dz_cells * (imag_s + imag_r))
    turn = dz_cells * (real_s + real_r)
    return (decay * jnp.cos(turn), decay * jnp.sin(turn))


def halves_np(table):
    high = table.astype(np.float32).astype(jnp.bfloat16)
    low = (table - high.astype(np.float64)).astype(np.float32).astype(jnp.bfloat16)
    return high, low


def block_tables():
    tables = []
    for axis, size in ((1, TALL), (0, BLK)):
        index = np.arange(size)
        angles = 2.0 * np.pi * (np.outer(index, index) % size) / size
        cos, sin = np.cos(angles), np.sin(angles)
        upper = np.block([[cos, sin], [-sin, cos]])
        lower = np.block([[cos, -sin], [sin, cos]])
        for table in (upper, lower) if axis == 1 else (lower, upper):
            high, low = halves_np(table)
            tables.append(np.concatenate([high, high, low], axis=axis))
    return tables


def twiddle_tables(outer):
    ka, b = np.arange(outer)[:, None], np.arange(BLK)[None, :]
    angles = 2.0 * np.pi * ka * b / (outer * BLK)
    middle = np.stack([np.cos(angles), np.sin(angles)]).astype(np.float32)
    rows = 2.0 * np.pi * np.outer(np.arange(RADIX), np.arange(TALL)) / NH
    offset = np.stack([np.cos(rows), np.sin(rows)]).astype(np.float32)
    middle = np.broadcast_to(middle[:, :, None], (2, outer, ROWS, BLK)).copy()
    return middle, np.broadcast_to(offset[..., None], (2, RADIX, TALL, BLK)).copy()


def halves(value):
    high = value.astype(jnp.bfloat16)
    return high, (value - high.astype(jnp.float32)).astype(jnp.bfloat16)


def dot(left, right):
    return jnp.dot(left, right, preferred_element_type=jnp.float32)


def aligned(start, size):
    return start if isinstance(start, int) else pl.multiple_of(start, size)


def pipelined(count, *stages):
    first, second, third = stages
    first(0, 0)
    second(0, 0)
    first(1, 1)

    @pl.loop(1, count // 2)
    def _(pair):
        tile = 2 * pair
        third(tile - 2, 0)
        second(tile - 1, 1)
        first(tile, 0)
        third(tile - 1, 1)
        second(tile, 0)
        first(tile + 1, 1)

    third(count - 2, 0)
    second(count - 1, 1)
    third(count - 1, 1)


def keep_rows(ref, value):
    size = value.shape[0]
    ref[:size], ref[size:] = halves(value)


def keep_lanes(ref, value):
    size = value.shape[1]
    ref[:, :size], ref[:, size:] = halves(value)


def left_product(table, ref):
    size = ref.shape[0] // 2
    return dot(table, jnp.concatenate([ref[...], ref[:size]], axis=0))


def right_product(ref, table):
    size = ref.shape[1] // 2
    return dot(jnp.concatenate([ref[...], ref[:, :size]], axis=1), table)


def cmul(real_a, imag_a, real_b, imag_b):
    return real_a * real_b - imag_a * imag_b, real_a * imag_b + imag_a * real_b


def cmul_conj(real_a, imag_a, real_b, imag_b):
    return real_a * real_b + imag_a * imag_b, imag_a * real_b - real_a * imag_b


def small_transform(values, sign):
    count = len(values)
    if count == 1:
        return values
    even = small_transform(values[0::2], sign)
    odd = small_transform(values[1::2], sign)
    first, second = [], []
    for k in range(count // 2):
        er, ei = even[k]
        xr, xi = odd[k]
        if k == 0:
            tr, ti = xr, xi
        elif 4 * k == count:
            tr, ti = (-xi, xr) if sign > 0 else (xi, -xr)
        else:
            c, s = math.cos(2 * math.pi * k / count), sign * math.sin(2 * math.pi * k / count)
            if 8 * k == count:
                tr, ti = ((xr - xi) * c, (xr + xi) * c) if sign > 0 else ((xr + xi) * c, (xi - xr) * c)
            elif 8 * k == 3 * count:
                tr, ti = ((xr + xi) * c, (xi - xr) * c) if sign > 0 else ((xr - xi) * c, (xr + xi) * c)
            else:
                tr, ti = xr * c - xi * s, xr * s + xi * c
        first.append((er + tr, ei + ti))
        second.append((er - tr, ei - ti))
    return first + second


def scale_code(biggest):
    return (jnp.floor(jnp.log(jnp.maximum(biggest, 1e-30)) * STEP_LOG) + 1.0).astype(jnp.int32)


def scale_of(code):
    return jnp.exp(code.astype(jnp.float32) * (1.0 / STEP_LOG)) * (1.0 / TOP)


def inverse_scale_of(code):
    return jnp.exp(code.astype(jnp.float32) * (-1.0 / STEP_LOG)) * TOP


def coded(value, inverse):
    return jnp.floor(value * inverse + 0.5).astype(jnp.int32)


def packed(high, low):
    return (high << 16) | (low & 0xFFFF)


def unpacked(word):
    return (word >> 16).astype(jnp.float32), ((word << 16) >> 16).astype(jnp.float32)


def contribution_kernel(place_ref, order_ref, slot_ref, bin_ref, data_ref, *rest, freqs):
    *sources, held, weight_ref, sems = rest
    sources, outs = sources[:-freqs], sources[-freqs:]
    groups, outer = outs[0].shape[0], outs[0].shape[1] - 1
    count = sources[0].shape[0]
    copies = [
        pltpu.make_async_copy(ref, weight_ref.at[pl.ds(n * count, count)], sems.at[n])
        for n, ref in enumerate(sources)
    ]
    for copy in copies:
        copy.start()
    for copy in copies:
        copy.wait()

    @pl.loop(0, groups)
    def _(group):
        for at in range(GROUP):
            slot = slot_ref[group * GROUP + at]
            source = bin_ref[group * GROUP + at]
            held[pl.ds(at, data_ref.shape[1], GROUP), :] = dot(data_ref[source], weight_ref[slot])
        for away, out_ref in enumerate(outs):
            base = (place_ref[0] ^ away) * (2 * outer * GROUP)

            def term(at):
                return held[pl.ds(pl.multiple_of(base + at * GROUP, GROUP), GROUP), :]

            biggest = functools.reduce(jnp.maximum, [jnp.abs(term(at)) for at in range(2 * outer)])
            code = scale_code(biggest)
            inverse = inverse_scale_of(code)
            for a in range(outer):
                words = packed(coded(term(a), inverse), coded(term(outer + a), inverse))
                out_ref[group, order_ref[a]] = words
            out_ref[group, outer] = code


def propagator_kernel(omega_ref, slow_ref, layers_ref, real_ref, imag_ref, turns_ref):
    steps, layer_total = slow_ref.shape
    for step in range(steps):
        layers = layers_ref[step]
        slow = functools.reduce(
            jnp.add, [jnp.where(layers == n, slow_ref[step, n], 0.0) for n in range(layer_total)]
        )
        turn = 2.0 * dz_cells * omega_ref[0] * (slow - 1.0)
        turns_ref[0, step] = jnp.cos(turn)
        turns_ref[1, step] = jnp.sin(turn)

    total = real_ref.shape[1]
    scale = 1.0 / (NH * total)
    omega_sq = omega_ref[0] * omega_ref[0]

    @pl.loop(0, NH // GROUP)
    def _(at):
        start = pl.multiple_of(at * GROUP, GROUP)
        row = lax.broadcasted_iota(jnp.int32, (GROUP, BLK), 0) + at * GROUP
        lane = lax.broadcasted_iota(jnp.int32, (GROUP, BLK), 1)
        offset_wave = signed_wave(RADIX * (row % TALL) + row // TALL, NH)
        for a in range(total // BLK):
            mid_wave = signed_wave(a + total // BLK * lane, total)
            real, imag = propagator(omega_sq, mid_wave, offset_wave)
            real_ref[pl.ds(start, GROUP), a * BLK : (a + 1) * BLK] = real * scale
            imag_ref[pl.ds(start, GROUP), a * BLK : (a + 1) * BLK] = imag * scale


def column_of(plane, a):
    lanes = pl.ds(aligned(a * BLK, BLK), BLK)
    return jnp.concatenate(
        [jnp.concatenate([plane[q, 0, :, lanes], plane[q, 1, :, lanes]], axis=0) for q in range(RADIX)],
        axis=1,
    )


def store_column(plane, a, value):
    lanes = pl.ds(aligned(a * BLK, BLK), BLK)
    for q in range(RADIX):
        for c in range(2):
            plane[q, c, :, lanes] = value[c * TALL : (c + 1) * TALL, q * BLK : (q + 1) * BLK]


def row_starts():
    return range(0, TALL, ROWS)


def forward_rows(values, offset_ref, start):
    rows = slice(start, start + ROWS)
    values = small_transform(values, -1)
    return values[:1] + [
        cmul_conj(*values[q], offset_ref[0, q, rows], offset_ref[1, q, rows]) for q in range(1, RADIX)
    ]


def inverse_rows(value, offset_ref, start):
    rows, below = slice(start, start + ROWS), slice(TALL + start, TALL + start + ROWS)
    values = []
    for q in range(RADIX):
        part = value[rows, q * BLK : (q + 1) * BLK], value[below, q * BLK : (q + 1) * BLK]
        values.append(cmul(*part, offset_ref[0, q, rows], offset_ref[1, q, rows]) if q else part)
    return small_transform(values, 1)


def assembled(blocks):
    return jnp.concatenate(
        [
            jnp.concatenate([values[q][c] for c in range(2) for values in blocks], axis=0)
            for q in range(RADIX)
        ],
        axis=1,
    )


def layer_turn(values, layer_ref, step, a):
    per = RADIX // layer_ref.shape[2]
    return [
        cmul(*part, layer_ref[0, step, g // per, a], layer_ref[1, step, g // per, a])
        for g, part in enumerate(values)
    ]


def midpoint_pass(plane, out, phase_refs, forward, inverse, middle_ref, first_kept, second_kept):
    outer = middle_ref.shape[1]
    lanes = [slice(a * BLK, (a + 1) * BLK) for a in range(outer)]
    tall = first_kept[0].shape[0] // outer
    per_half = TALL // tall
    chunks = range(0, tall, ROWS)

    def place(at):
        return at // per_half, (at % per_half) * tall

    def gathered(pieces):
        return jnp.concatenate([jnp.concatenate(pair, axis=1) for pair in pieces], axis=0)

    def forward_stage(at, parity):
        p, base = place(at)
        pieces = []
        for chunk in chunks:
            here = pl.ds(aligned(base + chunk, ROWS), ROWS)
            values = [(plane[p, 0, here, lane], plane[p, 1, here, lane]) for lane in lanes]
            values = small_transform(values, -1)
            for a in range(outer):
                pieces.append(cmul_conj(*values[a], middle_ref[0, a], middle_ref[1, a]))
        keep_lanes(first_kept[parity], gathered(pieces))

    def phase_stage(at, parity):
        value = right_product(first_kept[parity], forward[...])
        pieces = []
        for chunk in chunks:
            there = pl.ds(aligned(at * tall + chunk, ROWS), ROWS)
            for a in range(outer):
                row = chunk * outer + a * ROWS
                part = value[row : row + ROWS]
                pieces.append(
                    cmul(
                        part[:, :BLK], part[:, BLK:],
                        phase_refs[0][there, lanes[a]], phase_refs[1][there, lanes[a]],
                    )
                )
        keep_lanes(second_kept[parity], gathered(pieces))

    def inverse_stage(at, parity):
        p, base = place(at)
        value = right_product(second_kept[parity], inverse[...])
        for chunk in chunks:
            here = pl.ds(aligned(base + chunk, ROWS), ROWS)
            values = []
            for a in range(outer):
                row = chunk * outer + a * ROWS
                part = value[row : row + ROWS]
                values.append(
                    cmul(part[:, :BLK], part[:, BLK:], middle_ref[0, a], middle_ref[1, a])
                )
            values = small_transform(values, 1)
            for a in range(outer):
                out[p, 0, here, lanes[a]] = values[a][0]
                out[p, 1, here, lanes[a]] = values[a][1]

    pipelined(RADIX * per_half, forward_stage, phase_stage, inverse_stage)


def march_kernel(layer_ref, *rest, sources):
    code_refs, rest = rest[:sources], rest[sources:]
    (
        pick_ref, phase_real, phase_imag, rows_forward, rows_inverse, lanes_forward, lanes_inverse,
        middle_ref, offset_ref, other, plane, scales, *kept,
    ) = rest
    column_first, column_second, row_first, row_second, terms = (kept[n : n + 2] for n in range(0, 10, 2))
    groups = code_refs[0].shape[0]
    outer = middle_ref.shape[1]
    steps = layer_ref.shape[1]

    def words(a):
        return jnp.concatenate([ref[:, a].reshape(groups * GROUP, BLK) for ref in code_refs], axis=0)

    scales[...] = scale_of(words(outer))

    def decode_stage(a, parity):
        real, imag = unpacked(words(a))
        scale = scales[...]
        keep_rows(terms[parity], jnp.concatenate([real * scale, imag * scale], axis=1))

    def place_stage(a, parity):
        moved = dot(pick_ref[...], terms[parity][...])
        blocks = []
        for start in row_starts():
            values = []
            for g in range(RADIX):
                part = moved[g * TALL + start : g * TALL + start + ROWS]
                values.append((part[:, :BLK], part[:, BLK:]))
            blocks.append(forward_rows(values, offset_ref, start))
        keep_rows(column_second[parity], assembled(blocks))

    def store_stage(a, parity):
        store_column(plane, a, left_product(rows_forward[...], column_second[parity]))

    pipelined(outer, decode_stage, place_stage, store_stage)

    for step in range(steps):
        midpoint_pass(
            plane, other, (phase_real, phase_imag), lanes_forward, lanes_inverse, middle_ref, row_first, row_second
        )
        if step < steps - 1:

            def load_stage(a, parity):
                keep_rows(column_first[parity], column_of(other, a))

            def turn_stage(a, parity):
                value = left_product(rows_inverse[...], column_first[parity])
                blocks = []
                for start in row_starts():
                    values = layer_turn(inverse_rows(value, offset_ref, start), layer_ref, step, a)
                    blocks.append(forward_rows(values, offset_ref, start))
                keep_rows(column_second[parity], assembled(blocks))

            pipelined(outer, load_stage, turn_stage, store_stage)


def finish_kernel(dest_ref, layer_ref, plane_ref, rows_inverse, offset_ref, *rest):
    out_ref, kept = rest[-2:]
    here = plane_ref.shape[3] // BLK
    step = layer_ref.shape[1] - 1
    keep_rows(kept, jnp.concatenate([column_of(plane_ref, at) for at in range(here)], axis=1))
    value = left_product(rows_inverse[...], kept)
    for at in range(here):
        column = value[:, at * RADIX * BLK : (at + 1) * RADIX * BLK]
        found = [
            layer_turn(inverse_rows(column, offset_ref, start), layer_ref, step, dest_ref[0] * here + at)
            for start in row_starts()
        ]
        for c in range(2):
            biggest = functools.reduce(
                jnp.maximum, [jnp.abs(part[c]) for values in found for part in values]
            )
            code = scale_code(jnp.max(biggest, axis=0, keepdims=True))
            inverse = inverse_scale_of(code)
            row = at * 2 + c
            for start, values in zip(row_starts(), found):
                for g in range(RADIX // 2):
                    words = packed(
                        coded(values[g][c], inverse), coded(values[g + RADIX // 2][c], inverse)
                    )
                    first = (g * TALL + start) * 2 * here + row
                    out_ref[pl.ds(first, ROWS, 2 * here), :] = words
            out_ref[pl.ds(HALF * 2 * here + row, 1), :] = code


def result_kernel(freq_ref, code_ref, *rest):
    out_ref = rest[-1]
    per, tall = out_ref.shape[1:3]
    scale = scale_of(code_ref[per * tall :])[None]
    for half in range(2):

        @pl.when(pl.program_id(0) == half)
        def _():
            out_ref[0] = unpacked(code_ref[: per * tall].reshape(per, tall, BLK))[half] * scale


def take_kernel(mine_ref, counts_ref, source_ref, out_ref, sems):
    taken, entries = out_ref.shape[0], source_ref.shape[1]
    bins_here, stride = source_ref.shape[0], source_ref.shape[0] * entries // taken
    copies = []
    for n in range(taken):
        entry, bin_at = n * stride + mine_ref[0], 0
        for b in range(bins_here - 1):
            over = (bin_at == b) & (entry >= counts_ref[b])
            entry = jnp.where(over, entry - counts_ref[b], entry)
            bin_at = jnp.where(over, b + 1, bin_at)
        entry = jnp.minimum(entry, entries - 1)
        copies.append(
            pltpu.make_async_copy(source_ref.at[bin_at, entry], out_ref.at[n], sems.at[n])
        )
        copies[-1].start()
    for copy in copies:
        copy.wait()


def slot_lists(counts_all, targets_all, bins_local, fl, per_device, room):
    offs = counts_all.shape[0] // bins_local
    entries = targets_all.shape[1]
    counts_in = counts_all.reshape(offs, bins_local)
    live = jnp.sum(counts_in, axis=1)
    quarter = jnp.arange(fl, dtype=jnp.int32)
    held = (live[None, :] - quarter[:, None] + fl - 1) // fl
    upto = jnp.sum(
        jnp.where(jnp.arange(offs)[None, :] <= jnp.arange(offs)[:, None], held[:, None, :], 0), axis=2
    )
    at = jnp.arange(room, dtype=jnp.int32)
    past = (at[None, :, None] >= upto[:, None, :]).astype(jnp.int32)
    off_at = jnp.sum(past, axis=2)
    valid = off_at < offs
    off_at = jnp.minimum(off_at, offs - 1)
    start = jnp.sum(past * held[:, None, :], axis=2)
    nth = jnp.clip(at[None, :] - start, 0, per_device - 1)
    entry = nth * fl + quarter[:, None]
    bin_at = off_at * bins_local
    mine = off_at[:, :, None] == jnp.arange(offs)[None, None, :]
    for b in range(bins_local - 1):
        size = jnp.sum(jnp.where(mine, counts_in[None, None, :, b], 0), axis=2)
        over = (bin_at == off_at * bins_local + b) & (entry >= size)
        bin_at = bin_at + over
        entry = entry - jnp.where(over, size, 0)
    flat = bin_at * entries + entry
    total = targets_all.size
    picks = flat[:, :, None] == jnp.arange(total)[None, None, :]
    target = jnp.sum(jnp.where(picks, targets_all.reshape(1, 1, total), 0), axis=2)
    target = jnp.where(valid, target, -1)
    return off_at, nth, bin_at, target


def local(bins_data, operators, targets, counts, layer_index, slowness):
    off_count = lax.axis_size("off")
    mid_count = lax.axis_size("mid")
    bins_local, freq_total, _, mid_local = bins_data.shape
    entries = operators.shape[1]
    bins_total = bins_local * off_count
    fl = freq_total // off_count
    total_mid = mid_local * mid_count
    outer = total_mid // BLK
    mid_at, off_at = lax.axis_index("mid"), lax.axis_index("off")
    assert RADIX % layer_index.shape[1] == 0 and mid_count % fl == 0 and (bins_local * entries) % fl == 0
    mine = mid_at % fl
    rounds = mid_count // fl
    groups = (
        None if rounds == 1 else [list(range(g * fl, (g + 1) * fl)) for g in range(rounds)]
    )

    per_device = bins_local * entries // fl
    smem = pl.BlockSpec(memory_space=pltpu.SMEM)
    vmem = pl.BlockSpec(memory_space=pltpu.VMEM)
    hbm = pl.BlockSpec(memory_space=pl.ANY)
    own = pl.pallas_call(
        take_kernel,
        in_specs=[smem, smem, hbm],
        out_specs=vmem,
        out_shape=jax.ShapeDtypeStruct((per_device, BLK, BLK), jnp.bfloat16),
        scratch_shapes=[pltpu.SemaphoreType.DMA((per_device,))],
        compiler_params=pltpu.CompilerParams(vmem_limit_bytes=SMALL),
        name="take_own",
    )(mine.reshape(1), counts, operators)
    bins_data, own = lax.optimization_barrier((bins_data, own))
    cores = 2 if off_count % 2 == 0 else 1
    line = off_count // cores
    assert line & (line - 1) == 0 and fl & (fl - 1) == 0
    shares = [own]
    for away in range(1, line):
        low = away & -away
        shares.append(
            lax.ppermute(
                shares[away ^ low],
                "off",
                [(i, (i // cores ^ low) * cores + i % cores) for i in range(off_count)],
            )
        )
    if cores > 1:
        shares += [lax.ppermute(x, "off", [(i, i ^ 1) for i in range(off_count)]) for x in shares]

    pairs = fl * 2

    def extra(whole_numbers, copies):
        flat = whole_numbers.astype(jnp.bfloat16).reshape(1, 1, 1, -1)
        flat = jnp.pad(flat, ((0, 0), (0, 0), (0, pairs - 1), (0, mid_local - flat.shape[3])))
        return jnp.broadcast_to(flat, (1, copies, pairs, mid_local))

    lists = lax.optimization_barrier(jnp.concatenate([counts[:, None], targets], axis=1))
    data = bins_data.reshape(bins_local, off_count, pairs, mid_local)
    data = jnp.concatenate([data, extra(lists, off_count)], axis=0)
    data = lax.all_to_all(data, "off", split_axis=1, concat_axis=0, tiled=True)
    data = data.reshape(off_count, bins_local + 1, pairs, mid_local)
    lists = data[:, bins_local, 0, : lists.size].astype(jnp.int32).reshape(bins_total, 1 + entries)
    data = data[:, :bins_local].reshape(bins_total, pairs, mid_local)
    data = jnp.concatenate([data, extra(layer_index, 1)[0]], axis=0)
    assert mid_count & (mid_count - 1) == 0
    parts = [data] + [
        lax.ppermute(data, "mid", [(i, i ^ away) for i in range(mid_count)])
        for away in range(mid_count - 1, 0, -1)
    ]
    data = jnp.stack(parts[:1] + parts[:0:-1])
    partner = jnp.arange(mid_count, dtype=jnp.int32) ^ mid_at
    layers = data[:, bins_total, 0, : layer_index.size].astype(jnp.int32)
    layers = jnp.sum(
        jnp.where((partner[:, None] == jnp.arange(mid_count))[:, :, None], layers[None], 0), axis=1
    )
    layers = layers.reshape(mid_count, *layer_index.shape).transpose(1, 2, 0, 3)
    layers = layers.reshape(*layer_index.shape[:2], outer)
    data = data[:, :bins_total].reshape(mid_count, bins_total, pairs, mid_local // BLK, BLK)
    data = data.transpose(1, 2, 0, 3, 4).reshape(bins_total, pairs * outer, BLK)
    order = (partner[:, None] * (mid_local // BLK) + jnp.arange(mid_local // BLK)).reshape(outer)

    live_total = bins_total * entries // 2
    room = -(-(live_total + (fl - 1) * off_count) // fl)
    room = min(-(-room // GROUP) * GROUP, per_device * off_count)
    offs, nth, bins, goal = slot_lists(lists[:, 0], lists[:, 1:], bins_local, fl, per_device, room)
    side = (offs % cores != off_at % cores).astype(jnp.int32) * line
    slots = (side + ((offs // cores) ^ (off_at // cores))) * per_device + nth
    source = jnp.arange(fl, dtype=jnp.int32) ^ mine
    goal = jnp.sum(jnp.where((source[:, None] == jnp.arange(fl))[:, :, None], goal[None], 0), axis=1)
    pick = (
        jnp.tile(goal.reshape(1, fl * room), (1, 2))
        == lax.broadcasted_iota(jnp.int32, (NH, 2 * fl * room), 0)
    ).astype(jnp.bfloat16)
    own_slots = lax.dynamic_index_in_dim(slots, mine, 0, False)
    own_bins = lax.dynamic_index_in_dim(bins, mine, 0, False)
    list_groups = room // GROUP
    data, order, own_slots, own_bins, layers, pick = lax.optimization_barrier(
        (data, order, own_slots, own_bins, layers, pick)
    )
    shape = jax.ShapeDtypeStruct((list_groups, outer + 1, GROUP, BLK), jnp.int32)
    terms = pl.pallas_call(
        functools.partial(contribution_kernel, freqs=fl),
        in_specs=[smem, smem, smem, smem, vmem] + [hbm] * len(shares),
        out_specs=[vmem] * fl,
        out_shape=[shape] * fl,
        scratch_shapes=[
            pltpu.VMEM((fl * 2 * outer * GROUP, BLK), jnp.float32),
            pltpu.VMEM((len(shares) * per_device, BLK, BLK), jnp.bfloat16),
            pltpu.SemaphoreType.DMA((len(shares),)),
        ],
        compiler_params=pltpu.CompilerParams(vmem_limit_bytes=SMALL),
        name="contributions",
    )(mine.reshape(1), order, own_slots, own_bins, data, *shares)
    terms, freq_at = lax.optimization_barrier((terms, off_at * fl + mine))
    got = {0: terms[0]}
    for away in range(fl - 1, 0, -1):
        got[away] = lax.ppermute(terms[away], "mid", [(i, i ^ away) for i in range(mid_count)])
    terms = [got[away] for away in range(fl)]

    omega = math.pi * (0.1 + 0.8 * (freq_at.astype(jnp.float32) + 0.5) / freq_total)
    phase_real, phase_imag, layer_turns = pl.pallas_call(
        propagator_kernel,
        in_specs=[smem, smem, vmem],
        out_specs=[vmem] * 3,
        out_shape=[jax.ShapeDtypeStruct((NH, total_mid), jnp.float32)] * 2
        + [jax.ShapeDtypeStruct((2, *layers.shape), jnp.float32)],
        compiler_params=pltpu.CompilerParams(vmem_limit_bytes=SMALL),
        cost_estimate=pl.CostEstimate(
            flops=60 * NH * total_mid, bytes_accessed=8 * NH * total_mid, transcendentals=10 * NH * total_mid
        ),
        name="propagator",
    )(omega.reshape(1), slowness, layers)

    middle, offset_turn = twiddle_tables(outer)
    here = mid_local // BLK
    rows_out = (HALF + 1) * 2 * here
    tables = [jnp.asarray(t) for t in block_tables()]
    middle, offset_turn = jnp.asarray(middle), jnp.asarray(offset_turn)
    plane = pl.pallas_call(
        functools.partial(march_kernel, sources=fl),
        in_specs=[smem] + [vmem] * (fl + 9),
        out_specs=vmem,
        out_shape=jax.ShapeDtypeStruct((RADIX, 2, TALL, total_mid), jnp.float32),
        scratch_shapes=[
            pltpu.VMEM((RADIX, 2, TALL, total_mid), jnp.float32),
            pltpu.VMEM((fl * room, BLK), jnp.float32),
            *[pltpu.VMEM((4 * TALL, RADIX * BLK), jnp.bfloat16)] * 4,
            *[pltpu.VMEM((ROWS * CHUNKS * outer, 4 * BLK), jnp.bfloat16)] * 4,
            *[pltpu.VMEM((2 * fl * room, 2 * BLK), jnp.bfloat16)] * 2,
        ],
        compiler_params=pltpu.CompilerParams(vmem_limit_bytes=VMEM),
        name="march",
    )(layer_turns, *terms, pick, phase_real, phase_imag, *tables, middle, offset_turn)

    def finish(dest, *before):
        return pl.pallas_call(
            finish_kernel,
            grid_spec=pltpu.PrefetchScalarGridSpec(
                num_scalar_prefetch=1,
                grid=(1,),
                in_specs=[
                    smem,
                    pl.BlockSpec((RADIX, 2, TALL, mid_local), lambda i, dest: (0, 0, 0, dest[0])),
                    vmem,
                    vmem,
                ]
                + [hbm] * len(before),
                out_specs=pl.BlockSpec((rows_out, BLK), lambda i, dest: (0, 0)),
                scratch_shapes=[pltpu.VMEM((4 * TALL, RADIX * mid_local), jnp.bfloat16)],
            ),
            out_shape=jax.ShapeDtypeStruct((rows_out, BLK), jnp.int32),
            cost_estimate=pl.CostEstimate(
                flops=6 * NH * NH * 2 * BLK * here, bytes_accessed=6 * NH * mid_local, transcendentals=0
            ),
            compiler_params=pltpu.CompilerParams(vmem_limit_bytes=SMALL),
            name="finish",
        )(dest.reshape(1), layer_turns, plane, tables[1], offset_turn, *before)

    got, before = {}, []
    for ahead in [*range(fl - 1, 0, -1), 0]:
        dest = (mid_at // fl) * fl + (mine ^ ahead)
        block = finish(dest, *before)
        before = [block]
        if ahead:
            block = lax.ppermute(block, "mid", [(s, s ^ ahead) for s in range(mid_count)])
        got[ahead] = block

    field = None
    for ahead in [0, *range(fl - 1, 0, -1)]:
        freq = mine ^ ahead
        first = field is None
        field = pl.pallas_call(
            result_kernel,
            grid_spec=pltpu.PrefetchScalarGridSpec(
                num_scalar_prefetch=1,
                grid=(2,),
                in_specs=[vmem] if first else [vmem, hbm],
                out_specs=pl.BlockSpec((1, HALF, 2 * here, BLK), lambda i, f: (f[0], i, 0, 0)),
            ),
            out_shape=jax.ShapeDtypeStruct((fl, NH, 2 * here, BLK), jnp.float32),
            input_output_aliases={} if first else {2: 0},
            compiler_params=pltpu.CompilerParams(vmem_limit_bytes=SMALL),
            cost_estimate=pl.CostEstimate(
                flops=4 * NH * mid_local, bytes_accessed=12 * NH * mid_local, transcendentals=0
            ),
            name="result",
        )(freq.reshape(1), got[ahead], *([] if first else [field]))
    field = field.reshape(fl, NH, here, 2, BLK).transpose(0, 1, 3, 2, 4)
    return field.reshape(fl, NH, 2, mid_local)


def solution(mesh):
    in_specs = (
        P("off", None, None, "mid"),
        P("off", None, None, None),
        P("off", None),
        P("off"),
        P(None, None, "mid"),
        P(),
    )
    out_specs = P("off", None, None, "mid")
    return jax.shard_map(local, mesh=mesh, in_specs=in_specs, out_specs=out_specs, check_vma=False)
```

```python
import functools
import math

import jax
import jax.numpy as jnp
import numpy as np
from jax import lax
from jax.experimental import pallas as pl
from jax.experimental.pallas import tpu as pltpu
from jax.sharding import PartitionSpec as P

NH = 256
BLK = 128

dz_cells = 2.0
damping = 0.1

HALF = NH // 2
STEP_LOG = 64.0
TOP = 32767.0
GROUP = 8
ROWS = 8
CHUNKS = 2
VMEM = 28 * 1024 * 1024
SMALL = 10 * 1024 * 1024


def signed_wave(index, length):
    signed = (index + length // 2) % length - length // 2
    return signed.astype(jnp.float32) * (2.0 * math.pi / length)


def root_pair(level):
    magnitude = jnp.sqrt(level * level + damping * damping)
    larger = jnp.sqrt(0.5 * (magnitude + jnp.abs(level)))
    smaller = damping / (2.0 * larger)
    return (jnp.where(level >= 0, larger, smaller), jnp.where(level >= 0, smaller, larger))


def propagator(omega_sq, mid_wave, offset_wave):
    source = 0.5 * (mid_wave - offset_wave)
    receiver = 0.5 * (mid_wave + offset_wave)
    real_s, imag_s = root_pair(omega_sq - source * source)
    real_r, imag_r = root_pair(omega_sq - receiver * receiver)
    decay = jnp.exp(-dz_cells * (imag_s + imag_r))
    turn = dz_cells * (real_s + real_r)
    return (decay * jnp.cos(turn), decay * jnp.sin(turn))


def halves_np(table):
    high = table.astype(np.float32).astype(jnp.bfloat16)
    low = (table - high.astype(np.float64)).astype(np.float32).astype(jnp.bfloat16)
    return high, low


def block_tables():
    index = np.arange(BLK)
    angles = 2.0 * np.pi * (np.outer(index, index) % BLK) / BLK
    cos, sin = np.cos(angles), np.sin(angles)
    upper = np.block([[cos, sin], [-sin, cos]])
    lower = np.block([[cos, -sin], [sin, cos]])
    tables = []
    for axis, pair in ((1, (upper, lower)), (0, (lower, upper))):
        for table in pair:
            high, low = halves_np(table)
            tables.append(np.concatenate([high, high, low], axis=axis).astype(np.float32))
    return tables


def twiddle_tables(outer):
    ka, b = np.arange(outer)[:, None], np.arange(BLK)[None, :]
    angles = 2.0 * np.pi * ka * b / (outer * BLK)
    middle = np.stack([np.cos(angles), np.sin(angles)]).astype(np.float32)
    rows = 2.0 * np.pi * np.arange(HALF) / NH
    offset = np.stack([np.cos(rows), np.sin(rows)]).astype(np.float32)
    return middle, np.broadcast_to(offset[:, :, None], (2, HALF, BLK)).copy()


def halves(value):
    wide = value * 65537.0
    high = wide - (wide - value)
    return high, value - high


def dot(left, right):
    return jnp.dot(left, right, preferred_element_type=jnp.float32)


def aligned(start, size):
    return start if isinstance(start, int) else pl.multiple_of(start, size)


def pipelined(count, *stages):
    first, second, third = stages
    first(0, 0)
    second(0, 0)
    first(1, 1)

    @pl.loop(1, count // 2)
    def _(pair):
        tile = 2 * pair
        third(tile - 2, 0)
        second(tile - 1, 1)
        first(tile, 0)
        third(tile - 1, 1)
        second(tile, 0)
        first(tile + 1, 1)

    third(count - 2, 0)
    second(count - 1, 1)
    third(count - 1, 1)


def keep_rows(ref, value):
    size = value.shape[0]
    ref[:size], ref[size:] = halves(value)


def keep_lanes(ref, value):
    size = value.shape[1]
    ref[:, :size], ref[:, size:] = halves(value)


def left_product(table, ref):
    size = ref.shape[0] // 2
    return dot(table, jnp.concatenate([ref[...], ref[:size]], axis=0))


def right_product(ref, table):
    size = ref.shape[1] // 2
    return dot(jnp.concatenate([ref[...], ref[:, :size]], axis=1), table)


def cmul(real_a, imag_a, real_b, imag_b):
    return real_a * real_b - imag_a * imag_b, real_a * imag_b + imag_a * real_b


def small_transform(values, sign):
    count = len(values)
    if count == 1:
        return values
    even = small_transform(values[0::2], sign)
    odd = small_transform(values[1::2], sign)
    first, second = [], []
    for k in range(count // 2):
        er, ei = even[k]
        xr, xi = odd[k]
        if k == 0:
            tr, ti = xr, xi
        elif 4 * k == count:
            tr, ti = (-xi, xr) if sign > 0 else (xi, -xr)
        else:
            c, s = math.cos(2 * math.pi * k / count), sign * math.sin(2 * math.pi * k / count)
            if 8 * k == count:
                tr, ti = ((xr - xi) * c, (xr + xi) * c) if sign > 0 else ((xr + xi) * c, (xi - xr) * c)
            elif 8 * k == 3 * count:
                tr, ti = ((xr + xi) * c, (xi - xr) * c) if sign > 0 else ((xr - xi) * c, (xr + xi) * c)
            else:
                tr, ti = xr * c - xi * s, xr * s + xi * c
        first.append((er + tr, ei + ti))
        second.append((er - tr, ei - ti))
    return first + second


def scale_code(biggest):
    return (jnp.floor(jnp.log(jnp.maximum(biggest, 1e-30)) * STEP_LOG) + 1.0).astype(jnp.int32)


def scale_of(code):
    return jnp.exp(code.astype(jnp.float32) * (1.0 / STEP_LOG)) * (1.0 / TOP)


def inverse_scale_of(code):
    return jnp.exp(code.astype(jnp.float32) * (-1.0 / STEP_LOG)) * TOP


def coded(value, inverse):
    return jnp.floor(value * inverse + 0.5).astype(jnp.int32)


def packed(high, low):
    return (high << 16) | (low & 0xFFFF)


def unpacked(word):
    return (word >> 16).astype(jnp.float32), ((word << 16) >> 16).astype(jnp.float32)


def contribution_kernel(place_ref, order_ref, slot_ref, bin_ref, data_ref, *rest, freqs):
    *sources, held, weight_ref, sems = rest
    sources, outs = sources[:-freqs], sources[-freqs:]
    groups, outer = outs[0].shape[0], outs[0].shape[1] - 1
    count = sources[0].shape[0]
    copies = [
        pltpu.make_async_copy(ref, weight_ref.at[pl.ds(n * count, count)], sems.at[n])
        for n, ref in enumerate(sources)
    ]
    for copy in copies:
        copy.start()
    for copy in copies:
        copy.wait()

    @pl.loop(0, groups)
    def _(group):
        for at in range(GROUP):
            slot = slot_ref[group * GROUP + at]
            source = bin_ref[group * GROUP + at]
            held[pl.ds(at, data_ref.shape[1], GROUP), :] = dot(data_ref[source], weight_ref[slot])
        for away, out_ref in enumerate(outs):
            base = (place_ref[0] ^ away) * (2 * outer * GROUP)

            def term(at):
                return held[pl.ds(pl.multiple_of(base + at * GROUP, GROUP), GROUP), :]

            biggest = functools.reduce(jnp.maximum, [jnp.abs(term(at)) for at in range(2 * outer)])
            code = scale_code(biggest)
            inverse = inverse_scale_of(code)
            for a in range(outer):
                words = packed(coded(term(a), inverse), coded(term(outer + a), inverse))
                out_ref[group, order_ref[a]] = words
            out_ref[group, outer] = code


def column_of(plane, a):
    lanes = pl.ds(aligned(a * BLK, BLK), BLK)
    return jnp.concatenate(
        [
            jnp.concatenate([plane[p, 0, :, lanes], plane[p, 1, :, lanes]], axis=0)
            for p in range(2)
        ],
        axis=1,
    )


def store_column(plane, a, value):
    lanes = pl.ds(aligned(a * BLK, BLK), BLK)
    for p in range(2):
        for c in range(2):
            plane[p, c, :, lanes] = value[c * HALF : (c + 1) * HALF, p * BLK : (p + 1) * BLK]


def row_blocks(tall):
    return [slice(at * tall, (at + 1) * tall) for at in range(HALF // tall)]


def turn_at(offset_ref, rows):
    return offset_ref[0, rows], offset_ref[1, rows]


def forward_rows(low, high, turn):
    first = low[0] + high[0], low[1] + high[1]
    second = cmul(low[0] - high[0], low[1] - high[1], turn[0], -turn[1])
    return (*first, *second)


def inverse_rows(value, rows, turn):
    upper, below = rows, slice(HALF + rows.start, HALF + rows.stop)
    first = value[upper, :BLK], value[below, :BLK]
    second = cmul(value[upper, BLK:], value[below, BLK:], turn[0], turn[1])
    low = first[0] + second[0], first[1] + second[1]
    high = first[0] - second[0], first[1] - second[1]
    return low, high


def assembled(blocks):
    parts = [jnp.concatenate(part, axis=0) for part in zip(*blocks)]
    return jnp.concatenate(
        [jnp.concatenate(parts[:2], axis=0), jnp.concatenate(parts[2:], axis=0)], axis=1
    )


def propagator_kernel(omega_ref, slow_ref, layers_ref, real_ref, imag_ref, turns_ref):
    steps, layer_total = slow_ref.shape
    for step in range(steps):
        layers = layers_ref[step]
        slow = functools.reduce(
            jnp.add, [jnp.where(layers == n, slow_ref[step, n], 0.0) for n in range(layer_total)]
        )
        turn = 2.0 * dz_cells * omega_ref[0] * (slow - 1.0)
        turns_ref[0, step] = jnp.cos(turn)
        turns_ref[1, step] = jnp.sin(turn)

    total = real_ref.shape[1]
    scale = 1.0 / (NH * total)
    omega_sq = omega_ref[0] * omega_ref[0]

    @pl.loop(0, NH // GROUP)
    def _(at):
        start = pl.multiple_of(at * GROUP, GROUP)
        row = lax.broadcasted_iota(jnp.int32, (GROUP, BLK), 0) + at * GROUP
        lane = lax.broadcasted_iota(jnp.int32, (GROUP, BLK), 1)
        offset_wave = signed_wave(2 * (row % HALF) + row // HALF, NH)
        for a in range(total // BLK):
            mid_wave = signed_wave(a + total // BLK * lane, total)
            real, imag = propagator(omega_sq, mid_wave, offset_wave)
            real_ref[pl.ds(start, GROUP), a * BLK : (a + 1) * BLK] = real * scale
            imag_ref[pl.ds(start, GROUP), a * BLK : (a + 1) * BLK] = imag * scale


def layer_turn(pair, layer_ref, step, block, a):
    half = layer_ref.shape[2] // 2
    return [
        cmul(*part, layer_ref[0, step, block + p * half, a], layer_ref[1, step, block + p * half, a])
        for p, part in enumerate(pair)
    ]


def midpoint_pass(plane, out, phase_refs, forward, inverse, middle_ref, first_kept, second_kept):
    outer = middle_ref.shape[1]
    lanes = [slice(a * BLK, (a + 1) * BLK) for a in range(outer)]
    tall = first_kept[0].shape[0] // outer
    per_half = HALF // tall
    chunks = range(0, tall, ROWS)

    def place(at):
        return at // per_half, (at % per_half) * tall

    def gathered(pieces):
        return jnp.concatenate([jnp.concatenate(pair, axis=1) for pair in pieces], axis=0)

    def forward_stage(at, parity):
        p, base = place(at)
        pieces = []
        for chunk in chunks:
            here = pl.ds(aligned(base + chunk, ROWS), ROWS)
            values = [(plane[p, 0, here, lane], plane[p, 1, here, lane]) for lane in lanes]
            values = small_transform(values, -1)
            for a in range(outer):
                pieces.append(cmul(*values[a], middle_ref[0, a : a + 1], -middle_ref[1, a : a + 1]))
        keep_lanes(first_kept[parity], gathered(pieces))

    def phase_stage(at, parity):
        value = right_product(first_kept[parity], forward[...])
        pieces = []
        for chunk in chunks:
            there = pl.ds(aligned(at * tall + chunk, ROWS), ROWS)
            for a in range(outer):
                row = chunk * outer + a * ROWS
                part = value[row : row + ROWS]
                pieces.append(
                    cmul(
                        part[:, :BLK], part[:, BLK:],
                        phase_refs[0][there, lanes[a]], phase_refs[1][there, lanes[a]],
                    )
                )
        keep_lanes(second_kept[parity], gathered(pieces))

    def inverse_stage(at, parity):
        p, base = place(at)
        value = right_product(second_kept[parity], inverse[...])
        for chunk in chunks:
            here = pl.ds(aligned(base + chunk, ROWS), ROWS)
            values = []
            for a in range(outer):
                row = chunk * outer + a * ROWS
                part = value[row : row + ROWS]
                values.append(
                    cmul(part[:, :BLK], part[:, BLK:], middle_ref[0, a : a + 1], middle_ref[1, a : a + 1])
                )
            values = small_transform(values, 1)
            for a in range(outer):
                out[p, 0, here, lanes[a]] = values[a][0]
                out[p, 1, here, lanes[a]] = values[a][1]

    pipelined(2 * per_half, forward_stage, phase_stage, inverse_stage)


def march_kernel(layer_ref, *rest, sources):
    code_refs, rest = rest[:sources], rest[sources:]
    (
        pick_ref, phase_real, phase_imag, rows_forward, rows_inverse, lanes_forward, lanes_inverse,
        middle_ref, offset_ref, other, plane, scales, *kept,
    ) = rest
    column_first, column_second, row_first, row_second, terms = (kept[n : n + 2] for n in range(0, 10, 2))
    groups = code_refs[0].shape[0]
    outer = middle_ref.shape[1]
    steps = layer_ref.shape[1]
    tall = NH // layer_ref.shape[2]

    def words(a):
        return jnp.concatenate([ref[:, a].reshape(groups * GROUP, BLK) for ref in code_refs], axis=0)

    scales[...] = scale_of(words(outer))

    def decode_stage(a, parity):
        real, imag = unpacked(words(a))
        scale = scales[...]
        keep_rows(terms[parity], jnp.concatenate([real * scale, imag * scale], axis=1))

    def place_stage(a, parity):
        moved = dot(pick_ref[...], terms[parity][...])
        blocks = []
        for rows in row_blocks(tall):
            low, high = moved[rows], moved[HALF + rows.start : HALF + rows.stop]
            blocks.append(
                forward_rows(
                    (low[:, :BLK], low[:, BLK:]), (high[:, :BLK], high[:, BLK:]), turn_at(offset_ref, rows)
                )
            )
        keep_rows(column_second[parity], assembled(blocks))

    def store_stage(a, parity):
        store_column(plane, a, left_product(rows_forward[...], column_second[parity]))

    pipelined(outer, decode_stage, place_stage, store_stage)

    for step in range(steps):
        midpoint_pass(
            plane, other, (phase_real, phase_imag), lanes_forward, lanes_inverse, middle_ref, row_first, row_second
        )
        if step < steps - 1:

            def load_stage(a, parity):
                keep_rows(column_first[parity], column_of(other, a))

            def turn_stage(a, parity):
                value = left_product(rows_inverse[...], column_first[parity])
                blocks = []
                for block, rows in enumerate(row_blocks(tall)):
                    turn = turn_at(offset_ref, rows)
                    pair = inverse_rows(value, rows, turn)
                    blocks.append(forward_rows(*layer_turn(pair, layer_ref, step, block, a), turn))
                keep_rows(column_second[parity], assembled(blocks))

            pipelined(outer, load_stage, turn_stage, store_stage)


def finish_kernel(dest_ref, layer_ref, plane_ref, rows_inverse, offset_ref, *rest):
    out_ref, kept = rest[-2:]
    here = plane_ref.shape[3] // BLK
    tall = NH // layer_ref.shape[2]
    step = layer_ref.shape[1] - 1
    keep_rows(kept, jnp.concatenate([column_of(plane_ref, at) for at in range(here)], axis=1))
    value = left_product(rows_inverse[...], kept)
    columns = [value[:, at * 2 * BLK : (at + 1) * 2 * BLK] for at in range(here)]
    for at in range(here):
        found = []
        for block, rows in enumerate(row_blocks(tall)):
            pair = inverse_rows(columns[at], rows, turn_at(offset_ref, rows))
            found.append(layer_turn(pair, layer_ref, step, block, dest_ref[0] * here + at))
        for c in range(2):
            biggest = functools.reduce(jnp.maximum, [jnp.abs(part[c]) for pair in found for part in pair])
            code = scale_code(jnp.max(biggest, axis=0, keepdims=True))
            inverse = inverse_scale_of(code)
            row = at * 2 + c
            for block, pair in enumerate(found):
                words = packed(coded(pair[0][c], inverse), coded(pair[1][c], inverse))
                out_ref[pl.ds(block * tall * 2 * here + row, tall, 2 * here), :] = words
            out_ref[pl.ds(HALF * 2 * here + row, 1), :] = code


def result_kernel(freq_ref, code_ref, *rest):
    out_ref = rest[-1]
    per, tall = out_ref.shape[1:3]
    scale = scale_of(code_ref[per * tall :])[None]
    for half in range(2):

        @pl.when(pl.program_id(0) == half)
        def _():
            out_ref[0] = unpacked(code_ref[: per * tall].reshape(per, tall, BLK))[half] * scale


def take_kernel(mine_ref, counts_ref, source_ref, out_ref, sems):
    taken, entries = out_ref.shape[0], source_ref.shape[1]
    bins_here, stride = source_ref.shape[0], source_ref.shape[0] * entries // taken
    copies = []
    for n in range(taken):
        entry, bin_at = n * stride + mine_ref[0], 0
        for b in range(bins_here - 1):
            over = (bin_at == b) & (entry >= counts_ref[b])
            entry = jnp.where(over, entry - counts_ref[b], entry)
            bin_at = jnp.where(over, b + 1, bin_at)
        entry = jnp.minimum(entry, entries - 1)
        copies.append(
            pltpu.make_async_copy(source_ref.at[bin_at, entry], out_ref.at[n], sems.at[n])
        )
        copies[-1].start()
    for copy in copies:
        copy.wait()


def slot_lists(counts_all, targets_all, bins_local, fl, per_device, room):
    offs = counts_all.shape[0] // bins_local
    entries = targets_all.shape[1]
    counts_in = counts_all.reshape(offs, bins_local)
    live = jnp.sum(counts_in, axis=1)
    quarter = jnp.arange(fl, dtype=jnp.int32)
    held = (live[None, :] - quarter[:, None] + fl - 1) // fl
    upto = jnp.sum(
        jnp.where(jnp.arange(offs)[None, :] <= jnp.arange(offs)[:, None], held[:, None, :], 0), axis=2
    )
    at = jnp.arange(room, dtype=jnp.int32)
    past = (at[None, :, None] >= upto[:, None, :]).astype(jnp.int32)
    off_at = jnp.sum(past, axis=2)
    valid = off_at < offs
    off_at = jnp.minimum(off_at, offs - 1)
    start = jnp.sum(past * held[:, None, :], axis=2)
    nth = jnp.clip(at[None, :] - start, 0, per_device - 1)
    entry = nth * fl + quarter[:, None]
    bin_at = off_at * bins_local
    mine = off_at[:, :, None] == jnp.arange(offs)[None, None, :]
    for b in range(bins_local - 1):
        size = jnp.sum(jnp.where(mine, counts_in[None, None, :, b], 0), axis=2)
        over = (bin_at == off_at * bins_local + b) & (entry >= size)
        bin_at = bin_at + over
        entry = entry - jnp.where(over, size, 0)
    flat = bin_at * entries + entry
    total = targets_all.size
    picks = flat[:, :, None] == jnp.arange(total)[None, None, :]
    target = jnp.sum(jnp.where(picks, targets_all.reshape(1, 1, total), 0), axis=2)
    target = jnp.where(valid, target, -1)
    return off_at, nth, bin_at, target


def local(bins_data, operators, targets, counts, layer_index, slowness):
    off_count = lax.axis_size("off")
    mid_count = lax.axis_size("mid")
    bins_local, freq_total, _, mid_local = bins_data.shape
    entries = operators.shape[1]
    bins_total = bins_local * off_count
    fl = freq_total // off_count
    total_mid = mid_local * mid_count
    outer = total_mid // BLK
    mid_at, off_at = lax.axis_index("mid"), lax.axis_index("off")
    assert mid_count % fl == 0 and (bins_local * entries) % fl == 0
    mine = mid_at % fl
    rounds = mid_count // fl
    groups = (
        None if rounds == 1 else [list(range(g * fl, (g + 1) * fl)) for g in range(rounds)]
    )

    per_device = bins_local * entries // fl
    smem = pl.BlockSpec(memory_space=pltpu.SMEM)
    vmem = pl.BlockSpec(memory_space=pltpu.VMEM)
    hbm = pl.BlockSpec(memory_space=pl.ANY)
    own = pl.pallas_call(
        take_kernel,
        in_specs=[smem, smem, hbm],
        out_specs=vmem,
        out_shape=jax.ShapeDtypeStruct((per_device, BLK, BLK), jnp.bfloat16),
        scratch_shapes=[pltpu.SemaphoreType.DMA((per_device,))],
        compiler_params=pltpu.CompilerParams(vmem_limit_bytes=SMALL),
        name="take_own",
    )(mine.reshape(1), counts, operators)
    bins_data, own = lax.optimization_barrier((bins_data, own))
    cores = 2 if off_count % 2 == 0 else 1
    line = off_count // cores
    assert line & (line - 1) == 0 and fl & (fl - 1) == 0
    shares = [own]
    for away in range(1, line):
        low = away & -away
        shares.append(
            lax.ppermute(
                shares[away ^ low],
                "off",
                [(i, (i // cores ^ low) * cores + i % cores) for i in range(off_count)],
            )
        )
    if cores > 1:
        shares += [lax.ppermute(x, "off", [(i, i ^ 1) for i in range(off_count)]) for x in shares]

    pairs = fl * 2

    def extra(whole_numbers, copies):
        flat = whole_numbers.astype(jnp.bfloat16).reshape(1, 1, 1, -1)
        flat = jnp.pad(flat, ((0, 0), (0, 0), (0, pairs - 1), (0, mid_local - flat.shape[3])))
        return jnp.broadcast_to(flat, (1, copies, pairs, mid_local))

    lists = jnp.concatenate([counts[:, None], targets], axis=1)
    data = bins_data.reshape(bins_local, off_count, pairs, mid_local)
    data = jnp.concatenate([data, extra(lists, off_count)], axis=0)
    data = lax.all_to_all(data, "off", split_axis=1, concat_axis=0, tiled=True)

    data = data.reshape(off_count, bins_local + 1, pairs, mid_local)
    lists = data[:, bins_local, 0, : lists.size].astype(jnp.int32).reshape(bins_total, 1 + entries)
    data = data[:, :bins_local].reshape(bins_total, pairs, mid_local)
    data = jnp.concatenate([data, extra(layer_index, 1)[0]], axis=0)
    assert mid_count & (mid_count - 1) == 0
    parts = [data] + [
        lax.ppermute(data, "mid", [(i, i ^ away) for i in range(mid_count)])
        for away in range(mid_count - 1, 0, -1)
    ]
    data = jnp.stack(parts[:1] + parts[:0:-1])
    partner = jnp.arange(mid_count, dtype=jnp.int32) ^ mid_at
    layers = data[:, bins_total, 0, : layer_index.size].astype(jnp.int32)
    layers = jnp.sum(
        jnp.where((partner[:, None] == jnp.arange(mid_count))[:, :, None], layers[None], 0), axis=1
    )
    layers = layers.reshape(mid_count, *layer_index.shape).transpose(1, 2, 0, 3)
    layers = layers.reshape(*layer_index.shape[:2], outer)
    data = data[:, :bins_total].reshape(mid_count, bins_total, pairs, mid_local // BLK, BLK)
    data = data.transpose(1, 2, 0, 3, 4).reshape(bins_total, pairs * outer, BLK)
    order = (partner[:, None] * (mid_local // BLK) + jnp.arange(mid_local // BLK)).reshape(outer)

    live_total = bins_total * entries // 2
    room = -(-(live_total + (fl - 1) * off_count) // fl)
    room = min(-(-room // GROUP) * GROUP, per_device * off_count)
    offs, nth, bins, goal = slot_lists(lists[:, 0], lists[:, 1:], bins_local, fl, per_device, room)
    side = (offs % cores != off_at % cores).astype(jnp.int32) * line
    slots = (side + ((offs // cores) ^ (off_at // cores))) * per_device + nth
    source = jnp.arange(fl, dtype=jnp.int32) ^ mine
    goal = jnp.sum(jnp.where((source[:, None] == jnp.arange(fl))[:, :, None], goal[None], 0), axis=1)
    pick = (
        jnp.tile(goal.reshape(1, fl * room), (1, 2))
        == lax.broadcasted_iota(jnp.int32, (NH, 2 * fl * room), 0)
    ).astype(jnp.float32)
    own_slots = lax.dynamic_index_in_dim(slots, mine, 0, False)
    own_bins = lax.dynamic_index_in_dim(bins, mine, 0, False)
    list_groups = room // GROUP
    data, order, own_slots, own_bins, layers, pick = lax.optimization_barrier(
        (data, order, own_slots, own_bins, layers, pick)
    )
    shape = jax.ShapeDtypeStruct((list_groups, outer + 1, GROUP, BLK), jnp.int32)
    terms = pl.pallas_call(
        functools.partial(contribution_kernel, freqs=fl),
        in_specs=[smem, smem, smem, smem, vmem] + [hbm] * len(shares),
        out_specs=[vmem] * fl,
        out_shape=[shape] * fl,
        scratch_shapes=[
            pltpu.VMEM((fl * 2 * outer * GROUP, BLK), jnp.float32),
            pltpu.VMEM((len(shares) * per_device, BLK, BLK), jnp.bfloat16),
            pltpu.SemaphoreType.DMA((len(shares),)),
        ],
        compiler_params=pltpu.CompilerParams(vmem_limit_bytes=SMALL),
        name="contributions",
    )(mine.reshape(1), order, own_slots, own_bins, data, *shares)
    terms, freq_at = lax.optimization_barrier((terms, off_at * fl + mine))
    got = {0: terms[0]}
    for away in range(fl - 1, 0, -1):
        got[away] = lax.ppermute(terms[away], "mid", [(i, i ^ away) for i in range(mid_count)])
    terms = [got[away] for away in range(fl)]

    omega = math.pi * (0.1 + 0.8 * (freq_at.astype(jnp.float32) + 0.5) / freq_total)
    phase_real, phase_imag, layer_turns = pl.pallas_call(
        propagator_kernel,
        in_specs=[smem, smem, vmem],
        out_specs=[vmem] * 3,
        out_shape=[jax.ShapeDtypeStruct((NH, total_mid), jnp.float32)] * 2
        + [jax.ShapeDtypeStruct((2, *layers.shape), jnp.float32)],
        compiler_params=pltpu.CompilerParams(vmem_limit_bytes=SMALL),
        cost_estimate=pl.CostEstimate(
            flops=60 * NH * total_mid, bytes_accessed=8 * NH * total_mid, transcendentals=10 * NH * total_mid
        ),
        name="propagator",
    )(omega.reshape(1), slowness, layers)

    middle, offset_turn = twiddle_tables(outer)
    here = mid_local // BLK
    rows_out = (HALF + 1) * 2 * here
    tables = [jnp.asarray(t) for t in block_tables()]
    middle, offset_turn = jnp.asarray(middle), jnp.asarray(offset_turn)
    plane = pl.pallas_call(
        functools.partial(march_kernel, sources=fl),
        in_specs=[smem] + [vmem] * (fl + 9),
        out_specs=vmem,
        out_shape=jax.ShapeDtypeStruct((2, 2, HALF, total_mid), jnp.float32),
        scratch_shapes=[
            pltpu.VMEM((2, 2, HALF, total_mid), jnp.float32),
            pltpu.VMEM((fl * room, BLK), jnp.float32),
            *[pltpu.VMEM((2 * NH, 2 * BLK), jnp.float32)] * 4,
            *[pltpu.VMEM((ROWS * CHUNKS * outer, 4 * BLK), jnp.float32)] * 4,
            *[pltpu.VMEM((2 * fl * room, 2 * BLK), jnp.float32)] * 2,
        ],
        compiler_params=pltpu.CompilerParams(vmem_limit_bytes=VMEM),
        name="march",
    )(layer_turns, *terms, pick, phase_real, phase_imag, *tables, middle, offset_turn)

    def finish(dest, *before):
        return pl.pallas_call(
            finish_kernel,
            grid_spec=pltpu.PrefetchScalarGridSpec(
                num_scalar_prefetch=1,
                grid=(1,),
                in_specs=[
                    smem,
                    pl.BlockSpec((2, 2, HALF, mid_local), lambda i, dest: (0, 0, 0, dest[0])),
                    vmem,
                    vmem,
                ]
                + [hbm] * len(before),
                out_specs=pl.BlockSpec((rows_out, BLK), lambda i, dest: (0, 0)),
                scratch_shapes=[pltpu.VMEM((2 * NH, 2 * mid_local), jnp.float32)],
            ),
            out_shape=jax.ShapeDtypeStruct((rows_out, BLK), jnp.int32),
            cost_estimate=pl.CostEstimate(
                flops=6 * NH * NH * 2 * BLK * here, bytes_accessed=6 * NH * mid_local, transcendentals=0
            ),
            compiler_params=pltpu.CompilerParams(vmem_limit_bytes=SMALL),
            name="finish",
        )(dest.reshape(1), layer_turns, plane, tables[1], offset_turn, *before)

    got, before = {}, []
    for ahead in [*range(fl - 1, 0, -1), 0]:
        dest = (mid_at // fl) * fl + (mine ^ ahead)
        block = finish(dest, *before)
        before = [block]
        if ahead:
            block = lax.ppermute(block, "mid", [(s, s ^ ahead) for s in range(mid_count)])
        got[ahead] = block

    field = None
    for ahead in [0, *range(fl - 1, 0, -1)]:
        freq = mine ^ ahead
        first = field is None
        field = pl.pallas_call(
            result_kernel,
            grid_spec=pltpu.PrefetchScalarGridSpec(
                num_scalar_prefetch=1,
                grid=(2,),
                in_specs=[vmem] if first else [vmem, hbm],
                out_specs=pl.BlockSpec((1, HALF, 2 * here, BLK), lambda i, f: (f[0], i, 0, 0)),
            ),
            out_shape=jax.ShapeDtypeStruct((fl, NH, 2 * here, BLK), jnp.float32),
            input_output_aliases={} if first else {2: 0},
            compiler_params=pltpu.CompilerParams(vmem_limit_bytes=SMALL),
            cost_estimate=pl.CostEstimate(
                flops=4 * NH * mid_local, bytes_accessed=12 * NH * mid_local, transcendentals=0
            ),
            name="result",
        )(freq.reshape(1), got[ahead], *([] if first else [field]))
    field = field.reshape(fl, NH, here, 2, BLK).transpose(0, 1, 3, 2, 4)
    return field.reshape(fl, NH, 2, mid_local)


def solution(mesh):
    in_specs = (
        P("off", None, None, "mid"),
        P("off", None, None, None),
        P("off", None),
        P("off"),
        P(None, None, "mid"),
        P(),
    )
    out_specs = P("off", None, None, "mid")
    return jax.shard_map(local, mesh=mesh, in_specs=in_specs, out_specs=out_specs, check_vma=False)
```

```python
import functools
import math

import jax
import jax.numpy as jnp
import numpy as np
from jax import lax
from jax.experimental import pallas as pl
from jax.experimental.pallas import tpu as pltpu
from jax.sharding import PartitionSpec as P

NH = 256
BLK = 128

dz_cells = 2.0
damping = 0.1

HALF = NH // 2
STEP_LOG = 64.0
TOP = 32767.0
GROUP = 8
COLUMNS = 2
ROWS = 8
CHUNKS = 4
UNROLL = 2
VMEM = 28 * 1024 * 1024
SMALL = 10 * 1024 * 1024


def signed_wave(index, length):
    signed = (index + length // 2) % length - length // 2
    return signed.astype(jnp.float32) * (2.0 * math.pi / length)


def root_pair(level):
    magnitude = jnp.sqrt(level * level + damping * damping)
    larger = jnp.sqrt(0.5 * (magnitude + jnp.abs(level)))
    smaller = damping / (2.0 * larger)
    return (jnp.where(level >= 0, larger, smaller), jnp.where(level >= 0, smaller, larger))


def propagator(omega_sq, mid_wave, offset_wave):
    source = 0.5 * (mid_wave - offset_wave)
    receiver = 0.5 * (mid_wave + offset_wave)
    real_s, imag_s = root_pair(omega_sq - source * source)
    real_r, imag_r = root_pair(omega_sq - receiver * receiver)
    decay = jnp.exp(-dz_cells * (imag_s + imag_r))
    turn = dz_cells * (real_s + real_r)
    return (decay * jnp.cos(turn), decay * jnp.sin(turn))


def halves_np(table):
    high = table.astype(np.float32).astype(jnp.bfloat16)
    low = (table - high.astype(np.float64)).astype(np.float32).astype(jnp.bfloat16)
    return high, low


def block_tables():
    index = np.arange(BLK)
    angles = 2.0 * np.pi * (np.outer(index, index) % BLK) / BLK
    cos, sin = np.cos(angles), np.sin(angles)
    upper = np.block([[cos, sin], [-sin, cos]])
    lower = np.block([[cos, -sin], [sin, cos]])
    tables = []
    for axis, pair in ((1, (upper, lower)), (0, (lower, upper))):
        for table in pair:
            high, low = halves_np(table)
            tables.append(np.concatenate([high, high, low], axis=axis))
    return tables


def twiddle_tables(outer):
    ka, b = np.arange(outer)[:, None], np.arange(BLK)[None, :]
    angles = 2.0 * np.pi * ka * b / (outer * BLK)
    middle = np.stack([np.cos(angles), np.sin(angles)]).astype(np.float32)
    rows = 2.0 * np.pi * np.arange(HALF) / NH
    offset = np.stack([np.cos(rows), np.sin(rows)]).astype(np.float32)
    return middle, np.broadcast_to(offset[:, :, None], (2, HALF, BLK)).copy()


def halves(value):
    high = value.astype(jnp.bfloat16)
    return high, (value - high.astype(jnp.float32)).astype(jnp.bfloat16)


def dot(left, right):
    return jnp.dot(left, right, preferred_element_type=jnp.float32)


def left_product(table, value):
    high, low = halves(value)
    return dot(table, jnp.concatenate([high, low, high], axis=0))


def right_product(value, table):
    high, low = halves(value)
    return dot(jnp.concatenate([high, low, high], axis=1), table)


def cmul(real_a, imag_a, real_b, imag_b):
    return real_a * real_b - imag_a * imag_b, real_a * imag_b + imag_a * real_b


def small_transform(values, sign):
    count = len(values)
    if count == 1:
        return values
    even = small_transform(values[0::2], sign)
    odd = small_transform(values[1::2], sign)
    first, second = [], []
    for k in range(count // 2):
        er, ei = even[k]
        xr, xi = odd[k]
        if k == 0:
            tr, ti = xr, xi
        elif 4 * k == count:
            tr, ti = (-xi, xr) if sign > 0 else (xi, -xr)
        else:
            c, s = math.cos(2 * math.pi * k / count), sign * math.sin(2 * math.pi * k / count)
            if 8 * k == count:
                tr, ti = ((xr - xi) * c, (xr + xi) * c) if sign > 0 else ((xr + xi) * c, (xi - xr) * c)
            elif 8 * k == 3 * count:
                tr, ti = ((xr + xi) * c, (xi - xr) * c) if sign > 0 else ((xr - xi) * c, (xr + xi) * c)
            else:
                tr, ti = xr * c - xi * s, xr * s + xi * c
        first.append((er + tr, ei + ti))
        second.append((er - tr, ei - ti))
    return first + second


def scale_code(biggest):
    return (jnp.floor(jnp.log(jnp.maximum(biggest, 1e-30)) * STEP_LOG) + 1.0).astype(jnp.int32)


def scale_of(code):
    return jnp.exp(code.astype(jnp.float32) * (1.0 / STEP_LOG)) * (1.0 / TOP)


def inverse_scale_of(code):
    return jnp.exp(code.astype(jnp.float32) * (-1.0 / STEP_LOG)) * TOP


def coded(value, inverse):
    return jnp.floor(value * inverse + 0.5).astype(jnp.int32)


def packed(high, low):
    return (high << 16) | (low & 0xFFFF)


def unpacked(word):
    return (word >> 16).astype(jnp.float32), ((word << 16) >> 16).astype(jnp.float32)


def contribution_kernel(place_ref, order_ref, slot_ref, bin_ref, data_ref, *rest, freqs):
    *sources, held, weight_ref, sems = rest
    sources, outs = sources[:-freqs], sources[-freqs:]
    groups, outer = outs[0].shape[0], outs[0].shape[1] - 1
    count = sources[0].shape[0]
    copies = [
        pltpu.make_async_copy(ref, weight_ref.at[pl.ds(n * count, count)], sems.at[n])
        for n, ref in enumerate(sources)
    ]
    for copy in copies:
        copy.start()
    for copy in copies:
        copy.wait()

    @pl.loop(0, groups)
    def _(group):
        for at in range(GROUP):
            slot = slot_ref[group * GROUP + at]
            source = bin_ref[group * GROUP + at]
            held[pl.ds(at, data_ref.shape[1], GROUP), :] = dot(data_ref[source], weight_ref[slot])
        for away, out_ref in enumerate(outs):
            base = (place_ref[0] ^ away) * (2 * outer * GROUP)

            def term(at):
                return held[pl.ds(pl.multiple_of(base + at * GROUP, GROUP), GROUP), :]

            biggest = functools.reduce(jnp.maximum, [jnp.abs(term(at)) for at in range(2 * outer)])
            code = scale_code(biggest)
            inverse = inverse_scale_of(code)
            for a in range(outer):
                words = packed(coded(term(a), inverse), coded(term(outer + a), inverse))
                out_ref[group, order_ref[a]] = words
            out_ref[group, outer] = code


def column_of(plane, a):
    lanes = pl.ds(pl.multiple_of(a * BLK, BLK), BLK)
    return jnp.concatenate(
        [
            jnp.concatenate([plane[p, 0, :, lanes], plane[p, 1, :, lanes]], axis=0)
            for p in range(2)
        ],
        axis=1,
    )


def store_column(plane, a, value):
    lanes = pl.ds(pl.multiple_of(a * BLK, BLK), BLK)
    for p in range(2):
        for c in range(2):
            plane[p, c, :, lanes] = value[c * HALF : (c + 1) * HALF, p * BLK : (p + 1) * BLK]


def row_blocks(tall):
    return [slice(at * tall, (at + 1) * tall) for at in range(HALF // tall)]


def turn_at(offset_ref, rows):
    return offset_ref[0, rows], offset_ref[1, rows]


def forward_rows(low, high, turn):
    first = low[0] + high[0], low[1] + high[1]
    second = cmul(low[0] - high[0], low[1] - high[1], turn[0], -turn[1])
    return (*first, *second)


def inverse_rows(value, rows, turn):
    upper, below = rows, slice(HALF + rows.start, HALF + rows.stop)
    first = value[upper, :BLK], value[below, :BLK]
    second = cmul(value[upper, BLK:], value[below, BLK:], turn[0], turn[1])
    low = first[0] + second[0], first[1] + second[1]
    high = first[0] - second[0], first[1] - second[1]
    return low, high


def assembled(blocks):
    parts = [jnp.concatenate(part, axis=0) for part in zip(*blocks)]
    return jnp.concatenate(
        [jnp.concatenate(parts[:2], axis=0), jnp.concatenate(parts[2:], axis=0)], axis=1
    )


def propagator_kernel(omega_ref, slow_ref, layers_ref, real_ref, imag_ref, turns_ref):
    steps, layer_total = slow_ref.shape
    for step in range(steps):
        layers = layers_ref[step]
        slow = functools.reduce(
            jnp.add, [jnp.where(layers == n, slow_ref[step, n], 0.0) for n in range(layer_total)]
        )
        turn = 2.0 * dz_cells * omega_ref[0] * (slow - 1.0)
        turns_ref[0, step] = jnp.cos(turn)
        turns_ref[1, step] = jnp.sin(turn)

    total = real_ref.shape[1]
    scale = 1.0 / (NH * total)
    omega_sq = omega_ref[0] * omega_ref[0]

    @pl.loop(0, NH // GROUP)
    def _(at):
        start = pl.multiple_of(at * GROUP, GROUP)
        row = lax.broadcasted_iota(jnp.int32, (GROUP, BLK), 0) + at * GROUP
        lane = lax.broadcasted_iota(jnp.int32, (GROUP, BLK), 1)
        offset_wave = signed_wave(2 * (row % HALF) + row // HALF, NH)
        for a in range(total // BLK):
            mid_wave = signed_wave(a + total // BLK * lane, total)
            real, imag = propagator(omega_sq, mid_wave, offset_wave)
            real_ref[pl.ds(start, GROUP), a * BLK : (a + 1) * BLK] = real * scale
            imag_ref[pl.ds(start, GROUP), a * BLK : (a + 1) * BLK] = imag * scale


def offset_product(table, columns):
    value = left_product(table[...], jnp.concatenate(columns, axis=1))
    return [value[:, n * 2 * BLK : (n + 1) * 2 * BLK] for n in range(len(columns))]


def layer_turn(pair, layer_ref, step, block, a):
    half = layer_ref.shape[2] // 2
    return [
        cmul(*part, layer_ref[0, step, block + p * half, a], layer_ref[1, step, block + p * half, a])
        for p, part in enumerate(pair)
    ]


def midpoint_pass(plane, out, phase_refs, forward, inverse, middle_ref):
    outer = middle_ref.shape[1]
    lanes = [slice(a * BLK, (a + 1) * BLK) for a in range(outer)]
    tall = ROWS * CHUNKS
    per_half = HALF // tall

    @pl.loop(0, 2 * per_half, unroll=UNROLL)
    def _(at):
        p = at // per_half
        base = pl.multiple_of((at % per_half) * tall, tall)
        phase_base = pl.multiple_of(at * tall, tall)

        def gathered(pieces):
            return jnp.concatenate([jnp.concatenate(pair, axis=1) for pair in pieces], axis=0)

        pieces = []
        for chunk in range(CHUNKS):
            here = pl.ds(base + chunk * ROWS, ROWS)
            values = [(plane[p, 0, here, lane], plane[p, 1, here, lane]) for lane in lanes]
            values = small_transform(values, -1)
            for a in range(outer):
                pieces.append(cmul(*values[a], middle_ref[0, a : a + 1], -middle_ref[1, a : a + 1]))
        value = right_product(gathered(pieces), forward[...])
        pieces = []
        for chunk in range(CHUNKS):
            there = pl.ds(phase_base + chunk * ROWS, ROWS)
            for a in range(outer):
                row = (chunk * outer + a) * ROWS
                part = value[row : row + ROWS]
                pieces.append(
                    cmul(
                        part[:, :BLK], part[:, BLK:],
                        phase_refs[0][there, lanes[a]], phase_refs[1][there, lanes[a]],
                    )
                )
        value = right_product(gathered(pieces), inverse[...])
        for chunk in range(CHUNKS):
            here = pl.ds(base + chunk * ROWS, ROWS)
            values = []
            for a in range(outer):
                row = (chunk * outer + a) * ROWS
                part = value[row : row + ROWS]
                values.append(
                    cmul(part[:, :BLK], part[:, BLK:], middle_ref[0, a : a + 1], middle_ref[1, a : a + 1])
                )
            values = small_transform(values, 1)
            for a in range(outer):
                out[p, 0, here, lanes[a]] = values[a][0]
                out[p, 1, here, lanes[a]] = values[a][1]


def march_kernel(layer_ref, *rest, sources):
    code_refs, rest = rest[:sources], rest[sources:]
    (
        pick_ref, phase_real, phase_imag, rows_forward, rows_inverse, lanes_forward, lanes_inverse,
        middle_ref, offset_ref, other, plane, scales,
    ) = rest
    groups = code_refs[0].shape[0]
    outer = middle_ref.shape[1]
    steps = layer_ref.shape[1]
    tall = NH // layer_ref.shape[2]

    def words(a):
        return jnp.concatenate([ref[:, a].reshape(groups * GROUP, BLK) for ref in code_refs], axis=0)

    scales[...] = scale_of(words(outer))

    @pl.loop(0, outer // COLUMNS, unroll=2)
    def _(at):
        columns = []
        for a in range(COLUMNS):
            real, imag = unpacked(words(at * COLUMNS + a))
            scale = scales[...]
            value = jnp.concatenate([real * scale, imag * scale], axis=1)
            moved = dot(pick_ref[...], jnp.concatenate(halves(value), axis=0))
            blocks = []
            for rows in row_blocks(tall):
                low, high = moved[rows], moved[HALF + rows.start : HALF + rows.stop]
                blocks.append(
                    forward_rows(
                        (low[:, :BLK], low[:, BLK:]), (high[:, :BLK], high[:, BLK:]),
                        turn_at(offset_ref, rows),
                    )
                )
            columns.append(assembled(blocks))
        for a, value in enumerate(offset_product(rows_forward, columns)):
            store_column(plane, at * COLUMNS + a, value)

    for step in range(steps):
        midpoint_pass(plane, other, (phase_real, phase_imag), lanes_forward, lanes_inverse, middle_ref)
        if step < steps - 1:

            @pl.loop(0, outer // COLUMNS, unroll=2)
            def _(at):
                places = [at * COLUMNS + a for a in range(COLUMNS)]
                columns = []
                for a, value in zip(
                    places, offset_product(rows_inverse, [column_of(other, a) for a in places])
                ):
                    blocks = []
                    for block, rows in enumerate(row_blocks(tall)):
                        turn = turn_at(offset_ref, rows)
                        pair = inverse_rows(value, rows, turn)
                        blocks.append(forward_rows(*layer_turn(pair, layer_ref, step, block, a), turn))
                    columns.append(assembled(blocks))
                for a, value in zip(places, offset_product(rows_forward, columns)):
                    store_column(plane, a, value)


def finish_kernel(dest_ref, layer_ref, plane_ref, rows_inverse, offset_ref, *rest):
    out_ref = rest[-1]
    here = plane_ref.shape[3] // BLK
    tall = NH // layer_ref.shape[2]
    step = layer_ref.shape[1] - 1
    columns = offset_product(rows_inverse, [column_of(plane_ref, at) for at in range(here)])
    for at in range(here):
        found = []
        for block, rows in enumerate(row_blocks(tall)):
            pair = inverse_rows(columns[at], rows, turn_at(offset_ref, rows))
            found.append(layer_turn(pair, layer_ref, step, block, dest_ref[0] * here + at))
        for c in range(2):
            biggest = functools.reduce(jnp.maximum, [jnp.abs(part[c]) for pair in found for part in pair])
            code = scale_code(jnp.max(biggest, axis=0, keepdims=True))
            inverse = inverse_scale_of(code)
            row = at * 2 + c
            for block, pair in enumerate(found):
                words = packed(coded(pair[0][c], inverse), coded(pair[1][c], inverse))
                out_ref[pl.ds(block * tall * 2 * here + row, tall, 2 * here), :] = words
            out_ref[pl.ds(HALF * 2 * here + row, 1), :] = code


def result_kernel(freq_ref, code_ref, *rest):
    out_ref = rest[-1]
    per, tall = out_ref.shape[1:3]
    scale = scale_of(code_ref[per * tall :])[None]
    for half in range(2):

        @pl.when(pl.program_id(0) == half)
        def _():
            out_ref[0] = unpacked(code_ref[: per * tall].reshape(per, tall, BLK))[half] * scale


def take_kernel(mine_ref, counts_ref, source_ref, out_ref, sems):
    taken, entries = out_ref.shape[0], source_ref.shape[1]
    bins_here, stride = source_ref.shape[0], source_ref.shape[0] * entries // taken
    copies = []
    for n in range(taken):
        entry, bin_at = n * stride + mine_ref[0], 0
        for b in range(bins_here - 1):
            over = (bin_at == b) & (entry >= counts_ref[b])
            entry = jnp.where(over, entry - counts_ref[b], entry)
            bin_at = jnp.where(over, b + 1, bin_at)
        entry = jnp.minimum(entry, entries - 1)
        copies.append(
            pltpu.make_async_copy(source_ref.at[bin_at, entry], out_ref.at[n], sems.at[n])
        )
        copies[-1].start()
    for copy in copies:
        copy.wait()


def slot_lists(counts_all, targets_all, bins_local, fl, per_device, room):
    offs = counts_all.shape[0] // bins_local
    entries = targets_all.shape[1]
    counts_in = counts_all.reshape(offs, bins_local)
    live = jnp.sum(counts_in, axis=1)
    quarter = jnp.arange(fl, dtype=jnp.int32)
    held = (live[None, :] - quarter[:, None] + fl - 1) // fl
    upto = jnp.sum(
        jnp.where(jnp.arange(offs)[None, :] <= jnp.arange(offs)[:, None], held[:, None, :], 0), axis=2
    )
    at = jnp.arange(room, dtype=jnp.int32)
    past = (at[None, :, None] >= upto[:, None, :]).astype(jnp.int32)
    off_at = jnp.sum(past, axis=2)
    valid = off_at < offs
    off_at = jnp.minimum(off_at, offs - 1)
    start = jnp.sum(past * held[:, None, :], axis=2)
    nth = jnp.clip(at[None, :] - start, 0, per_device - 1)
    entry = nth * fl + quarter[:, None]
    bin_at = off_at * bins_local
    mine = off_at[:, :, None] == jnp.arange(offs)[None, None, :]
    for b in range(bins_local - 1):
        size = jnp.sum(jnp.where(mine, counts_in[None, None, :, b], 0), axis=2)
        over = (bin_at == off_at * bins_local + b) & (entry >= size)
        bin_at = bin_at + over
        entry = entry - jnp.where(over, size, 0)
    flat = bin_at * entries + entry
    total = targets_all.size
    picks = flat[:, :, None] == jnp.arange(total)[None, None, :]
    target = jnp.sum(jnp.where(picks, targets_all.reshape(1, 1, total), 0), axis=2)
    target = jnp.where(valid, target, -1)
    return off_at, nth, bin_at, target


def local(bins_data, operators, targets, counts, layer_index, slowness):
    off_count = lax.axis_size("off")
    mid_count = lax.axis_size("mid")
    bins_local, freq_total, _, mid_local = bins_data.shape
    entries = operators.shape[1]
    bins_total = bins_local * off_count
    fl = freq_total // off_count
    total_mid = mid_local * mid_count
    outer = total_mid // BLK
    mid_at, off_at = lax.axis_index("mid"), lax.axis_index("off")
    assert mid_count % fl == 0 and (bins_local * entries) % fl == 0
    mine = mid_at % fl
    rounds = mid_count // fl
    groups = (
        None if rounds == 1 else [list(range(g * fl, (g + 1) * fl)) for g in range(rounds)]
    )

    per_device = bins_local * entries // fl
    smem = pl.BlockSpec(memory_space=pltpu.SMEM)
    vmem = pl.BlockSpec(memory_space=pltpu.VMEM)
    hbm = pl.BlockSpec(memory_space=pl.ANY)
    own = pl.pallas_call(
        take_kernel,
        in_specs=[smem, smem, hbm],
        out_specs=vmem,
        out_shape=jax.ShapeDtypeStruct((per_device, BLK, BLK), jnp.bfloat16),
        scratch_shapes=[pltpu.SemaphoreType.DMA((per_device,))],
        compiler_params=pltpu.CompilerParams(vmem_limit_bytes=SMALL),
        name="take_own",
    )(mine.reshape(1), counts, operators)
    bins_data, own = lax.optimization_barrier((bins_data, own))
    cores = 2 if off_count % 2 == 0 else 1
    line = off_count // cores
    assert line & (line - 1) == 0 and fl & (fl - 1) == 0
    shares = [own]
    for away in range(1, line):
        low = away & -away
        shares.append(
            lax.ppermute(
                shares[away ^ low],
                "off",
                [(i, (i // cores ^ low) * cores + i % cores) for i in range(off_count)],
            )
        )
    if cores > 1:
        shares += [lax.ppermute(x, "off", [(i, i ^ 1) for i in range(off_count)]) for x in shares]

    pairs = fl * 2

    def extra(whole_numbers, copies):
        flat = whole_numbers.astype(jnp.bfloat16).reshape(1, 1, 1, -1)
        flat = jnp.pad(flat, ((0, 0), (0, 0), (0, pairs - 1), (0, mid_local - flat.shape[3])))
        return jnp.broadcast_to(flat, (1, copies, pairs, mid_local))

    lists = jnp.concatenate([counts[:, None], targets], axis=1)
    data = bins_data.reshape(bins_local, off_count, pairs, mid_local)
    data = jnp.concatenate([data, extra(lists, off_count)], axis=0)
    data = lax.all_to_all(data, "off", split_axis=1, concat_axis=0, tiled=True)

    data = data.reshape(off_count, bins_local + 1, pairs, mid_local)
    lists = data[:, bins_local, 0, : lists.size].astype(jnp.int32).reshape(bins_total, 1 + entries)
    data = data[:, :bins_local].reshape(bins_total, pairs, mid_local)
    data = jnp.concatenate([data, extra(layer_index, 1)[0]], axis=0)
    assert mid_count & (mid_count - 1) == 0
    parts = [data] + [
        lax.ppermute(data, "mid", [(i, i ^ away) for i in range(mid_count)])
        for away in range(mid_count - 1, 0, -1)
    ]
    data = jnp.stack(parts[:1] + parts[:0:-1])
    partner = jnp.arange(mid_count, dtype=jnp.int32) ^ mid_at
    layers = data[:, bins_total, 0, : layer_index.size].astype(jnp.int32)
    layers = jnp.sum(
        jnp.where((partner[:, None] == jnp.arange(mid_count))[:, :, None], layers[None], 0), axis=1
    )
    layers = layers.reshape(mid_count, *layer_index.shape).transpose(1, 2, 0, 3)
    layers = layers.reshape(*layer_index.shape[:2], outer)
    data = data[:, :bins_total].reshape(mid_count, bins_total, pairs, mid_local // BLK, BLK)
    data = data.transpose(1, 2, 0, 3, 4).reshape(bins_total, pairs * outer, BLK)
    order = (partner[:, None] * (mid_local // BLK) + jnp.arange(mid_local // BLK)).reshape(outer)

    live_total = bins_total * entries // 2
    room = -(-(live_total + (fl - 1) * off_count) // fl)
    room = min(-(-room // GROUP) * GROUP, per_device * off_count)
    offs, nth, bins, goal = slot_lists(lists[:, 0], lists[:, 1:], bins_local, fl, per_device, room)
    side = (offs % cores != off_at % cores).astype(jnp.int32) * line
    slots = (side + ((offs // cores) ^ (off_at // cores))) * per_device + nth
    source = jnp.arange(fl, dtype=jnp.int32) ^ mine
    goal = jnp.sum(jnp.where((source[:, None] == jnp.arange(fl))[:, :, None], goal[None], 0), axis=1)
    pick = (
        jnp.tile(goal.reshape(1, fl * room), (1, 2))
        == lax.broadcasted_iota(jnp.int32, (NH, 2 * fl * room), 0)
    ).astype(jnp.bfloat16)
    own_slots = lax.dynamic_index_in_dim(slots, mine, 0, False)
    own_bins = lax.dynamic_index_in_dim(bins, mine, 0, False)
    list_groups = room // GROUP
    data, order, own_slots, own_bins, layers, pick = lax.optimization_barrier(
        (data, order, own_slots, own_bins, layers, pick)
    )
    shape = jax.ShapeDtypeStruct((list_groups, outer + 1, GROUP, BLK), jnp.int32)
    terms = pl.pallas_call(
        functools.partial(contribution_kernel, freqs=fl),
        in_specs=[smem, smem, smem, smem, vmem] + [hbm] * len(shares),
        out_specs=[vmem] * fl,
        out_shape=[shape] * fl,
        scratch_shapes=[
            pltpu.VMEM((fl * 2 * outer * GROUP, BLK), jnp.float32),
            pltpu.VMEM((len(shares) * per_device, BLK, BLK), jnp.bfloat16),
            pltpu.SemaphoreType.DMA((len(shares),)),
        ],
        compiler_params=pltpu.CompilerParams(vmem_limit_bytes=SMALL),
        name="contributions",
    )(mine.reshape(1), order, own_slots, own_bins, data, *shares)
    terms, freq_at = lax.optimization_barrier((terms, off_at * fl + mine))
    got = {0: terms[0]}
    for away in range(fl - 1, 0, -1):
        got[away] = lax.ppermute(terms[away], "mid", [(i, i ^ away) for i in range(mid_count)])
    terms = [got[away] for away in range(fl)]

    omega = math.pi * (0.1 + 0.8 * (freq_at.astype(jnp.float32) + 0.5) / freq_total)
    phase_real, phase_imag, layer_turns = pl.pallas_call(
        propagator_kernel,
        in_specs=[smem, smem, vmem],
        out_specs=[vmem] * 3,
        out_shape=[jax.ShapeDtypeStruct((NH, total_mid), jnp.float32)] * 2
        + [jax.ShapeDtypeStruct((2, *layers.shape), jnp.float32)],
        compiler_params=pltpu.CompilerParams(vmem_limit_bytes=SMALL),
        cost_estimate=pl.CostEstimate(
            flops=60 * NH * total_mid, bytes_accessed=8 * NH * total_mid, transcendentals=10 * NH * total_mid
        ),
        name="propagator",
    )(omega.reshape(1), slowness, layers)

    middle, offset_turn = twiddle_tables(outer)
    here = mid_local // BLK
    rows_out = (HALF + 1) * 2 * here
    tables = [jnp.asarray(t) for t in block_tables()]
    middle, offset_turn = jnp.asarray(middle), jnp.asarray(offset_turn)
    plane = pl.pallas_call(
        functools.partial(march_kernel, sources=fl),
        in_specs=[smem] + [vmem] * (fl + 9),
        out_specs=vmem,
        out_shape=jax.ShapeDtypeStruct((2, 2, HALF, total_mid), jnp.float32),
        scratch_shapes=[
            pltpu.VMEM((2, 2, HALF, total_mid), jnp.float32),
            pltpu.VMEM((fl * room, BLK), jnp.float32),
        ],
        compiler_params=pltpu.CompilerParams(vmem_limit_bytes=VMEM),
        name="march",
    )(layer_turns, *terms, pick, phase_real, phase_imag, *tables, middle, offset_turn)

    def finish(dest, *before):
        return pl.pallas_call(
            finish_kernel,
            grid_spec=pltpu.PrefetchScalarGridSpec(
                num_scalar_prefetch=1,
                grid=(1,),
                in_specs=[
                    smem,
                    pl.BlockSpec((2, 2, HALF, mid_local), lambda i, dest: (0, 0, 0, dest[0])),
                    vmem,
                    vmem,
                ]
                + [hbm] * len(before),
                out_specs=pl.BlockSpec((rows_out, BLK), lambda i, dest: (0, 0)),
            ),
            out_shape=jax.ShapeDtypeStruct((rows_out, BLK), jnp.int32),
            cost_estimate=pl.CostEstimate(
                flops=6 * NH * NH * 2 * BLK * here, bytes_accessed=6 * NH * mid_local, transcendentals=0
            ),
            compiler_params=pltpu.CompilerParams(vmem_limit_bytes=SMALL),
            name="finish",
        )(dest.reshape(1), layer_turns, plane, tables[1], offset_turn, *before)

    got, before = {}, []
    for ahead in [*range(fl - 1, 0, -1), 0]:
        dest = (mid_at // fl) * fl + (mine ^ ahead)
        block = finish(dest, *before)
        before = [block]
        if ahead:
            block = lax.ppermute(block, "mid", [(s, s ^ ahead) for s in range(mid_count)])
        got[ahead] = block

    field = None
    for ahead in [0, *range(fl - 1, 0, -1)]:
        freq = mine ^ ahead
        first = field is None
        field = pl.pallas_call(
            result_kernel,
            grid_spec=pltpu.PrefetchScalarGridSpec(
                num_scalar_prefetch=1,
                grid=(2,),
                in_specs=[vmem] if first else [vmem, hbm],
                out_specs=pl.BlockSpec((1, HALF, 2 * here, BLK), lambda i, f: (f[0], i, 0, 0)),
            ),
            out_shape=jax.ShapeDtypeStruct((fl, NH, 2 * here, BLK), jnp.float32),
            input_output_aliases={} if first else {2: 0},
            compiler_params=pltpu.CompilerParams(vmem_limit_bytes=SMALL),
            cost_estimate=pl.CostEstimate(
                flops=4 * NH * mid_local, bytes_accessed=12 * NH * mid_local, transcendentals=0
            ),
            name="result",
        )(freq.reshape(1), got[ahead], *([] if first else [field]))
    field = field.reshape(fl, NH, here, 2, BLK).transpose(0, 1, 3, 2, 4)
    return field.reshape(fl, NH, 2, mid_local)


def solution(mesh):
    in_specs = (
        P("off", None, None, "mid"),
        P("off", None, None, None),
        P("off", None),
        P("off"),
        P(None, None, "mid"),
        P(),
    )
    out_specs = P("off", None, None, "mid")
    return jax.shard_map(local, mesh=mesh, in_specs=in_specs, out_specs=out_specs, check_vma=False)
```

```python
import functools
import math

import jax
import jax.numpy as jnp
import numpy as np
from jax import lax
from jax.experimental import pallas as pl
from jax.experimental.pallas import tpu as pltpu
from jax.sharding import PartitionSpec as P

NH = 256
BLK = 128

dz_cells = 2.0
damping = 0.1

HALF = NH // 2
STEP_LOG = 64.0
TOP = 32767.0
GROUP = 8
COLUMNS = 4
ROWS = 8
CHUNKS = 8
UNROLL = 1
VMEM = 28 * 1024 * 1024
SMALL = 10 * 1024 * 1024


def signed_wave(index, length):
    signed = (index + length // 2) % length - length // 2
    return signed.astype(jnp.float32) * (2.0 * math.pi / length)


def root_pair(level):
    magnitude = jnp.sqrt(level * level + damping * damping)
    larger = jnp.sqrt(0.5 * (magnitude + jnp.abs(level)))
    smaller = damping / (2.0 * larger)
    return (jnp.where(level >= 0, larger, smaller), jnp.where(level >= 0, smaller, larger))


def propagator(omega_sq, mid_wave, offset_wave):
    source = 0.5 * (mid_wave - offset_wave)
    receiver = 0.5 * (mid_wave + offset_wave)
    real_s, imag_s = root_pair(omega_sq - source * source)
    real_r, imag_r = root_pair(omega_sq - receiver * receiver)
    decay = jnp.exp(-dz_cells * (imag_s + imag_r))
    turn = dz_cells * (real_s + real_r)
    return (decay * jnp.cos(turn), decay * jnp.sin(turn))


def halves_np(table):
    high = table.astype(np.float32).astype(jnp.bfloat16)
    low = (table - high.astype(np.float64)).astype(np.float32).astype(jnp.bfloat16)
    return high, low


def block_tables():
    index = np.arange(BLK)
    angles = 2.0 * np.pi * (np.outer(index, index) % BLK) / BLK
    cos, sin = np.cos(angles), np.sin(angles)
    upper = np.block([[cos, sin], [-sin, cos]])
    lower = np.block([[cos, -sin], [sin, cos]])
    tables = []
    for axis, pair in ((1, (upper, lower)), (0, (lower, upper))):
        for table in pair:
            high, low = halves_np(table)
            tables.append(np.concatenate([high, high, low], axis=axis))
    return tables


def twiddle_tables(outer):
    ka, b = np.arange(outer)[:, None], np.arange(BLK)[None, :]
    angles = 2.0 * np.pi * ka * b / (outer * BLK)
    middle = np.stack([np.cos(angles), np.sin(angles)]).astype(np.float32)
    rows = 2.0 * np.pi * np.arange(HALF) / NH
    offset = np.stack([np.cos(rows), np.sin(rows)]).astype(np.float32)
    return middle, np.broadcast_to(offset[:, :, None], (2, HALF, BLK)).copy()


def halves(value):
    high = value.astype(jnp.bfloat16)
    return high, (value - high.astype(jnp.float32)).astype(jnp.bfloat16)


def dot(left, right):
    return jnp.dot(left, right, preferred_element_type=jnp.float32)


def left_product(table, value):
    high, low = halves(value)
    return dot(table, jnp.concatenate([high, low, high], axis=0))


def right_product(value, table):
    high, low = halves(value)
    return dot(jnp.concatenate([high, low, high], axis=1), table)


def cmul(real_a, imag_a, real_b, imag_b):
    return real_a * real_b - imag_a * imag_b, real_a * imag_b + imag_a * real_b


def small_transform(values, sign):
    count = len(values)
    if count == 1:
        return values
    even = small_transform(values[0::2], sign)
    odd = small_transform(values[1::2], sign)
    first, second = [], []
    for k in range(count // 2):
        er, ei = even[k]
        xr, xi = odd[k]
        if k == 0:
            tr, ti = xr, xi
        elif 4 * k == count:
            tr, ti = (-xi, xr) if sign > 0 else (xi, -xr)
        else:
            c, s = math.cos(2 * math.pi * k / count), sign * math.sin(2 * math.pi * k / count)
            if 8 * k == count:
                tr, ti = ((xr - xi) * c, (xr + xi) * c) if sign > 0 else ((xr + xi) * c, (xi - xr) * c)
            elif 8 * k == 3 * count:
                tr, ti = ((xr + xi) * c, (xi - xr) * c) if sign > 0 else ((xr - xi) * c, (xr + xi) * c)
            else:
                tr, ti = xr * c - xi * s, xr * s + xi * c
        first.append((er + tr, ei + ti))
        second.append((er - tr, ei - ti))
    return first + second


def scale_code(biggest):
    return (jnp.floor(jnp.log(jnp.maximum(biggest, 1e-30)) * STEP_LOG) + 1.0).astype(jnp.int32)


def scale_of(code):
    return jnp.exp(code.astype(jnp.float32) * (1.0 / STEP_LOG)) * (1.0 / TOP)


def inverse_scale_of(code):
    return jnp.exp(code.astype(jnp.float32) * (-1.0 / STEP_LOG)) * TOP


def coded(value, inverse):
    return jnp.floor(value * inverse + 0.5).astype(jnp.int32)


def packed(high, low):
    return (high << 16) | (low & 0xFFFF)


def unpacked(word):
    return (word >> 16).astype(jnp.float32), ((word << 16) >> 16).astype(jnp.float32)


def contribution_kernel(place_ref, order_ref, slot_ref, bin_ref, data_ref, *rest, freqs):
    *sources, held, weight_ref, sems = rest
    sources, outs = sources[:-freqs], sources[-freqs:]
    groups, outer = outs[0].shape[0], outs[0].shape[1] - 1
    count = sources[0].shape[0]
    copies = [
        pltpu.make_async_copy(ref, weight_ref.at[pl.ds(n * count, count)], sems.at[n])
        for n, ref in enumerate(sources)
    ]
    for copy in copies:
        copy.start()
    for copy in copies:
        copy.wait()

    @pl.loop(0, groups)
    def _(group):
        for at in range(GROUP):
            slot = slot_ref[group * GROUP + at]
            source = bin_ref[group * GROUP + at]
            held[pl.ds(at, data_ref.shape[1], GROUP), :] = dot(data_ref[source], weight_ref[slot])
        for away, out_ref in enumerate(outs):
            base = (place_ref[0] ^ away) * (2 * outer * GROUP)

            def term(at):
                return held[pl.ds(pl.multiple_of(base + at * GROUP, GROUP), GROUP), :]

            biggest = functools.reduce(jnp.maximum, [jnp.abs(term(at)) for at in range(2 * outer)])
            code = scale_code(biggest)
            inverse = inverse_scale_of(code)
            for a in range(outer):
                words = packed(coded(term(a), inverse), coded(term(outer + a), inverse))
                out_ref[group, order_ref[a]] = words
            out_ref[group, outer] = code


def column_of(plane, a):
    lanes = pl.ds(pl.multiple_of(a * BLK, BLK), BLK)
    return jnp.concatenate(
        [
            jnp.concatenate([plane[p, 0, :, lanes], plane[p, 1, :, lanes]], axis=0)
            for p in range(2)
        ],
        axis=1,
    )


def store_column(plane, a, value):
    lanes = pl.ds(pl.multiple_of(a * BLK, BLK), BLK)
    for p in range(2):
        for c in range(2):
            plane[p, c, :, lanes] = value[c * HALF : (c + 1) * HALF, p * BLK : (p + 1) * BLK]


def row_blocks(tall):
    return [slice(at * tall, (at + 1) * tall) for at in range(HALF // tall)]


def turn_at(offset_ref, rows):
    return offset_ref[0, rows], offset_ref[1, rows]


def forward_rows(low, high, turn):
    first = low[0] + high[0], low[1] + high[1]
    second = cmul(low[0] - high[0], low[1] - high[1], turn[0], -turn[1])
    return (*first, *second)


def inverse_rows(value, rows, turn):
    upper, below = rows, slice(HALF + rows.start, HALF + rows.stop)
    first = value[upper, :BLK], value[below, :BLK]
    second = cmul(value[upper, BLK:], value[below, BLK:], turn[0], turn[1])
    low = first[0] + second[0], first[1] + second[1]
    high = first[0] - second[0], first[1] - second[1]
    return low, high


def assembled(blocks):
    parts = [jnp.concatenate(part, axis=0) for part in zip(*blocks)]
    return jnp.concatenate(
        [jnp.concatenate(parts[:2], axis=0), jnp.concatenate(parts[2:], axis=0)], axis=1
    )


def propagator_kernel(omega_ref, slow_ref, layers_ref, real_ref, imag_ref, turns_ref):
    steps, layer_total = slow_ref.shape
    for step in range(steps):
        layers = layers_ref[step]
        slow = functools.reduce(
            jnp.add, [jnp.where(layers == n, slow_ref[step, n], 0.0) for n in range(layer_total)]
        )
        turn = 2.0 * dz_cells * omega_ref[0] * (slow - 1.0)
        turns_ref[0, step] = jnp.cos(turn)
        turns_ref[1, step] = jnp.sin(turn)

    total = real_ref.shape[1]
    scale = 1.0 / (NH * total)
    omega_sq = omega_ref[0] * omega_ref[0]

    @pl.loop(0, NH // GROUP)
    def _(at):
        start = pl.multiple_of(at * GROUP, GROUP)
        row = lax.broadcasted_iota(jnp.int32, (GROUP, BLK), 0) + at * GROUP
        lane = lax.broadcasted_iota(jnp.int32, (GROUP, BLK), 1)
        offset_wave = signed_wave(2 * (row % HALF) + row // HALF, NH)
        for a in range(total // BLK):
            mid_wave = signed_wave(a + total // BLK * lane, total)
            real, imag = propagator(omega_sq, mid_wave, offset_wave)
            real_ref[pl.ds(start, GROUP), a * BLK : (a + 1) * BLK] = real * scale
            imag_ref[pl.ds(start, GROUP), a * BLK : (a + 1) * BLK] = imag * scale


def offset_product(table, columns):
    value = left_product(table[...], jnp.concatenate(columns, axis=1))
    return [value[:, n * 2 * BLK : (n + 1) * 2 * BLK] for n in range(len(columns))]


def layer_turn(pair, layer_ref, step, block, a):
    half = layer_ref.shape[2] // 2
    return [
        cmul(*part, layer_ref[0, step, block + p * half, a], layer_ref[1, step, block + p * half, a])
        for p, part in enumerate(pair)
    ]


def midpoint_pass(plane, out, phase_refs, forward, inverse, middle_ref):
    outer = middle_ref.shape[1]
    lanes = [slice(a * BLK, (a + 1) * BLK) for a in range(outer)]
    tall = ROWS * CHUNKS
    per_half = HALF // tall

    @pl.loop(0, 2 * per_half, unroll=UNROLL)
    def _(at):
        p = at // per_half
        base = pl.multiple_of((at % per_half) * tall, tall)
        phase_base = pl.multiple_of(at * tall, tall)

        def gathered(pieces):
            return jnp.concatenate([jnp.concatenate(pair, axis=1) for pair in pieces], axis=0)

        pieces = []
        for chunk in range(CHUNKS):
            here = pl.ds(base + chunk * ROWS, ROWS)
            values = [(plane[p, 0, here, lane], plane[p, 1, here, lane]) for lane in lanes]
            values = small_transform(values, -1)
            for a in range(outer):
                pieces.append(cmul(*values[a], middle_ref[0, a : a + 1], -middle_ref[1, a : a + 1]))
        value = right_product(gathered(pieces), forward[...])
        pieces = []
        for chunk in range(CHUNKS):
            there = pl.ds(phase_base + chunk * ROWS, ROWS)
            for a in range(outer):
                row = (chunk * outer + a) * ROWS
                part = value[row : row + ROWS]
                pieces.append(
                    cmul(
                        part[:, :BLK], part[:, BLK:],
                        phase_refs[0][there, lanes[a]], phase_refs[1][there, lanes[a]],
                    )
                )
        value = right_product(gathered(pieces), inverse[...])
        for chunk in range(CHUNKS):
            here = pl.ds(base + chunk * ROWS, ROWS)
            values = []
            for a in range(outer):
                row = (chunk * outer + a) * ROWS
                part = value[row : row + ROWS]
                values.append(
                    cmul(part[:, :BLK], part[:, BLK:], middle_ref[0, a : a + 1], middle_ref[1, a : a + 1])
                )
            values = small_transform(values, 1)
            for a in range(outer):
                out[p, 0, here, lanes[a]] = values[a][0]
                out[p, 1, here, lanes[a]] = values[a][1]


def march_kernel(layer_ref, *rest, sources):
    code_refs, rest = rest[:sources], rest[sources:]
    (
        pick_ref, phase_real, phase_imag, rows_forward, rows_inverse, lanes_forward, lanes_inverse,
        middle_ref, offset_ref, other, plane, scales,
    ) = rest
    groups = code_refs[0].shape[0]
    outer = middle_ref.shape[1]
    steps = layer_ref.shape[1]
    tall = NH // layer_ref.shape[2]

    def words(a):
        return jnp.concatenate([ref[:, a].reshape(groups * GROUP, BLK) for ref in code_refs], axis=0)

    scales[...] = scale_of(words(outer))

    @pl.loop(0, outer // COLUMNS, unroll=1)
    def _(at):
        columns = []
        for a in range(COLUMNS):
            real, imag = unpacked(words(at * COLUMNS + a))
            scale = scales[...]
            value = jnp.concatenate([real * scale, imag * scale], axis=1)
            moved = dot(pick_ref[...], jnp.concatenate(halves(value), axis=0))
            blocks = []
            for rows in row_blocks(tall):
                low, high = moved[rows], moved[HALF + rows.start : HALF + rows.stop]
                blocks.append(
                    forward_rows(
                        (low[:, :BLK], low[:, BLK:]), (high[:, :BLK], high[:, BLK:]),
                        turn_at(offset_ref, rows),
                    )
                )
            columns.append(assembled(blocks))
        for a, value in enumerate(offset_product(rows_forward, columns)):
            store_column(plane, at * COLUMNS + a, value)

    for step in range(steps):
        midpoint_pass(plane, other, (phase_real, phase_imag), lanes_forward, lanes_inverse, middle_ref)
        if step < steps - 1:

            @pl.loop(0, outer // COLUMNS, unroll=1)
            def _(at):
                places = [at * COLUMNS + a for a in range(COLUMNS)]
                columns = []
                for a, value in zip(
                    places, offset_product(rows_inverse, [column_of(other, a) for a in places])
                ):
                    blocks = []
                    for block, rows in enumerate(row_blocks(tall)):
                        turn = turn_at(offset_ref, rows)
                        pair = inverse_rows(value, rows, turn)
                        blocks.append(forward_rows(*layer_turn(pair, layer_ref, step, block, a), turn))
                    columns.append(assembled(blocks))
                for a, value in zip(places, offset_product(rows_forward, columns)):
                    store_column(plane, a, value)


def finish_kernel(dest_ref, layer_ref, plane_ref, rows_inverse, offset_ref, *rest):
    out_ref = rest[-1]
    here = plane_ref.shape[3] // BLK
    tall = NH // layer_ref.shape[2]
    step = layer_ref.shape[1] - 1
    columns = offset_product(rows_inverse, [column_of(plane_ref, at) for at in range(here)])
    for at in range(here):
        found = []
        for block, rows in enumerate(row_blocks(tall)):
            pair = inverse_rows(columns[at], rows, turn_at(offset_ref, rows))
            found.append(layer_turn(pair, layer_ref, step, block, dest_ref[0] * here + at))
        for c in range(2):
            biggest = functools.reduce(jnp.maximum, [jnp.abs(part[c]) for pair in found for part in pair])
            code = scale_code(jnp.max(biggest, axis=0, keepdims=True))
            inverse = inverse_scale_of(code)
            row = at * 2 + c
            for block, pair in enumerate(found):
                words = packed(coded(pair[0][c], inverse), coded(pair[1][c], inverse))
                out_ref[pl.ds(block * tall * 2 * here + row, tall, 2 * here), :] = words
            out_ref[pl.ds(HALF * 2 * here + row, 1), :] = code


def result_kernel(freq_ref, code_ref, *rest):
    out_ref = rest[-1]
    per, tall = out_ref.shape[1:3]
    scale = scale_of(code_ref[per * tall :])[None]
    for half in range(2):

        @pl.when(pl.program_id(0) == half)
        def _():
            out_ref[0] = unpacked(code_ref[: per * tall].reshape(per, tall, BLK))[half] * scale


def take_kernel(mine_ref, counts_ref, source_ref, out_ref, sems):
    taken, entries = out_ref.shape[0], source_ref.shape[1]
    bins_here, stride = source_ref.shape[0], source_ref.shape[0] * entries // taken
    copies = []
    for n in range(taken):
        entry, bin_at = n * stride + mine_ref[0], 0
        for b in range(bins_here - 1):
            over = (bin_at == b) & (entry >= counts_ref[b])
            entry = jnp.where(over, entry - counts_ref[b], entry)
            bin_at = jnp.where(over, b + 1, bin_at)
        entry = jnp.minimum(entry, entries - 1)
        copies.append(
            pltpu.make_async_copy(source_ref.at[bin_at, entry], out_ref.at[n], sems.at[n])
        )
        copies[-1].start()
    for copy in copies:
        copy.wait()


def slot_lists(counts_all, targets_all, bins_local, fl, per_device, room):
    offs = counts_all.shape[0] // bins_local
    entries = targets_all.shape[1]
    counts_in = counts_all.reshape(offs, bins_local)
    live = jnp.sum(counts_in, axis=1)
    quarter = jnp.arange(fl, dtype=jnp.int32)
    held = (live[None, :] - quarter[:, None] + fl - 1) // fl
    upto = jnp.sum(
        jnp.where(jnp.arange(offs)[None, :] <= jnp.arange(offs)[:, None], held[:, None, :], 0), axis=2
    )
    at = jnp.arange(room, dtype=jnp.int32)
    past = (at[None, :, None] >= upto[:, None, :]).astype(jnp.int32)
    off_at = jnp.sum(past, axis=2)
    valid = off_at < offs
    off_at = jnp.minimum(off_at, offs - 1)
    start = jnp.sum(past * held[:, None, :], axis=2)
    nth = jnp.clip(at[None, :] - start, 0, per_device - 1)
    entry = nth * fl + quarter[:, None]
    bin_at = off_at * bins_local
    mine = off_at[:, :, None] == jnp.arange(offs)[None, None, :]
    for b in range(bins_local - 1):
        size = jnp.sum(jnp.where(mine, counts_in[None, None, :, b], 0), axis=2)
        over = (bin_at == off_at * bins_local + b) & (entry >= size)
        bin_at = bin_at + over
        entry = entry - jnp.where(over, size, 0)
    flat = bin_at * entries + entry
    total = targets_all.size
    picks = flat[:, :, None] == jnp.arange(total)[None, None, :]
    target = jnp.sum(jnp.where(picks, targets_all.reshape(1, 1, total), 0), axis=2)
    target = jnp.where(valid, target, -1)
    return off_at, nth, bin_at, target


def local(bins_data, operators, targets, counts, layer_index, slowness):
    off_count = lax.axis_size("off")
    mid_count = lax.axis_size("mid")
    bins_local, freq_total, _, mid_local = bins_data.shape
    entries = operators.shape[1]
    bins_total = bins_local * off_count
    fl = freq_total // off_count
    total_mid = mid_local * mid_count
    outer = total_mid // BLK
    mid_at, off_at = lax.axis_index("mid"), lax.axis_index("off")
    assert mid_count % fl == 0 and (bins_local * entries) % fl == 0
    mine = mid_at % fl
    rounds = mid_count // fl
    groups = (
        None if rounds == 1 else [list(range(g * fl, (g + 1) * fl)) for g in range(rounds)]
    )

    per_device = bins_local * entries // fl
    smem = pl.BlockSpec(memory_space=pltpu.SMEM)
    vmem = pl.BlockSpec(memory_space=pltpu.VMEM)
    hbm = pl.BlockSpec(memory_space=pl.ANY)
    own = pl.pallas_call(
        take_kernel,
        in_specs=[smem, smem, hbm],
        out_specs=vmem,
        out_shape=jax.ShapeDtypeStruct((per_device, BLK, BLK), jnp.bfloat16),
        scratch_shapes=[pltpu.SemaphoreType.DMA((per_device,))],
        compiler_params=pltpu.CompilerParams(vmem_limit_bytes=SMALL),
        name="take_own",
    )(mine.reshape(1), counts, operators)
    bins_data, own = lax.optimization_barrier((bins_data, own))
    cores = 2 if off_count % 2 == 0 else 1
    line = off_count // cores
    assert line & (line - 1) == 0 and fl & (fl - 1) == 0
    shares = [own]
    for away in range(1, line):
        low = away & -away
        shares.append(
            lax.ppermute(
                shares[away ^ low],
                "off",
                [(i, (i // cores ^ low) * cores + i % cores) for i in range(off_count)],
            )
        )
    if cores > 1:
        shares += [lax.ppermute(x, "off", [(i, i ^ 1) for i in range(off_count)]) for x in shares]

    pairs = fl * 2

    def extra(whole_numbers, copies):
        flat = whole_numbers.astype(jnp.bfloat16).reshape(1, 1, 1, -1)
        flat = jnp.pad(flat, ((0, 0), (0, 0), (0, pairs - 1), (0, mid_local - flat.shape[3])))
        return jnp.broadcast_to(flat, (1, copies, pairs, mid_local))

    lists = jnp.concatenate([counts[:, None], targets], axis=1)
    data = bins_data.reshape(bins_local, off_count, pairs, mid_local)
    data = jnp.concatenate([data, extra(lists, off_count)], axis=0)
    data = lax.all_to_all(data, "off", split_axis=1, concat_axis=0, tiled=True)

    data = data.reshape(off_count, bins_local + 1, pairs, mid_local)
    lists = data[:, bins_local, 0, : lists.size].astype(jnp.int32).reshape(bins_total, 1 + entries)
    data = data[:, :bins_local].reshape(bins_total, pairs, mid_local)
    data = jnp.concatenate([data, extra(layer_index, 1)[0]], axis=0)
    assert mid_count & (mid_count - 1) == 0
    parts = [data] + [
        lax.ppermute(data, "mid", [(i, i ^ away) for i in range(mid_count)])
        for away in range(mid_count - 1, 0, -1)
    ]
    data = jnp.stack(parts[:1] + parts[:0:-1])
    partner = jnp.arange(mid_count, dtype=jnp.int32) ^ mid_at
    layers = data[:, bins_total, 0, : layer_index.size].astype(jnp.int32)
    layers = jnp.sum(
        jnp.where((partner[:, None] == jnp.arange(mid_count))[:, :, None], layers[None], 0), axis=1
    )
    layers = layers.reshape(mid_count, *layer_index.shape).transpose(1, 2, 0, 3)
    layers = layers.reshape(*layer_index.shape[:2], outer)
    data = data[:, :bins_total].reshape(mid_count, bins_total, pairs, mid_local // BLK, BLK)
    data = data.transpose(1, 2, 0, 3, 4).reshape(bins_total, pairs * outer, BLK)
    order = (partner[:, None] * (mid_local // BLK) + jnp.arange(mid_local // BLK)).reshape(outer)

    live_total = bins_total * entries // 2
    room = -(-(live_total + (fl - 1) * off_count) // fl)
    room = min(-(-room // GROUP) * GROUP, per_device * off_count)
    offs, nth, bins, goal = slot_lists(lists[:, 0], lists[:, 1:], bins_local, fl, per_device, room)
    side = (offs % cores != off_at % cores).astype(jnp.int32) * line
    slots = (side + ((offs // cores) ^ (off_at // cores))) * per_device + nth
    source = jnp.arange(fl, dtype=jnp.int32) ^ mine
    goal = jnp.sum(jnp.where((source[:, None] == jnp.arange(fl))[:, :, None], goal[None], 0), axis=1)
    pick = (
        jnp.tile(goal.reshape(1, fl * room), (1, 2))
        == lax.broadcasted_iota(jnp.int32, (NH, 2 * fl * room), 0)
    ).astype(jnp.bfloat16)
    own_slots = lax.dynamic_index_in_dim(slots, mine, 0, False)
    own_bins = lax.dynamic_index_in_dim(bins, mine, 0, False)
    list_groups = room // GROUP
    data, order, own_slots, own_bins, layers, pick = lax.optimization_barrier(
        (data, order, own_slots, own_bins, layers, pick)
    )
    shape = jax.ShapeDtypeStruct((list_groups, outer + 1, GROUP, BLK), jnp.int32)
    terms = pl.pallas_call(
        functools.partial(contribution_kernel, freqs=fl),
        in_specs=[smem, smem, smem, smem, vmem] + [hbm] * len(shares),
        out_specs=[vmem] * fl,
        out_shape=[shape] * fl,
        scratch_shapes=[
            pltpu.VMEM((fl * 2 * outer * GROUP, BLK), jnp.float32),
            pltpu.VMEM((len(shares) * per_device, BLK, BLK), jnp.bfloat16),
            pltpu.SemaphoreType.DMA((len(shares),)),
        ],
        compiler_params=pltpu.CompilerParams(vmem_limit_bytes=SMALL),
        name="contributions",
    )(mine.reshape(1), order, own_slots, own_bins, data, *shares)
    terms, freq_at = lax.optimization_barrier((terms, off_at * fl + mine))
    got = {0: terms[0]}
    for away in range(fl - 1, 0, -1):
        got[away] = lax.ppermute(terms[away], "mid", [(i, i ^ away) for i in range(mid_count)])
    terms = [got[away] for away in range(fl)]

    omega = math.pi * (0.1 + 0.8 * (freq_at.astype(jnp.float32) + 0.5) / freq_total)
    phase_real, phase_imag, layer_turns = pl.pallas_call(
        propagator_kernel,
        in_specs=[smem, smem, vmem],
        out_specs=[vmem] * 3,
        out_shape=[jax.ShapeDtypeStruct((NH, total_mid), jnp.float32)] * 2
        + [jax.ShapeDtypeStruct((2, *layers.shape), jnp.float32)],
        compiler_params=pltpu.CompilerParams(vmem_limit_bytes=SMALL),
        cost_estimate=pl.CostEstimate(
            flops=60 * NH * total_mid, bytes_accessed=8 * NH * total_mid, transcendentals=10 * NH * total_mid
        ),
        name="propagator",
    )(omega.reshape(1), slowness, layers)

    middle, offset_turn = twiddle_tables(outer)
    here = mid_local // BLK
    rows_out = (HALF + 1) * 2 * here
    tables = [jnp.asarray(t) for t in block_tables()]
    middle, offset_turn = jnp.asarray(middle), jnp.asarray(offset_turn)
    plane = pl.pallas_call(
        functools.partial(march_kernel, sources=fl),
        in_specs=[smem] + [vmem] * (fl + 9),
        out_specs=vmem,
        out_shape=jax.ShapeDtypeStruct((2, 2, HALF, total_mid), jnp.float32),
        scratch_shapes=[
            pltpu.VMEM((2, 2, HALF, total_mid), jnp.float32),
            pltpu.VMEM((fl * room, BLK), jnp.float32),
        ],
        compiler_params=pltpu.CompilerParams(vmem_limit_bytes=VMEM),
        name="march",
    )(layer_turns, *terms, pick, phase_real, phase_imag, *tables, middle, offset_turn)

    def finish(dest, *before):
        return pl.pallas_call(
            finish_kernel,
            grid_spec=pltpu.PrefetchScalarGridSpec(
                num_scalar_prefetch=1,
                grid=(1,),
                in_specs=[
                    smem,
                    pl.BlockSpec((2, 2, HALF, mid_local), lambda i, dest: (0, 0, 0, dest[0])),
                    vmem,
                    vmem,
                ]
                + [hbm] * len(before),
                out_specs=pl.BlockSpec((rows_out, BLK), lambda i, dest: (0, 0)),
            ),
            out_shape=jax.ShapeDtypeStruct((rows_out, BLK), jnp.int32),
            cost_estimate=pl.CostEstimate(
                flops=6 * NH * NH * 2 * BLK * here, bytes_accessed=6 * NH * mid_local, transcendentals=0
            ),
            compiler_params=pltpu.CompilerParams(vmem_limit_bytes=SMALL),
            name="finish",
        )(dest.reshape(1), layer_turns, plane, tables[1], offset_turn, *before)

    got, before = {}, []
    for ahead in [*range(fl - 1, 0, -1), 0]:
        dest = (mid_at // fl) * fl + (mine ^ ahead)
        block = finish(dest, *before)
        before = [block]
        if ahead:
            block = lax.ppermute(block, "mid", [(s, s ^ ahead) for s in range(mid_count)])
        got[ahead] = block

    field = None
    for ahead in [0, *range(fl - 1, 0, -1)]:
        freq = mine ^ ahead
        first = field is None
        field = pl.pallas_call(
            result_kernel,
            grid_spec=pltpu.PrefetchScalarGridSpec(
                num_scalar_prefetch=1,
                grid=(2,),
                in_specs=[vmem] if first else [vmem, hbm],
                out_specs=pl.BlockSpec((1, HALF, 2 * here, BLK), lambda i, f: (f[0], i, 0, 0)),
            ),
            out_shape=jax.ShapeDtypeStruct((fl, NH, 2 * here, BLK), jnp.float32),
            input_output_aliases={} if first else {2: 0},
            compiler_params=pltpu.CompilerParams(vmem_limit_bytes=SMALL),
            cost_estimate=pl.CostEstimate(
                flops=4 * NH * mid_local, bytes_accessed=12 * NH * mid_local, transcendentals=0
            ),
            name="result",
        )(freq.reshape(1), got[ahead], *([] if first else [field]))
    field = field.reshape(fl, NH, here, 2, BLK).transpose(0, 1, 3, 2, 4)
    return field.reshape(fl, NH, 2, mid_local)


def solution(mesh):
    in_specs = (
        P("off", None, None, "mid"),
        P("off", None, None, None),
        P("off", None),
        P("off"),
        P(None, None, "mid"),
        P(),
    )
    out_specs = P("off", None, None, "mid")
    return jax.shard_map(local, mesh=mesh, in_specs=in_specs, out_specs=out_specs, check_vma=False)
```

```python
import functools
import math

import jax
import jax.numpy as jnp
import numpy as np
from jax import lax
from jax.experimental import pallas as pl
from jax.experimental.pallas import tpu as pltpu
from jax.sharding import PartitionSpec as P

NH = 256
BLK = 128

dz_cells = 2.0
damping = 0.1

HALF = NH // 2
STEP_LOG = 64.0
TOP = 32767.0
GROUP = 8
COLUMNS = 8
ROWS = 8
CHUNKS = 16
UNROLL = 1
VMEM = 28 * 1024 * 1024
SMALL = 10 * 1024 * 1024


def signed_wave(index, length):
    signed = (index + length // 2) % length - length // 2
    return signed.astype(jnp.float32) * (2.0 * math.pi / length)


def root_pair(level):
    magnitude = jnp.sqrt(level * level + damping * damping)
    larger = jnp.sqrt(0.5 * (magnitude + jnp.abs(level)))
    smaller = damping / (2.0 * larger)
    return (jnp.where(level >= 0, larger, smaller), jnp.where(level >= 0, smaller, larger))


def propagator(omega_sq, mid_wave, offset_wave):
    source = 0.5 * (mid_wave - offset_wave)
    receiver = 0.5 * (mid_wave + offset_wave)
    real_s, imag_s = root_pair(omega_sq - source * source)
    real_r, imag_r = root_pair(omega_sq - receiver * receiver)
    decay = jnp.exp(-dz_cells * (imag_s + imag_r))
    turn = dz_cells * (real_s + real_r)
    return (decay * jnp.cos(turn), decay * jnp.sin(turn))


def halves_np(table):
    high = table.astype(np.float32).astype(jnp.bfloat16)
    low = (table - high.astype(np.float64)).astype(np.float32).astype(jnp.bfloat16)
    return high, low


def block_tables():
    index = np.arange(BLK)
    angles = 2.0 * np.pi * (np.outer(index, index) % BLK) / BLK
    cos, sin = np.cos(angles), np.sin(angles)
    upper = np.block([[cos, sin], [-sin, cos]])
    lower = np.block([[cos, -sin], [sin, cos]])
    tables = []
    for axis, pair in ((1, (upper, lower)), (0, (lower, upper))):
        for table in pair:
            high, low = halves_np(table)
            tables.append(np.concatenate([high, high, low], axis=axis))
    return tables


def twiddle_tables(outer):
    ka, b = np.arange(outer)[:, None], np.arange(BLK)[None, :]
    angles = 2.0 * np.pi * ka * b / (outer * BLK)
    middle = np.stack([np.cos(angles), np.sin(angles)]).astype(np.float32)
    rows = 2.0 * np.pi * np.arange(HALF) / NH
    offset = np.stack([np.cos(rows), np.sin(rows)]).astype(np.float32)
    return middle, np.broadcast_to(offset[:, :, None], (2, HALF, BLK)).copy()


def halves(value):
    high = value.astype(jnp.bfloat16)
    return high, (value - high.astype(jnp.float32)).astype(jnp.bfloat16)


def dot(left, right):
    return jnp.dot(left, right, preferred_element_type=jnp.float32)


def left_product(table, value):
    high, low = halves(value)
    return dot(table, jnp.concatenate([high, low, high], axis=0))


def right_product(value, table):
    high, low = halves(value)
    return dot(jnp.concatenate([high, low, high], axis=1), table)


def cmul(real_a, imag_a, real_b, imag_b):
    return real_a * real_b - imag_a * imag_b, real_a * imag_b + imag_a * real_b


def small_transform(values, sign):
    count = len(values)
    if count == 1:
        return values
    even = small_transform(values[0::2], sign)
    odd = small_transform(values[1::2], sign)
    first, second = [], []
    for k in range(count // 2):
        er, ei = even[k]
        xr, xi = odd[k]
        if k == 0:
            tr, ti = xr, xi
        elif 4 * k == count:
            tr, ti = (-xi, xr) if sign > 0 else (xi, -xr)
        else:
            c, s = math.cos(2 * math.pi * k / count), sign * math.sin(2 * math.pi * k / count)
            if 8 * k == count:
                tr, ti = ((xr - xi) * c, (xr + xi) * c) if sign > 0 else ((xr + xi) * c, (xi - xr) * c)
            elif 8 * k == 3 * count:
                tr, ti = ((xr + xi) * c, (xi - xr) * c) if sign > 0 else ((xr - xi) * c, (xr + xi) * c)
            else:
                tr, ti = xr * c - xi * s, xr * s + xi * c
        first.append((er + tr, ei + ti))
        second.append((er - tr, ei - ti))
    return first + second


def scale_code(biggest):
    return (jnp.floor(jnp.log(jnp.maximum(biggest, 1e-30)) * STEP_LOG) + 1.0).astype(jnp.int32)


def scale_of(code):
    return jnp.exp(code.astype(jnp.float32) * (1.0 / STEP_LOG)) * (1.0 / TOP)


def inverse_scale_of(code):
    return jnp.exp(code.astype(jnp.float32) * (-1.0 / STEP_LOG)) * TOP


def coded(value, inverse):
    return jnp.floor(value * inverse + 0.5).astype(jnp.int32)


def packed(high, low):
    return (high << 16) | (low & 0xFFFF)


def unpacked(word):
    return (word >> 16).astype(jnp.float32), ((word << 16) >> 16).astype(jnp.float32)


def contribution_kernel(place_ref, order_ref, slot_ref, bin_ref, data_ref, *rest, freqs):
    *sources, held, weight_ref, sems = rest
    sources, outs = sources[:-freqs], sources[-freqs:]
    groups, outer = outs[0].shape[0], outs[0].shape[1] - 1
    count = sources[0].shape[0]
    copies = [
        pltpu.make_async_copy(ref, weight_ref.at[pl.ds(n * count, count)], sems.at[n])
        for n, ref in enumerate(sources)
    ]
    for copy in copies:
        copy.start()
    for copy in copies:
        copy.wait()

    @pl.loop(0, groups)
    def _(group):
        for at in range(GROUP):
            slot = slot_ref[group * GROUP + at]
            source = bin_ref[group * GROUP + at]
            held[pl.ds(at, data_ref.shape[1], GROUP), :] = dot(data_ref[source], weight_ref[slot])
        for away, out_ref in enumerate(outs):
            base = (place_ref[0] ^ away) * (2 * outer * GROUP)

            def term(at):
                return held[pl.ds(pl.multiple_of(base + at * GROUP, GROUP), GROUP), :]

            biggest = functools.reduce(jnp.maximum, [jnp.abs(term(at)) for at in range(2 * outer)])
            code = scale_code(biggest)
            inverse = inverse_scale_of(code)
            for a in range(outer):
                words = packed(coded(term(a), inverse), coded(term(outer + a), inverse))
                out_ref[group, order_ref[a]] = words
            out_ref[group, outer] = code


def column_of(plane, a):
    lanes = pl.ds(pl.multiple_of(a * BLK, BLK), BLK)
    return jnp.concatenate(
        [
            jnp.concatenate([plane[p, 0, :, lanes], plane[p, 1, :, lanes]], axis=0)
            for p in range(2)
        ],
        axis=1,
    )


def store_column(plane, a, value):
    lanes = pl.ds(pl.multiple_of(a * BLK, BLK), BLK)
    for p in range(2):
        for c in range(2):
            plane[p, c, :, lanes] = value[c * HALF : (c + 1) * HALF, p * BLK : (p + 1) * BLK]


def row_blocks(tall):
    return [slice(at * tall, (at + 1) * tall) for at in range(HALF // tall)]


def turn_at(offset_ref, rows):
    return offset_ref[0, rows], offset_ref[1, rows]


def forward_rows(low, high, turn):
    first = low[0] + high[0], low[1] + high[1]
    second = cmul(low[0] - high[0], low[1] - high[1], turn[0], -turn[1])
    return (*first, *second)


def inverse_rows(value, rows, turn):
    upper, below = rows, slice(HALF + rows.start, HALF + rows.stop)
    first = value[upper, :BLK], value[below, :BLK]
    second = cmul(value[upper, BLK:], value[below, BLK:], turn[0], turn[1])
    low = first[0] + second[0], first[1] + second[1]
    high = first[0] - second[0], first[1] - second[1]
    return low, high


def assembled(blocks):
    parts = [jnp.concatenate(part, axis=0) for part in zip(*blocks)]
    return jnp.concatenate(
        [jnp.concatenate(parts[:2], axis=0), jnp.concatenate(parts[2:], axis=0)], axis=1
    )


def propagator_kernel(omega_ref, slow_ref, layers_ref, real_ref, imag_ref, turns_ref):
    steps, layer_total = slow_ref.shape
    for step in range(steps):
        layers = layers_ref[step]
        slow = functools.reduce(
            jnp.add, [jnp.where(layers == n, slow_ref[step, n], 0.0) for n in range(layer_total)]
        )
        turn = 2.0 * dz_cells * omega_ref[0] * (slow - 1.0)
        turns_ref[0, step] = jnp.cos(turn)
        turns_ref[1, step] = jnp.sin(turn)

    total = real_ref.shape[1]
    scale = 1.0 / (NH * total)
    omega_sq = omega_ref[0] * omega_ref[0]

    @pl.loop(0, NH // GROUP)
    def _(at):
        start = pl.multiple_of(at * GROUP, GROUP)
        row = lax.broadcasted_iota(jnp.int32, (GROUP, BLK), 0) + at * GROUP
        lane = lax.broadcasted_iota(jnp.int32, (GROUP, BLK), 1)
        offset_wave = signed_wave(2 * (row % HALF) + row // HALF, NH)
        for a in range(total // BLK):
            mid_wave = signed_wave(a + total // BLK * lane, total)
            real, imag = propagator(omega_sq, mid_wave, offset_wave)
            real_ref[pl.ds(start, GROUP), a * BLK : (a + 1) * BLK] = real * scale
            imag_ref[pl.ds(start, GROUP), a * BLK : (a + 1) * BLK] = imag * scale


def offset_product(table, columns):
    value = left_product(table[...], jnp.concatenate(columns, axis=1))
    return [value[:, n * 2 * BLK : (n + 1) * 2 * BLK] for n in range(len(columns))]


def layer_turn(pair, layer_ref, step, block, a):
    half = layer_ref.shape[2] // 2
    return [
        cmul(*part, layer_ref[0, step, block + p * half, a], layer_ref[1, step, block + p * half, a])
        for p, part in enumerate(pair)
    ]


def midpoint_pass(plane, out, phase_refs, forward, inverse, middle_ref):
    outer = middle_ref.shape[1]
    lanes = [slice(a * BLK, (a + 1) * BLK) for a in range(outer)]
    tall = ROWS * CHUNKS
    per_half = HALF // tall

    @pl.loop(0, 2 * per_half, unroll=UNROLL)
    def _(at):
        p = at // per_half
        base = pl.multiple_of((at % per_half) * tall, tall)
        phase_base = pl.multiple_of(at * tall, tall)

        def gathered(pieces):
            return jnp.concatenate([jnp.concatenate(pair, axis=1) for pair in pieces], axis=0)

        pieces = []
        for chunk in range(CHUNKS):
            here = pl.ds(base + chunk * ROWS, ROWS)
            values = [(plane[p, 0, here, lane], plane[p, 1, here, lane]) for lane in lanes]
            values = small_transform(values, -1)
            for a in range(outer):
                pieces.append(cmul(*values[a], middle_ref[0, a : a + 1], -middle_ref[1, a : a + 1]))
        value = right_product(gathered(pieces), forward[...])
        pieces = []
        for chunk in range(CHUNKS):
            there = pl.ds(phase_base + chunk * ROWS, ROWS)
            for a in range(outer):
                row = (chunk * outer + a) * ROWS
                part = value[row : row + ROWS]
                pieces.append(
                    cmul(
                        part[:, :BLK], part[:, BLK:],
                        phase_refs[0][there, lanes[a]], phase_refs[1][there, lanes[a]],
                    )
                )
        value = right_product(gathered(pieces), inverse[...])
        for chunk in range(CHUNKS):
            here = pl.ds(base + chunk * ROWS, ROWS)
            values = []
            for a in range(outer):
                row = (chunk * outer + a) * ROWS
                part = value[row : row + ROWS]
                values.append(
                    cmul(part[:, :BLK], part[:, BLK:], middle_ref[0, a : a + 1], middle_ref[1, a : a + 1])
                )
            values = small_transform(values, 1)
            for a in range(outer):
                out[p, 0, here, lanes[a]] = values[a][0]
                out[p, 1, here, lanes[a]] = values[a][1]


def march_kernel(layer_ref, *rest, sources):
    code_refs, rest = rest[:sources], rest[sources:]
    (
        pick_ref, phase_real, phase_imag, rows_forward, rows_inverse, lanes_forward, lanes_inverse,
        middle_ref, offset_ref, other, plane, scales,
    ) = rest
    groups = code_refs[0].shape[0]
    outer = middle_ref.shape[1]
    steps = layer_ref.shape[1]
    tall = NH // layer_ref.shape[2]

    def words(a):
        return jnp.concatenate([ref[:, a].reshape(groups * GROUP, BLK) for ref in code_refs], axis=0)

    scales[...] = scale_of(words(outer))

    @pl.loop(0, outer // COLUMNS, unroll=1)
    def _(at):
        columns = []
        for a in range(COLUMNS):
            real, imag = unpacked(words(at * COLUMNS + a))
            scale = scales[...]
            value = jnp.concatenate([real * scale, imag * scale], axis=1)
            moved = dot(pick_ref[...], jnp.concatenate(halves(value), axis=0))
            blocks = []
            for rows in row_blocks(tall):
                low, high = moved[rows], moved[HALF + rows.start : HALF + rows.stop]
                blocks.append(
                    forward_rows(
                        (low[:, :BLK], low[:, BLK:]), (high[:, :BLK], high[:, BLK:]),
                        turn_at(offset_ref, rows),
                    )
                )
            columns.append(assembled(blocks))
        for a, value in enumerate(offset_product(rows_forward, columns)):
            store_column(plane, at * COLUMNS + a, value)

    for step in range(steps):
        midpoint_pass(plane, other, (phase_real, phase_imag), lanes_forward, lanes_inverse, middle_ref)
        if step < steps - 1:

            @pl.loop(0, outer // COLUMNS, unroll=1)
            def _(at):
                places = [at * COLUMNS + a for a in range(COLUMNS)]
                columns = []
                for a, value in zip(
                    places, offset_product(rows_inverse, [column_of(other, a) for a in places])
                ):
                    blocks = []
                    for block, rows in enumerate(row_blocks(tall)):
                        turn = turn_at(offset_ref, rows)
                        pair = inverse_rows(value, rows, turn)
                        blocks.append(forward_rows(*layer_turn(pair, layer_ref, step, block, a), turn))
                    columns.append(assembled(blocks))
                for a, value in zip(places, offset_product(rows_forward, columns)):
                    store_column(plane, a, value)


def finish_kernel(dest_ref, layer_ref, plane_ref, rows_inverse, offset_ref, *rest):
    out_ref = rest[-1]
    here = plane_ref.shape[3] // BLK
    tall = NH // layer_ref.shape[2]
    step = layer_ref.shape[1] - 1
    columns = offset_product(rows_inverse, [column_of(plane_ref, at) for at in range(here)])
    for at in range(here):
        found = []
        for block, rows in enumerate(row_blocks(tall)):
            pair = inverse_rows(columns[at], rows, turn_at(offset_ref, rows))
            found.append(layer_turn(pair, layer_ref, step, block, dest_ref[0] * here + at))
        for c in range(2):
            biggest = functools.reduce(jnp.maximum, [jnp.abs(part[c]) for pair in found for part in pair])
            code = scale_code(jnp.max(biggest, axis=0, keepdims=True))
            inverse = inverse_scale_of(code)
            row = at * 2 + c
            for block, pair in enumerate(found):
                words = packed(coded(pair[0][c], inverse), coded(pair[1][c], inverse))
                out_ref[pl.ds(block * tall * 2 * here + row, tall, 2 * here), :] = words
            out_ref[pl.ds(HALF * 2 * here + row, 1), :] = code


def result_kernel(freq_ref, code_ref, *rest):
    out_ref = rest[-1]
    per, tall = out_ref.shape[1:3]
    scale = scale_of(code_ref[per * tall :])[None]
    for half in range(2):

        @pl.when(pl.program_id(0) == half)
        def _():
            out_ref[0] = unpacked(code_ref[: per * tall].reshape(per, tall, BLK))[half] * scale


def take_kernel(mine_ref, counts_ref, source_ref, out_ref, sems):
    taken, entries = out_ref.shape[0], source_ref.shape[1]
    bins_here, stride = source_ref.shape[0], source_ref.shape[0] * entries // taken
    copies = []
    for n in range(taken):
        entry, bin_at = n * stride + mine_ref[0], 0
        for b in range(bins_here - 1):
            over = (bin_at == b) & (entry >= counts_ref[b])
            entry = jnp.where(over, entry - counts_ref[b], entry)
            bin_at = jnp.where(over, b + 1, bin_at)
        entry = jnp.minimum(entry, entries - 1)
        copies.append(
            pltpu.make_async_copy(source_ref.at[bin_at, entry], out_ref.at[n], sems.at[n])
        )
        copies[-1].start()
    for copy in copies:
        copy.wait()


def slot_lists(counts_all, targets_all, bins_local, fl, per_device, room):
    offs = counts_all.shape[0] // bins_local
    entries = targets_all.shape[1]
    counts_in = counts_all.reshape(offs, bins_local)
    live = jnp.sum(counts_in, axis=1)
    quarter = jnp.arange(fl, dtype=jnp.int32)
    held = (live[None, :] - quarter[:, None] + fl - 1) // fl
    upto = jnp.sum(
        jnp.where(jnp.arange(offs)[None, :] <= jnp.arange(offs)[:, None], held[:, None, :], 0), axis=2
    )
    at = jnp.arange(room, dtype=jnp.int32)
    past = (at[None, :, None] >= upto[:, None, :]).astype(jnp.int32)
    off_at = jnp.sum(past, axis=2)
    valid = off_at < offs
    off_at = jnp.minimum(off_at, offs - 1)
    start = jnp.sum(past * held[:, None, :], axis=2)
    nth = jnp.clip(at[None, :] - start, 0, per_device - 1)
    entry = nth * fl + quarter[:, None]
    bin_at = off_at * bins_local
    mine = off_at[:, :, None] == jnp.arange(offs)[None, None, :]
    for b in range(bins_local - 1):
        size = jnp.sum(jnp.where(mine, counts_in[None, None, :, b], 0), axis=2)
        over = (bin_at == off_at * bins_local + b) & (entry >= size)
        bin_at = bin_at + over
        entry = entry - jnp.where(over, size, 0)
    flat = bin_at * entries + entry
    total = targets_all.size
    picks = flat[:, :, None] == jnp.arange(total)[None, None, :]
    target = jnp.sum(jnp.where(picks, targets_all.reshape(1, 1, total), 0), axis=2)
    target = jnp.where(valid, target, -1)
    return off_at, nth, bin_at, target


def local(bins_data, operators, targets, counts, layer_index, slowness):
    off_count = lax.axis_size("off")
    mid_count = lax.axis_size("mid")
    bins_local, freq_total, _, mid_local = bins_data.shape
    entries = operators.shape[1]
    bins_total = bins_local * off_count
    fl = freq_total // off_count
    total_mid = mid_local * mid_count
    outer = total_mid // BLK
    mid_at, off_at = lax.axis_index("mid"), lax.axis_index("off")
    assert mid_count % fl == 0 and (bins_local * entries) % fl == 0
    mine = mid_at % fl
    rounds = mid_count // fl
    groups = (
        None if rounds == 1 else [list(range(g * fl, (g + 1) * fl)) for g in range(rounds)]
    )

    per_device = bins_local * entries // fl
    smem = pl.BlockSpec(memory_space=pltpu.SMEM)
    vmem = pl.BlockSpec(memory_space=pltpu.VMEM)
    hbm = pl.BlockSpec(memory_space=pl.ANY)
    own = pl.pallas_call(
        take_kernel,
        in_specs=[smem, smem, hbm],
        out_specs=vmem,
        out_shape=jax.ShapeDtypeStruct((per_device, BLK, BLK), jnp.bfloat16),
        scratch_shapes=[pltpu.SemaphoreType.DMA((per_device,))],
        compiler_params=pltpu.CompilerParams(vmem_limit_bytes=SMALL),
        name="take_own",
    )(mine.reshape(1), counts, operators)
    bins_data, own = lax.optimization_barrier((bins_data, own))
    cores = 2 if off_count % 2 == 0 else 1
    line = off_count // cores
    assert line & (line - 1) == 0 and fl & (fl - 1) == 0
    shares = [own]
    for away in range(1, line):
        low = away & -away
        shares.append(
            lax.ppermute(
                shares[away ^ low],
                "off",
                [(i, (i // cores ^ low) * cores + i % cores) for i in range(off_count)],
            )
        )
    if cores > 1:
        shares += [lax.ppermute(x, "off", [(i, i ^ 1) for i in range(off_count)]) for x in shares]

    pairs = fl * 2

    def extra(whole_numbers, copies):
        flat = whole_numbers.astype(jnp.bfloat16).reshape(1, 1, 1, -1)
        flat = jnp.pad(flat, ((0, 0), (0, 0), (0, pairs - 1), (0, mid_local - flat.shape[3])))
        return jnp.broadcast_to(flat, (1, copies, pairs, mid_local))

    lists = jnp.concatenate([counts[:, None], targets], axis=1)
    data = bins_data.reshape(bins_local, off_count, pairs, mid_local)
    data = jnp.concatenate([data, extra(lists, off_count)], axis=0)
    data = lax.all_to_all(data, "off", split_axis=1, concat_axis=0, tiled=True)

    data = data.reshape(off_count, bins_local + 1, pairs, mid_local)
    lists = data[:, bins_local, 0, : lists.size].astype(jnp.int32).reshape(bins_total, 1 + entries)
    data = data[:, :bins_local].reshape(bins_total, pairs, mid_local)
    data = jnp.concatenate([data, extra(layer_index, 1)[0]], axis=0)
    assert mid_count & (mid_count - 1) == 0
    parts = [data] + [
        lax.ppermute(data, "mid", [(i, i ^ away) for i in range(mid_count)])
        for away in range(mid_count - 1, 0, -1)
    ]
    data = jnp.stack(parts[:1] + parts[:0:-1])
    partner = jnp.arange(mid_count, dtype=jnp.int32) ^ mid_at
    layers = data[:, bins_total, 0, : layer_index.size].astype(jnp.int32)
    layers = jnp.sum(
        jnp.where((partner[:, None] == jnp.arange(mid_count))[:, :, None], layers[None], 0), axis=1
    )
    layers = layers.reshape(mid_count, *layer_index.shape).transpose(1, 2, 0, 3)
    layers = layers.reshape(*layer_index.shape[:2], outer)
    data = data[:, :bins_total].reshape(mid_count, bins_total, pairs, mid_local // BLK, BLK)
    data = data.transpose(1, 2, 0, 3, 4).reshape(bins_total, pairs * outer, BLK)
    order = (partner[:, None] * (mid_local // BLK) + jnp.arange(mid_local // BLK)).reshape(outer)

    live_total = bins_total * entries // 2
    room = -(-(live_total + (fl - 1) * off_count) // fl)
    room = min(-(-room // GROUP) * GROUP, per_device * off_count)
    offs, nth, bins, goal = slot_lists(lists[:, 0], lists[:, 1:], bins_local, fl, per_device, room)
    side = (offs % cores != off_at % cores).astype(jnp.int32) * line
    slots = (side + ((offs // cores) ^ (off_at // cores))) * per_device + nth
    source = jnp.arange(fl, dtype=jnp.int32) ^ mine
    goal = jnp.sum(jnp.where((source[:, None] == jnp.arange(fl))[:, :, None], goal[None], 0), axis=1)
    pick = (
        jnp.tile(goal.reshape(1, fl * room), (1, 2))
        == lax.broadcasted_iota(jnp.int32, (NH, 2 * fl * room), 0)
    ).astype(jnp.bfloat16)
    own_slots = lax.dynamic_index_in_dim(slots, mine, 0, False)
    own_bins = lax.dynamic_index_in_dim(bins, mine, 0, False)
    list_groups = room // GROUP
    data, order, own_slots, own_bins, layers, pick = lax.optimization_barrier(
        (data, order, own_slots, own_bins, layers, pick)
    )
    shape = jax.ShapeDtypeStruct((list_groups, outer + 1, GROUP, BLK), jnp.int32)
    terms = pl.pallas_call(
        functools.partial(contribution_kernel, freqs=fl),
        in_specs=[smem, smem, smem, smem, vmem] + [hbm] * len(shares),
        out_specs=[vmem] * fl,
        out_shape=[shape] * fl,
        scratch_shapes=[
            pltpu.VMEM((fl * 2 * outer * GROUP, BLK), jnp.float32),
            pltpu.VMEM((len(shares) * per_device, BLK, BLK), jnp.bfloat16),
            pltpu.SemaphoreType.DMA((len(shares),)),
        ],
        compiler_params=pltpu.CompilerParams(vmem_limit_bytes=SMALL),
        name="contributions",
    )(mine.reshape(1), order, own_slots, own_bins, data, *shares)
    terms, freq_at = lax.optimization_barrier((terms, off_at * fl + mine))
    got = {0: terms[0]}
    for away in range(fl - 1, 0, -1):
        got[away] = lax.ppermute(terms[away], "mid", [(i, i ^ away) for i in range(mid_count)])
    terms = [got[away] for away in range(fl)]

    omega = math.pi * (0.1 + 0.8 * (freq_at.astype(jnp.float32) + 0.5) / freq_total)
    phase_real, phase_imag, layer_turns = pl.pallas_call(
        propagator_kernel,
        in_specs=[smem, smem, vmem],
        out_specs=[vmem] * 3,
        out_shape=[jax.ShapeDtypeStruct((NH, total_mid), jnp.float32)] * 2
        + [jax.ShapeDtypeStruct((2, *layers.shape), jnp.float32)],
        compiler_params=pltpu.CompilerParams(vmem_limit_bytes=SMALL),
        cost_estimate=pl.CostEstimate(
            flops=60 * NH * total_mid, bytes_accessed=8 * NH * total_mid, transcendentals=10 * NH * total_mid
        ),
        name="propagator",
    )(omega.reshape(1), slowness, layers)

    middle, offset_turn = twiddle_tables(outer)
    here = mid_local // BLK
    rows_out = (HALF + 1) * 2 * here
    tables = [jnp.asarray(t) for t in block_tables()]
    middle, offset_turn = jnp.asarray(middle), jnp.asarray(offset_turn)
    plane = pl.pallas_call(
        functools.partial(march_kernel, sources=fl),
        in_specs=[smem] + [vmem] * (fl + 9),
        out_specs=vmem,
        out_shape=jax.ShapeDtypeStruct((2, 2, HALF, total_mid), jnp.float32),
        scratch_shapes=[
            pltpu.VMEM((2, 2, HALF, total_mid), jnp.float32),
            pltpu.VMEM((fl * room, BLK), jnp.float32),
        ],
        compiler_params=pltpu.CompilerParams(vmem_limit_bytes=VMEM),
        name="march",
    )(layer_turns, *terms, pick, phase_real, phase_imag, *tables, middle, offset_turn)

    def finish(dest, *before):
        return pl.pallas_call(
            finish_kernel,
            grid_spec=pltpu.PrefetchScalarGridSpec(
                num_scalar_prefetch=1,
                grid=(1,),
                in_specs=[
                    smem,
                    pl.BlockSpec((2, 2, HALF, mid_local), lambda i, dest: (0, 0, 0, dest[0])),
                    vmem,
                    vmem,
                ]
                + [hbm] * len(before),
                out_specs=pl.BlockSpec((rows_out, BLK), lambda i, dest: (0, 0)),
            ),
            out_shape=jax.ShapeDtypeStruct((rows_out, BLK), jnp.int32),
            cost_estimate=pl.CostEstimate(
                flops=6 * NH * NH * 2 * BLK * here, bytes_accessed=6 * NH * mid_local, transcendentals=0
            ),
            compiler_params=pltpu.CompilerParams(vmem_limit_bytes=SMALL),
            name="finish",
        )(dest.reshape(1), layer_turns, plane, tables[1], offset_turn, *before)

    got, before = {}, []
    for ahead in [*range(fl - 1, 0, -1), 0]:
        dest = (mid_at // fl) * fl + (mine ^ ahead)
        block = finish(dest, *before)
        before = [block]
        if ahead:
            block = lax.ppermute(block, "mid", [(s, s ^ ahead) for s in range(mid_count)])
        got[ahead] = block

    field = None
    for ahead in [0, *range(fl - 1, 0, -1)]:
        freq = mine ^ ahead
        first = field is None
        field = pl.pallas_call(
            result_kernel,
            grid_spec=pltpu.PrefetchScalarGridSpec(
                num_scalar_prefetch=1,
                grid=(2,),
                in_specs=[vmem] if first else [vmem, hbm],
                out_specs=pl.BlockSpec((1, HALF, 2 * here, BLK), lambda i, f: (f[0], i, 0, 0)),
            ),
            out_shape=jax.ShapeDtypeStruct((fl, NH, 2 * here, BLK), jnp.float32),
            input_output_aliases={} if first else {2: 0},
            compiler_params=pltpu.CompilerParams(vmem_limit_bytes=SMALL),
            cost_estimate=pl.CostEstimate(
                flops=4 * NH * mid_local, bytes_accessed=12 * NH * mid_local, transcendentals=0
            ),
            name="result",
        )(freq.reshape(1), got[ahead], *([] if first else [field]))
    field = field.reshape(fl, NH, here, 2, BLK).transpose(0, 1, 3, 2, 4)
    return field.reshape(fl, NH, 2, mid_local)


def solution(mesh):
    in_specs = (
        P("off", None, None, "mid"),
        P("off", None, None, None),
        P("off", None),
        P("off"),
        P(None, None, "mid"),
        P(),
    )
    out_specs = P("off", None, None, "mid")
    return jax.shard_map(local, mesh=mesh, in_specs=in_specs, out_specs=out_specs, check_vma=False)
```
